32 devices in a mesh: groups: 2 (over x), ctx: 8 (over z, y), head: 2 (over core).
Axes of the slice: x: 2, y: 2, z: 4, core: 2. Of those that a mesh axis runs over, the one named last changes fastest.
Arguments:
- q_nope: bfloat16 [2048, 8192], P(('groups', 'ctx'), 'head'), parts along dimension 0, may hold values from -6 to 6
- q_rope: bfloat16 [2048, 4096], P(('groups', 'ctx'), 'head'), parts along dimension 0, may hold values from -18 to 18
- latent_cache: bfloat16 [2304, 512], P(('groups', 'ctx')), parts along dimension 0, may hold values from -6 to 6
- rope_keys: bfloat16 [2304, 64], P(('groups', 'ctx')), parts along dimension 0, may hold values from -6 to 6
- w_absorb: bfloat16 [64, 128, 512], P('head'), may hold values from -0.5 to 0.5
- w_value: bfloat16 [64, 512, 128], P('head'), may hold values from -0.25 to 0.25
- w_output: bfloat16 [8192, 7168], P('head', 'ctx'), may hold values from -0.0625 to 0.0625
- span_offset: int32 [2], P('groups'), parts along dimension 0, may hold values from 0 to 128
- valid_lengths: int32 [16], P('groups'), parts along dimension 0, may hold values from 72 to 144, as said below
Outputs:
- mixed: bfloat16 [2048, 7168], P(('groups', 'head'), 'ctx'), parts along dimension 0
The draws below stay inside these ranges and needn't reach their ends.
There are 2 independent parts, one for each index of `groups`. The reference program is written for one: setup_inputs(seed, part) draws one part's arguments, and reference() takes and returns one part's arrays. A program takes and returns all parts, laid end to end along the dimension named above; an argument that names none is the same for every part. Nothing has to cross between parts.
Inputs may be any that keep to these rules, and one draw needn't show every extreme that they name: `valid_lengths`: one shard of each part has exactly 144 valid rows.
All inputs are finite; a program needn't handle non-finite values.
Results may differ from the reference program's by a relative error of at most 0.009.
Values may be sent and summed in bfloat16 or wider, within the bound.
No kernel may reach another device: no remote copies, remote signals or barrier semaphores. Data moves between devices by JAX's collectives and lax.ppermute only.
A program may use at most 128 MiB of HBM per device.

```python
import math
import jax
import jax.numpy as jnp
from jax import lax

D = 7168
H = 64
NOPE = 128
ROPE = 64
LAT = 512
VDIM = 128
Q_DEV = 128
C_DEV = 144
QTOK = 1024
CTX = 1152
N_CTX = 8


def draw_rope_keys(key, part):
    key = jax.random.fold_in(key, 11)
    base = jnp.clip(jax.random.normal(key, (CTX, ROPE), jnp.float32), -6.0, 6.0)
    return base.astype(jnp.bfloat16)


def draw_q_rope(key, part):
    key = jax.random.fold_in(key, 12)
    base = jnp.clip(jax.random.normal(key, (QTOK, H * ROPE), jnp.float32), -6.0, 6.0)
    return base.astype(jnp.bfloat16)


def draw_valid_lengths(key, part):
    key = jax.random.fold_in(key, 13)
    lengths = jax.random.randint(key, (N_CTX,), C_DEV // 2, C_DEV + 1, jnp.int32)
    full_shard = jax.random.randint(jax.random.fold_in(key, 1), (), 0, N_CTX, jnp.int32)
    return jnp.where(jnp.arange(N_CTX, dtype=jnp.int32) == full_shard, jnp.int32(C_DEV), lengths)


def block_levels(rng, shape, cuts, low, largest):
    gain, own = 1.0, jax.random.fold_in(rng, 6)
    for axis_at, shards_of in cuts:
        steps = jnp.exp(jax.random.uniform(jax.random.fold_in(own, axis_at), (shards_of,), jnp.float32, low / len(cuts), largest / len(cuts)))
        gain = gain * jnp.repeat(steps, shape[axis_at] // shards_of).reshape([-1 if axis == axis_at else 1 for axis in range(len(shape))])
    return gain


def centred(key, dims, width, bound, pieces=(), held_as=jnp.bfloat16):
    values = width * jax.random.normal(key, dims, jnp.float32)
    if pieces:
        values = values * block_levels(key, dims, pieces, -0.22, 0.18)
    return jnp.clip(values, -bound, bound).astype(held_as)


def setup_inputs(seed: int = 0, part: int = 0) -> dict:
    seeds = jax.random.split(jax.random.key(seed), 10)
    own_keys = jax.random.split(jax.random.fold_in(seeds[9], part), 10)
    return {
        "q_nope": centred(own_keys[0], (QTOK, H * NOPE), 1.0, 6.0, ((0, 8), (1, 2))),
        "q_rope": draw_q_rope(jax.random.fold_in(jax.random.fold_in(seeds[9], part), 71), part),
        "latent_cache": centred(own_keys[2], (CTX, LAT), 1.0, 6.0, ((0, 8),)),
        "rope_keys": draw_rope_keys(jax.random.fold_in(jax.random.fold_in(seeds[9], part), 71), part),
        "w_absorb": centred(seeds[4], (H, NOPE, LAT), NOPE ** -0.5, 0.5, ((0, 2),)),
        "w_value": centred(seeds[5], (H, LAT, VDIM), LAT ** -0.5, 0.25, ((0, 2),)),
        "w_output": centred(seeds[6], (H * VDIM, D), (H * VDIM) ** -0.5, 0.0625, ((0, 2), (1, 8))),
        "span_offset": jax.random.randint(own_keys[7], (1,), 0, C_DEV * N_CTX - Q_DEV * N_CTX + 1).astype(jnp.int32),
        "valid_lengths": draw_valid_lengths(jax.random.fold_in(jax.random.fold_in(seeds[9], part), 71), part),
    }


def reference(q_nope, q_rope, latent_cache, rope_keys, w_absorb, w_value, w_output, span_offset, valid_lengths):
    head_count = w_absorb.shape[0]
    hp = lax.Precision.HIGHEST
    query_lat = jnp.einsum('qhd,hdc->hqc', q_nope.reshape(QTOK, head_count, NOPE).astype(jnp.float32), w_absorb.astype(jnp.float32), precision=hp).astype(jnp.bfloat16)
    query_rot = q_rope.reshape(QTOK, head_count, ROPE).transpose(1, 0, 2)
    positions = span_offset[0] + jnp.arange(QTOK, dtype=jnp.int32)
    key_index = jnp.arange(CTX, dtype=jnp.int32)
    shard_limit = jnp.repeat(valid_lengths, C_DEV, total_repeat_length=CTX)
    visible = (key_index % C_DEV < shard_limit)[None, :] & (key_index[None, :] <= positions[:, None])
    cache_wide = latent_cache.astype(jnp.float32)
    rope_wide = rope_keys.astype(jnp.float32)
    score_scale = 1.0 / math.sqrt(NOPE + ROPE)

    def one_head(operands):
        query_block, rot_block, value_map = operands
        scores = (jnp.dot(query_block.astype(jnp.float32), cache_wide.T, precision=hp) + jnp.dot(rot_block.astype(jnp.float32), rope_wide.T, precision=hp)) * score_scale
        scores = jnp.where(visible, scores, jnp.float32(-1e+30))
        row_max = lax.optimization_barrier(jnp.max(scores, axis=-1, keepdims=True))
        expo = jnp.where(visible, jnp.exp(scores - row_max), jnp.float32(0.0))
        row_total = lax.optimization_barrier(jnp.sum(expo, axis=-1, keepdims=True))
        probs = lax.optimization_barrier(expo.astype(jnp.bfloat16)).astype(jnp.float32)
        weighted = jnp.dot(probs, cache_wide, precision=hp)
        latent_out = lax.optimization_barrier((weighted / row_total).astype(jnp.bfloat16)).astype(jnp.float32)
        return jnp.dot(latent_out, value_map.astype(jnp.float32), precision=hp).astype(jnp.bfloat16)
    per_head = lax.map(one_head, (query_lat, query_rot, w_value))
    head_out = per_head.transpose(1, 0, 2).reshape(QTOK, head_count * VDIM)
    return jnp.dot(head_out, w_output, preferred_element_type=jnp.float32).astype(jnp.bfloat16)
```

```python
import functools
import math

import jax
import jax.numpy as jnp
from jax import lax
from jax.experimental import pallas as pl
from jax.experimental.pallas import tpu as pltpu
from jax.sharding import PartitionSpec as P

F32 = jnp.float32
BF16 = jnp.bfloat16
MASKED = -1e30
CHUNKS = 8


def params(mib):
    return pltpu.CompilerParams(vmem_limit_bytes=mib * 1024 * 1024)


def basis_of(shards):
    if shards == 8:
        return (6, 2, 1)
    return tuple(1 << bit for bit in reversed(range(shards.bit_length() - 1)))


def exchange(x, mask, shards):
    return lax.ppermute(x, "ctx", [(i, i ^ mask) for i in range(shards)])


def spread(x, shards):
    blocks = {0: x}
    for mask in basis_of(shards):
        blocks.update({key ^ mask: exchange(block, mask, shards) for key, block in blocks.items()})
    return blocks


def prep_kernel(heads, nope, rope, per_shard, order, limits, base, q_ref, r_ref, w_ref, lat_ref, bias_ref):
    tokens = q_ref.shape[0]
    latent = w_ref.shape[2]
    for head in range(heads):
        rows = slice(head * tokens, (head + 1) * tokens)
        lat = jnp.dot(
            q_ref[:, head * nope : (head + 1) * nope], w_ref[head], preferred_element_type=F32
        )
        lat_ref[rows, :latent] = lat.astype(BF16)
        lat_ref[rows, latent:] = r_ref[:, head * rope : (head + 1) * rope]

    @pl.when(pl.program_id(0) == 0)
    def _():
        keys = bias_ref.shape[1]
        column = lax.broadcasted_iota(jnp.int32, (1, keys), 1)
        place = jnp.full((1, keys), 2**30, jnp.int32)
        for at in range(keys // per_shard):
            inner = column - at * per_shard
            mine = (inner >= 0) & (inner < limits[at])
            place = jnp.where(mine, inner + order[at] * per_shard, place)
        position = base[0] + lax.broadcasted_iota(jnp.int32, bias_ref.shape, 0)
        bias_ref[...] = jnp.where(place <= position, F32(0.0), F32(MASKED))


def prep(q_nope, q_rope, w_absorb, order, limits, base, per_shard):
    heads, nope, latent = w_absorb.shape
    tokens = q_nope.shape[0]
    rope = q_rope.shape[1] // heads
    step = 4
    keys = per_shard * order.shape[0]
    smem = pl.BlockSpec(memory_space=pltpu.SMEM)
    return pl.pallas_call(
        functools.partial(prep_kernel, step, nope, rope, per_shard),
        grid=(heads // step,),
        in_specs=[
            smem,
            smem,
            smem,
            pl.BlockSpec((tokens, step * nope), lambda i: (0, i)),
            pl.BlockSpec((tokens, step * rope), lambda i: (0, i)),
            pl.BlockSpec((step, nope, latent), lambda i: (i, 0, 0)),
        ],
        out_specs=[
            pl.BlockSpec((step * tokens, latent + rope), lambda i: (i, 0)),
            pl.BlockSpec((tokens, keys), lambda i: (0, 0)),
        ],
        out_shape=[
            jax.ShapeDtypeStruct((heads * tokens, latent + rope), BF16),
            jax.ShapeDtypeStruct((tokens, keys), F32),
        ],
        compiler_params=params(32),
        cost_estimate=pl.CostEstimate(
            flops=2 * heads * tokens * nope * latent, bytes_accessed=12 << 20, transcendentals=0
        ),
        name="prep",
    )(order, limits, base, q_nope, q_rope, w_absorb)


def attend_kernel(heads, shards, scale, *refs):
    q_ref, bias_ref, w_ref = refs[:3]
    parts = refs[3 : 3 + shards]
    out_ref, kv, scores, probs, total, sem = refs[3 + shards :]
    tokens = bias_ref.shape[0]
    per_shard = parts[0].shape[0]
    latent, value = w_ref.shape[1:]
    copies = [
        pltpu.make_async_copy(part, kv.at[pl.ds(at * per_shard, per_shard)], sem.at[at])
        for at, part in enumerate(parts)
    ]
    for copy in copies:
        copy.start()
    for copy in copies:
        copy.wait()
    scores[...] = lax.dot_general(
        q_ref[...], kv[...], (((1,), (1,)), ((), ())), preferred_element_type=F32
    )
    for head in range(heads):
        rows = slice(head * tokens, (head + 1) * tokens)
        masked = scores[rows, :] + bias_ref[...]
        top = jnp.max(masked, axis=-1, keepdims=True)
        expo = jnp.exp2((masked - top) * F32(scale))
        total[rows, :] = jnp.sum(expo, axis=-1, keepdims=True)
        probs[rows, :] = expo.astype(BF16)
    weighted = jnp.dot(probs[...], kv[:, :latent], preferred_element_type=F32)
    mixed = (weighted / total[...]).astype(BF16)
    for head in range(heads):
        rows = slice(head * tokens, (head + 1) * tokens)
        out = jnp.dot(mixed[rows, :], w_ref[head], preferred_element_type=F32)
        out_ref[:, head * value : (head + 1) * value] = out.astype(BF16)


def attend(chunk, heads, queries, bias, w_value, parts, scale):
    tokens, keys = bias.shape
    depth = queries.shape[1]
    _, latent, value = w_value.shape
    shards = len(parts)
    rows = heads * tokens
    return pl.pallas_call(
        functools.partial(attend_kernel, heads, shards, scale * math.log2(math.e)),
        grid=(1,),
        in_specs=[
            pl.BlockSpec((rows, depth), lambda i: (chunk, 0)),
            pl.BlockSpec((tokens, keys), lambda i: (0, 0)),
            pl.BlockSpec((heads, latent, value), lambda i: (chunk, 0, 0)),
        ]
        + [pl.BlockSpec(memory_space=pl.ANY)] * shards,
        out_specs=pl.BlockSpec((tokens, heads * value), lambda i: (0, 0)),
        out_shape=jax.ShapeDtypeStruct((tokens, heads * value), BF16),
        scratch_shapes=[
            pltpu.VMEM((keys, depth), BF16),
            pltpu.VMEM((rows, keys), F32),
            pltpu.VMEM((rows, keys), BF16),
            pltpu.VMEM((rows, 1), F32),
            pltpu.SemaphoreType.DMA((shards,)),
        ],
        compiler_params=params(40),
        cost_estimate=pl.CostEstimate(
            flops=2 * rows * (keys * (depth + latent) + latent * value),
            bytes_accessed=4 << 20,
            transcendentals=rows * keys,
        ),
        name=f"attend{chunk}",
    )(queries, bias, w_value, *parts)


def project_kernel(shards, first, *refs):
    w_ref = refs[0]
    parts = refs[1 : 1 + shards]
    refs = refs[1 + shards :]
    if first:
        out_ref, gathered, sem = refs
        acc_ref = None
    else:
        acc_ref, out_ref, gathered, sem = refs
    tokens = parts[0].shape[0]
    step = pl.program_id(0)
    each = shards // pl.num_programs(0)
    copies = [
        pltpu.make_async_copy(part, gathered.at[pl.ds(at * tokens, tokens)], sem.at[at])
        for at, part in enumerate(parts)
    ]

    @pl.when(step == 0)
    def _():
        for copy in copies:
            copy.start()

    for at in range(shards):
        @pl.when(step == at // each)
        def _(at=at):
            copies[at].wait()

    rows = each * tokens
    start = pl.multiple_of(step * rows, rows)
    product = jnp.dot(gathered[pl.ds(start, rows), :], w_ref[...], preferred_element_type=F32)
    if first:
        out_ref[...] = product
    else:
        out_ref[...] = acc_ref[...] + product


def project(chunk, parts, w_output, acc, each=2):
    shards = len(parts)
    tokens, depth = parts[0].shape
    columns = w_output.shape[1]
    block = pl.BlockSpec((each * tokens, columns), lambda i: (i, 0))
    return pl.pallas_call(
        functools.partial(project_kernel, shards, acc is None),
        grid=(shards // each,),
        in_specs=[pl.BlockSpec((depth, columns), lambda i: (chunk, 0))]
        + [pl.BlockSpec(memory_space=pl.ANY)] * shards
        + ([] if acc is None else [block]),
        out_specs=block,
        out_shape=jax.ShapeDtypeStruct((shards * tokens, columns), F32),
        scratch_shapes=[
            pltpu.VMEM((shards * tokens, depth), BF16),
            pltpu.SemaphoreType.DMA((shards,)),
        ],
        input_output_aliases={} if acc is None else {1 + shards: 0},
        compiler_params=params(32),
        cost_estimate=pl.CostEstimate(
            flops=2 * shards * tokens * depth * columns,
            bytes_accessed=8 << 20,
            transcendentals=0,
        ),
        name=f"project{chunk}",
    )(w_output, *parts, *([] if acc is None else [acc]))


def finish_kernel(shards, half, *refs):
    choice, w_ref = refs[:2]
    parts = refs[2 : 2 + shards]
    acc_ref, out_ref, gathered, sem = refs[2 + shards :]
    tokens = parts[0].shape[0]
    width = shards // 2
    for side in range(2):
        copies = [
            pltpu.make_async_copy(part, gathered.at[pl.ds(at * tokens, tokens)], sem.at[at])
            for at, part in enumerate(parts[side * width : (side + 1) * width])
        ]

        @pl.when(choice[half] == side)
        def _(copies=copies):
            for copy in copies:
                copy.start()
            for copy in copies:
                copy.wait()

    product = jnp.dot(gathered[...], w_ref[...], preferred_element_type=F32)
    out_ref[...] = (acc_ref[...] + product).astype(out_ref.dtype)


def finish(chunk, half, choice, parts, w_output, acc, dtype):
    shards = len(parts)
    tokens, depth = parts[0].shape
    columns = w_output.shape[1]
    rows = shards * tokens // 2
    return pl.pallas_call(
        functools.partial(finish_kernel, shards, half),
        grid_spec=pltpu.PrefetchScalarGridSpec(
            num_scalar_prefetch=1,
            grid=(1,),
            in_specs=[pl.BlockSpec((depth, columns), lambda i, choice: (chunk, 0))]
            + [pl.BlockSpec(memory_space=pl.ANY)] * shards
            + [pl.BlockSpec((rows, columns), lambda i, choice: (choice[half], 0))],
            out_specs=pl.BlockSpec((rows, columns), lambda i, choice: (0, 0)),
            scratch_shapes=[
                pltpu.VMEM((rows, depth), BF16),
                pltpu.SemaphoreType.DMA((shards // 2,)),
            ],
        ),
        out_shape=jax.ShapeDtypeStruct((rows, columns), dtype),
        compiler_params=params(32),
        cost_estimate=pl.CostEstimate(
            flops=2 * rows * depth * columns, bytes_accessed=4 << 20, transcendentals=0
        ),
        name=f"finish{half}",
    )(choice, w_output, *parts, acc)


def join_kernel(order, mine_ref, other_ref, out_ref):
    out_ref[...] = (mine_ref[...] + other_ref[...].astype(F32)).astype(BF16)


def join(order, mine, other, tokens):
    rows, columns = mine.shape
    block = pl.BlockSpec((tokens, columns), lambda i, order: (i, 0))
    return pl.pallas_call(
        join_kernel,
        grid_spec=pltpu.PrefetchScalarGridSpec(
            num_scalar_prefetch=1,
            grid=(rows // tokens,),
            in_specs=[block, block],
            out_specs=pl.BlockSpec((tokens, columns), lambda i, order: (order[i], 0)),
        ),
        out_shape=jax.ShapeDtypeStruct((rows, columns), BF16),
        cost_estimate=pl.CostEstimate(
            flops=rows * columns, bytes_accessed=4 << 20, transcendentals=0
        ),
        name="join",
    )(order, mine, other)


def local(
    q_nope, q_rope, latent_cache, rope_keys, w_absorb, w_value, w_output, span_offset, valid_lengths
):
    head_count, nope_dim, _ = w_absorb.shape
    tokens = q_nope.shape[0]
    rope_dim = rope_keys.shape[1]
    per_shard = latent_cache.shape[0]
    shards = valid_lengths.shape[0]
    me = lax.axis_index("ctx")
    side = lax.axis_index("head")

    cache = spread(jnp.concatenate([latent_cache, rope_keys], axis=1), shards)
    keys = sorted(cache)
    order = jnp.asarray(keys, jnp.int32) ^ me
    limits = valid_lengths[order]
    base = span_offset + me * tokens
    queries, bias = prep(q_nope, q_rope, w_absorb, order, limits, base, per_shard)
    cache = [cache[key] for key in keys]

    mine = me // (shards // 2)
    choice = jnp.stack([jnp.where(mine == side, 1, 0), jnp.where(mine == side, 0, 1)])
    scale = 1.0 / math.sqrt(nope_dim + rope_dim)
    heads = head_count // CHUNKS
    acc = None
    for chunk in range(CHUNKS):
        out = attend(chunk, heads, queries, bias, w_value, cache, scale)
        gathered = spread(out, shards)
        parts = [gathered[key] for key in keys]
        if chunk < CHUNKS - 1:
            acc = project(chunk, parts, w_output, acc)
    last = CHUNKS - 1
    give = finish(last, 0, choice, parts, w_output, acc, BF16)
    other = lax.ppermute(give, "head", [(0, 1), (1, 0)])
    kept = finish(last, 1, choice, parts, w_output, acc, F32)
    places = jnp.arange(shards // 2, dtype=jnp.int32) ^ (me % (shards // 2))
    return join(places, kept, other, tokens)


def solution(mesh):
    return jax.shard_map(
        local,
        mesh=mesh,
        in_specs=(
            P(("groups", "ctx"), "head"),
            P(("groups", "ctx"), "head"),
            P(("groups", "ctx"), None),
            P(("groups", "ctx"), None),
            P("head", None, None),
            P("head", None, None),
            P("head", "ctx"),
            P("groups"),
            P("groups"),
        ),
        out_specs=P(("groups", "head"), "ctx"),
        check_vma=False,
    )
```

```python
import functools
import math

import jax
import jax.numpy as jnp
from jax import lax
from jax.experimental import pallas as pl
from jax.experimental.pallas import tpu as pltpu
from jax.sharding import PartitionSpec as P

F32 = jnp.float32
BF16 = jnp.bfloat16
MASKED = -1e30
LANES = 128
STEP = 4
PIECES = (1, 2, 2, 2, 1)
ANYWHERE = pl.BlockSpec(memory_space=pl.ANY)
SCALARS = pl.BlockSpec(memory_space=pltpu.SMEM)


def params():
    return pltpu.CompilerParams(vmem_limit_bytes=58 * 1024 * 1024)


def cost(flops, size, exps=0):
    return pl.CostEstimate(flops=flops, bytes_accessed=size, transcendentals=exps)


def basis_of(shards):
    if shards == 8:
        return (6, 2, 1)
    return tuple(1 << bit for bit in reversed(range(shards.bit_length() - 1)))


def exchange(x, mask, shards):
    return lax.ppermute(x, "ctx", [(i, i ^ mask) for i in range(shards)])


def sibling(x):
    return lax.ppermute(x, "head", [(0, 1), (1, 0)])


def stack_kernel(first_ref, second_ref, out_ref):
    out_ref[0] = first_ref[...]
    out_ref[1] = second_ref[...]


def stack(first, second):
    return pl.pallas_call(
        stack_kernel,
        out_shape=jax.ShapeDtypeStruct((2, *first.shape), first.dtype),
        compiler_params=params(),
        cost_estimate=cost(0, 4 * first.size * first.dtype.itemsize),
        name="stack",
    )(first, second)


def spread(x, shards):
    first, *rest = basis_of(shards)
    pairs = {0: stack(x, exchange(x, first, shards))}
    for mask in rest:
        pairs.update({key ^ mask: exchange(pair, mask, shards) for key, pair in pairs.items()})
    return pairs


def pack_kernel(own, side, latent_ref, rope_ref, out_ref):
    rows, latent = latent_ref.shape
    rope = rope_ref.shape[0]
    turned = rope_ref[...].astype(F32).T.astype(BF16)
    out_ref[:, latent:] = jnp.zeros((own, out_ref.shape[1] - latent), BF16)
    for at in range(2):
        span = slice(0, own) if at == 0 else slice(rows - own, rows)

        @pl.when(side[0] == at)
        def _(span=span):
            out_ref[:, :latent] = latent_ref[span, :]
            out_ref[:, latent : latent + rope] = turned[span, :]


def pack(side, latent_cache, rope_keys, own, depth):
    return pl.pallas_call(
        functools.partial(pack_kernel, own),
        in_specs=[SCALARS, pl.BlockSpec(), pl.BlockSpec()],
        out_shape=jax.ShapeDtypeStruct((own, depth), BF16),
        compiler_params=params(),
        cost_estimate=cost(0, 1 << 20),
        name="pack",
    )(side, latent_cache, rope_keys.T)


def prep_kernel(nope, rope, per_shard, own, order, limits, base, q_ref, r_ref, w_ref, lat_ref, bias_ref):
    tokens = q_ref.shape[0]
    heads, _, latent = w_ref.shape
    lat_ref[:, latent + rope :] = jnp.zeros(
        (heads * tokens, lat_ref.shape[1] - latent - rope), BF16
    )
    for head in range(heads):
        rows = slice(head * tokens, (head + 1) * tokens)
        lat = jnp.dot(
            q_ref[:, head * nope : (head + 1) * nope], w_ref[head], preferred_element_type=F32
        )
        lat_ref[rows, :latent] = lat.astype(BF16)
        lat_ref[rows, latent : latent + rope] = r_ref[:, head * rope : (head + 1) * rope]

    @pl.when(pl.program_id(0) == 0)
    def _():
        keys = bias_ref.shape[1]
        column = lax.broadcasted_iota(jnp.int32, (1, keys), 1)
        place = jnp.full((1, keys), 2**30, jnp.int32)
        side = base[1]
        for at in range(keys // per_shard):
            inner = column - at * per_shard
            mine = jnp.where(side == 0, inner, inner + (per_shard - own))
            others = jnp.where(side == 0, inner, inner - own)
            row = jnp.where(inner < own, mine, others)
            here = (inner >= 0) & (inner < per_shard) & (row < limits[at])
            place = jnp.where(here, row + order[at] * per_shard, place)
        position = base[0] + lax.broadcasted_iota(jnp.int32, bias_ref.shape, 0)
        bias_ref[...] = jnp.where(place <= position, F32(0.0), F32(MASKED))


def prep(q_nope, q_rope, w_absorb, order, limits, base, per_shard, own, depth):
    heads, nope, latent = w_absorb.shape
    tokens = q_nope.shape[0]
    rope = q_rope.shape[1] // heads
    keys = per_shard * order.shape[0]
    return pl.pallas_call(
        functools.partial(prep_kernel, nope, rope, per_shard, own),
        grid=(heads // STEP,),
        in_specs=[
            SCALARS,
            SCALARS,
            SCALARS,
            pl.BlockSpec((tokens, STEP * nope), lambda i: (0, i)),
            pl.BlockSpec((tokens, STEP * rope), lambda i: (0, i)),
            pl.BlockSpec((STEP, nope, latent), lambda i: (i, 0, 0)),
        ],
        out_specs=[
            pl.BlockSpec((STEP * tokens, depth), lambda i: (i, 0)),
            pl.BlockSpec((tokens, keys), lambda i: (0, 0)),
        ],
        out_shape=[
            jax.ShapeDtypeStruct((heads * tokens, depth), BF16),
            jax.ShapeDtypeStruct((tokens, keys), F32),
        ],
        compiler_params=params(),
        cost_estimate=cost(2 * heads * tokens * nope * latent, 12 << 20),
        name="prep",
    )(order, limits, base, q_nope, q_rope, w_absorb)


def join_kernel(groups, own, side, *refs):
    mine = refs[:groups]
    theirs = refs[groups : 2 * groups]
    out_ref, sem = refs[2 * groups :]
    per_shard = out_ref.shape[0] // (2 * groups)
    rest = per_shard - own
    skip = pl.multiple_of((1 - side[0]) * (own - rest), own - rest)
    copies = []
    for at in range(2 * groups):
        group, inner = at // 2, at % 2
        start = at * per_shard
        copies.append(
            pltpu.make_async_copy(
                mine[group].at[inner], out_ref.at[pl.ds(start, own)], sem.at[2 * at]
            )
        )
        copies.append(
            pltpu.make_async_copy(
                theirs[group].at[inner, pl.ds(skip, rest)],
                out_ref.at[pl.ds(start + own, rest)],
                sem.at[2 * at + 1],
            )
        )
    for copy in copies:
        copy.start()
    for copy in copies:
        copy.wait()


def join(side, mine, theirs, per_shard):
    groups = len(mine)
    _, own, depth = mine[0].shape
    return pl.pallas_call(
        functools.partial(join_kernel, groups, own),
        in_specs=[SCALARS] + [ANYWHERE] * (2 * groups),
        out_shape=jax.ShapeDtypeStruct((2 * groups * per_shard, depth), BF16),
        scratch_shapes=[pltpu.SemaphoreType.DMA((4 * groups,))],
        compiler_params=params(),
        cost_estimate=cost(0, 4 << 20),
        name="join",
    )(side, *mine, *theirs)


def attend_kernel(scale, q_ref, bias_ref, w_ref, kv_ref, *refs):
    out_ref, scores, probs = refs[-3:]
    tokens = bias_ref.shape[0]
    heads, latent, value = w_ref.shape
    pair = scores.shape[1] // tokens

    def score(at):
        rows = slice(at * pair * tokens, (at + 1) * pair * tokens)
        scores[at % 2] = lax.dot_general(
            q_ref[rows, :], kv_ref[...], (((1,), (1,)), ((), ())), preferred_element_type=F32
        )

    def weigh(at):
        totals = []
        for head in range(pair):
            rows = slice(head * tokens, (head + 1) * tokens)
            masked = scores[at % 2, rows, :] + bias_ref[...]
            top = jnp.max(masked, axis=-1, keepdims=True)
            expo = jnp.exp2((masked - top) * F32(scale))
            totals.append(jnp.sum(expo, axis=-1, keepdims=True))
            probs[at % 2, rows, :] = expo.astype(BF16)
        weighted = jnp.dot(probs[at % 2], kv_ref[:, :latent], preferred_element_type=F32)
        for head in range(pair):
            rows = slice(head * tokens, (head + 1) * tokens)
            mixed = (weighted[rows, :] / totals[head]).astype(BF16)
            which = at * pair + head
            out = jnp.dot(mixed, w_ref[which], preferred_element_type=F32)
            out_ref[:, which * value : (which + 1) * value] = out.astype(BF16)

    score(0)
    for at in range(heads // pair):
        if at + 1 < heads // pair:
            score(at + 1)
        weigh(at)


def attend(start, steps, queries, bias, w_value, kv, scale, after=()):
    tokens, keys = bias.shape
    depth = queries.shape[1]
    _, latent, value = w_value.shape
    rows = STEP * tokens
    return pl.pallas_call(
        functools.partial(attend_kernel, scale * math.log2(math.e)),
        grid=(steps,),
        in_specs=[
            pl.BlockSpec((rows, depth), lambda i: (start + i, 0)),
            pl.BlockSpec((tokens, keys), lambda i: (0, 0)),
            pl.BlockSpec((STEP, latent, value), lambda i: (start + i, 0, 0)),
            pl.BlockSpec((keys, depth), lambda i: (0, 0)),
        ]
        + [ANYWHERE] * len(after),
        out_specs=pl.BlockSpec((tokens, STEP * value), lambda i: (0, i)),
        out_shape=jax.ShapeDtypeStruct((tokens, steps * STEP * value), BF16),
        scratch_shapes=[
            pltpu.VMEM((2, rows // 2, keys), F32),
            pltpu.VMEM((2, rows // 2, keys), BF16),
        ],
        compiler_params=params(),
        cost_estimate=cost(
            steps * 2 * rows * (keys * (depth + latent) + latent * value),
            (2 + steps) << 20,
            steps * rows * keys,
        ),
        name=f"attend{start}",
    )(queries, bias, w_value, kv, *after)


def project_kernel(start, groups, first, *refs):
    w_ref = refs[0]
    pairs = refs[1 : 1 + groups]
    out_ref, gathered, weights, sem = refs[-4:]
    tokens, depth = pairs[0].shape[1:]
    step = pl.program_id(0)
    each = 2 * groups // pl.num_programs(0)
    copies = [
        pltpu.make_async_copy(
            pairs[at % groups].at[at // groups],
            gathered.at[pl.ds(at * tokens, tokens)],
            sem.at[at],
        )
        for at in range(2 * groups)
    ]
    fetch = pltpu.make_async_copy(w_ref.at[pl.ds(start, depth)], weights, sem.at[2 * groups])

    @pl.when(step == 0)
    def _():
        fetch.start()
        for copy in copies:
            copy.start()
        fetch.wait()

    for at in range(2 * groups):
        @pl.when(step == at // each)
        def _(at=at):
            copies[at].wait()

    rows = each * tokens
    span = pl.ds(pl.multiple_of(step * rows, rows), rows)
    product = jnp.dot(gathered[span, :], weights[...], preferred_element_type=F32)
    out_ref[...] = product if first else refs[1 + groups][...] + product


def project(start, pairs, w_output, acc, each=2):
    groups = len(pairs)
    _, tokens, depth = pairs[0].shape
    columns = w_output.shape[1]
    rows = 2 * groups * tokens
    block = pl.BlockSpec((each * tokens, columns), lambda i: (i, 0))
    return pl.pallas_call(
        functools.partial(project_kernel, start, groups, acc is None),
        grid=(2 * groups // each,),
        in_specs=[ANYWHERE] * (1 + groups) + ([] if acc is None else [block]),
        out_specs=block,
        out_shape=jax.ShapeDtypeStruct((rows, columns), F32),
        scratch_shapes=[
            pltpu.VMEM((rows, depth), BF16),
            pltpu.VMEM((depth, columns), BF16),
            pltpu.SemaphoreType.DMA((2 * groups + 1,)),
        ],
        input_output_aliases={} if acc is None else {1 + groups: 0},
        compiler_params=params(),
        cost_estimate=cost(2 * rows * depth * columns, 10 << 20),
        name=f"project{start}",
    )(w_output, *pairs, *([] if acc is None else [acc]))


def finish_kernel(start, groups, choice, places, w_ref, *refs):
    pairs = refs[:groups]
    acc_ref, out_ref, gathered, weights, sem = refs[groups:]
    tokens, depth = pairs[0].shape[1:]
    copies = [
        pltpu.make_async_copy(
            pairs[at].at[choice[0]], gathered.at[pl.ds(at * tokens, tokens)], sem.at[at]
        )
        for at in range(groups)
    ]
    copies.append(pltpu.make_async_copy(w_ref.at[pl.ds(start, depth)], weights, sem.at[groups]))
    for copy in copies:
        copy.start()
    for copy in copies:
        copy.wait()
    product = jnp.dot(gathered[...], weights[...], preferred_element_type=F32)
    for at in range(groups):
        rows = slice(at * tokens, (at + 1) * tokens)
        to = pl.ds(pl.multiple_of(places[at] * tokens, tokens), tokens)
        out_ref[to, :] = (acc_ref[rows, :] + product[rows, :]).astype(out_ref.dtype)


def finish(start, choice, places, pairs, w_output, acc, dtype):
    groups = len(pairs)
    _, tokens, depth = pairs[0].shape
    columns = w_output.shape[1]
    rows = groups * tokens
    return pl.pallas_call(
        functools.partial(finish_kernel, start, groups),
        grid_spec=pltpu.PrefetchScalarGridSpec(
            num_scalar_prefetch=2,
            grid=(1,),
            in_specs=[ANYWHERE] * (1 + groups)
            + [pl.BlockSpec((rows, columns), lambda i, choice, places: (choice[0], 0))],
            out_specs=pl.BlockSpec((rows, columns), lambda i, choice, places: (0, 0)),
            scratch_shapes=[
                pltpu.VMEM((rows, depth), BF16),
                pltpu.VMEM((depth, columns), BF16),
                pltpu.SemaphoreType.DMA((groups + 1,)),
            ],
        ),
        out_shape=jax.ShapeDtypeStruct((rows, columns), dtype),
        compiler_params=params(),
        cost_estimate=cost(2 * rows * depth * columns, 6 << 20),
        name="finish",
    )(choice, places, w_output, *pairs, acc)


def local(
    q_nope, q_rope, latent_cache, rope_keys, w_absorb, w_value, w_output, span_offset, valid_lengths
):
    head_count, nope_dim, latent = w_absorb.shape
    tokens = q_nope.shape[0]
    rope_dim = rope_keys.shape[1]
    per_shard = latent_cache.shape[0]
    shards = valid_lengths.shape[0]
    value = w_value.shape[2]
    depth = -(-(latent + rope_dim) // LANES) * LANES
    own = -(-per_shard // 32) * 16
    me = lax.axis_index("ctx").astype(jnp.int32)
    side = lax.axis_index("head").astype(jnp.int32)
    sides = side[None]

    far = basis_of(shards)[0]
    mine = spread(pack(sides, latent_cache, rope_keys, own, depth), shards)
    keys = sorted(mine)
    theirs = {key: sibling(pair) for key, pair in mine.items()}
    owners = [key ^ (far * inner) for key in keys for inner in range(2)]
    order = jnp.asarray(owners, jnp.int32) ^ me
    limits = valid_lengths[order]
    base = jnp.concatenate([span_offset + me * tokens, sides])
    queries, bias = prep(
        q_nope, q_rope, w_absorb, order, limits, base, per_shard, own, depth
    )
    kv = join(sides, [mine[key] for key in keys], [theirs[key] for key in keys], per_shard)

    scale = 1.0 / math.sqrt(nope_dim + rope_dim)
    acc = None
    start = 0
    stacks = []
    for chunk, piece in enumerate(PIECES):
        steps = piece * head_count // (STEP * sum(PIECES))
        after = stacks[:-1][-1:]
        out = attend(start, steps, queries, bias, w_value, kv, scale, after)
        gathered = spread(out, shards)
        pairs = [gathered[key] for key in keys]
        stacks.append(gathered[0])
        row = start * STEP * value
        if chunk < len(PIECES) - 1:
            acc = project(row, pairs, w_output, acc)
        start += steps

    half = shards // 2
    keep = jnp.where(me // half == side, 0, 1).astype(jnp.int32)
    near = jnp.asarray(keys, jnp.int32) ^ me
    give = 1 - keep
    kept_places = (near ^ (far * keep)) % half
    give_places = (near ^ (far * give)) % half
    sent = finish(row, give[None], give_places, pairs, w_output, acc, BF16)
    other = sibling(sent)
    kept = finish(row, keep[None], kept_places, pairs, w_output, acc, F32)
    return (kept + other.astype(F32)).astype(BF16)


def solution(mesh):
    return jax.shard_map(
        local,
        mesh=mesh,
        in_specs=(
            P(("groups", "ctx"), "head"),
            P(("groups", "ctx"), "head"),
            P(("groups", "ctx"), None),
            P(("groups", "ctx"), None),
            P("head", None, None),
            P("head", None, None),
            P("head", "ctx"),
            P("groups"),
            P("groups"),
        ),
        out_specs=P(("groups", "head"), "ctx"),
        check_vma=False,
    )
```

```python
import functools
import math

import jax
import jax.numpy as jnp
from jax import lax
from jax.experimental import pallas as pl
from jax.experimental.pallas import tpu as pltpu
from jax.sharding import PartitionSpec as P

F32 = jnp.float32
BF16 = jnp.bfloat16
MASKED = -1e30
LANES = 128
STEP = 4
PIECES = (1, 2, 2, 2, 1)
LOCAL = pl.BlockSpec(memory_space=pltpu.VMEM)
ANYWHERE = pl.BlockSpec(memory_space=pl.ANY)
SCALARS = pl.BlockSpec(memory_space=pltpu.SMEM)


def params(mib):
    return pltpu.CompilerParams(vmem_limit_bytes=mib * 1024 * 1024)


def cost(flops, size, exps=0):
    return pl.CostEstimate(flops=flops, bytes_accessed=size, transcendentals=exps)


def held(x):
    return pltpu.with_memory_space_constraint(x, pltpu.VMEM)


def basis_of(shards):
    if shards == 8:
        return (6, 2, 1)
    return tuple(1 << bit for bit in reversed(range(shards.bit_length() - 1)))


def exchange(x, mask, shards):
    return lax.ppermute(x, "ctx", [(i, i ^ mask) for i in range(shards)])


def sibling(x):
    return lax.ppermute(x, "head", [(0, 1), (1, 0)])


def stack_kernel(first_ref, second_ref, *refs):
    out_ref = refs[-1]
    out_ref[0] = first_ref[...]
    out_ref[1] = second_ref[...]


def stack(first, second, after=()):
    return pl.pallas_call(
        stack_kernel,
        in_specs=[LOCAL, LOCAL] + [ANYWHERE] * len(after),
        out_specs=LOCAL,
        out_shape=pltpu.VMEM((2, *first.shape), first.dtype),
        compiler_params=params(2),
        cost_estimate=cost(0, 1024),
        name="stack",
    )(held(first), held(second), *after)


def spread(x, shards, after=()):
    first, *rest = basis_of(shards)
    pairs = {0: stack(x, exchange(x, first, shards), after)}
    for mask in rest:
        pairs.update({key ^ mask: exchange(pair, mask, shards) for key, pair in pairs.items()})
    return pairs


def pack_kernel(own, latent_ref, rope_ref, out_ref):
    rows, latent = latent_ref.shape
    rope = rope_ref.shape[0]
    side = lax.axis_index("head")
    turned = rope_ref[...].astype(F32).T.astype(BF16)
    out_ref[:, latent:] = jnp.zeros((own, out_ref.shape[1] - latent), BF16)
    for at in range(2):
        span = slice(0, own) if at == 0 else slice(rows - own, rows)

        @pl.when(side == at)
        def _(span=span):
            out_ref[:, :latent] = latent_ref[span, :]
            out_ref[:, latent : latent + rope] = turned[span, :]


def pack(latent_cache, rope_keys, own, depth):
    return pl.pallas_call(
        functools.partial(pack_kernel, own),
        in_specs=[LOCAL, LOCAL],
        out_specs=LOCAL,
        out_shape=pltpu.VMEM((own, depth), BF16),
        compiler_params=params(2),
        cost_estimate=cost(0, 1024),
        name="pack",
    )(latent_cache, rope_keys.T)


def mask_kernel(own, owners, span_ref, valid_ref, bias_ref):
    tokens, keys = bias_ref.shape
    per_shard = keys // len(owners)
    me, side = lax.axis_index("ctx"), lax.axis_index("head")
    column = lax.broadcasted_iota(jnp.int32, (1, keys), 1)
    place = jnp.full((1, keys), 2**30, jnp.int32)
    for at, owner in enumerate(owners):
        shard = me ^ owner
        inner = column - at * per_shard
        mine = jnp.where(side == 0, inner, inner + (per_shard - own))
        others = jnp.where(side == 0, inner, inner - own)
        row = jnp.where(inner < own, mine, others)
        here = (inner >= 0) & (inner < per_shard) & (row < valid_ref[shard])
        place = jnp.where(here, row + shard * per_shard, place)
    position = span_ref[0] + me * tokens + lax.broadcasted_iota(jnp.int32, (tokens, keys), 0)
    bias_ref[...] = jnp.where(place <= position, F32(0.0), F32(MASKED))


def mask(span_offset, valid_lengths, owners, tokens, per_shard, own):
    return pl.pallas_call(
        functools.partial(mask_kernel, own, owners),
        in_specs=[SCALARS, SCALARS],
        out_specs=LOCAL,
        out_shape=pltpu.VMEM((tokens, per_shard * len(owners)), F32),
        compiler_params=params(4),
        cost_estimate=cost(0, 1024),
        name="mask",
    )(span_offset, valid_lengths)


def prep_kernel(q_hbm, r_hbm, w_hbm, lat_ref, q_ref, r_ref, w_ref, sem):
    tokens = q_ref.shape[0]
    heads, nope, latent = w_ref.shape
    rope = r_ref.shape[1] // heads
    whole = (
        pltpu.make_async_copy(q_hbm, q_ref, sem.at[0]),
        pltpu.make_async_copy(r_hbm, r_ref, sem.at[1]),
    )
    pieces = [
        pltpu.make_async_copy(
            w_hbm.at[pl.ds(at, STEP)], w_ref.at[pl.ds(at, STEP)], sem.at[2 + at // STEP]
        )
        for at in range(0, heads, STEP)
    ]
    for copy in (*whole, *pieces):
        copy.start()
    lat_ref[:, latent + rope :] = jnp.zeros(
        (heads * tokens, lat_ref.shape[1] - latent - rope), BF16
    )
    for copy in whole:
        copy.wait()
    for head in range(heads):
        if head % STEP == 0:
            pieces[head // STEP].wait()
        rows = slice(head * tokens, (head + 1) * tokens)
        lat = jnp.dot(
            q_ref[:, head * nope : (head + 1) * nope], w_ref[head], preferred_element_type=F32
        )
        lat_ref[rows, :latent] = lat.astype(BF16)
        lat_ref[rows, latent : latent + rope] = r_ref[:, head * rope : (head + 1) * rope]


def prep(q_nope, q_rope, w_absorb, depth):
    heads = w_absorb.shape[0]
    tokens = q_nope.shape[0]
    arrays = (q_nope, q_rope, w_absorb)
    return pl.pallas_call(
        prep_kernel,
        in_specs=[ANYWHERE] * 3,
        out_specs=LOCAL,
        out_shape=pltpu.VMEM((heads * tokens, depth), BF16),
        scratch_shapes=[pltpu.VMEM(x.shape, x.dtype) for x in arrays]
        + [pltpu.SemaphoreType.DMA((2 + heads // STEP,))],
        compiler_params=params(10),
        cost_estimate=cost(0, 1024),
        name="prep",
    )(*(pltpu.with_memory_space_constraint(x, pltpu.HBM) for x in arrays))


def join_kernel(groups, own, *refs):
    mine = refs[:groups]
    theirs = refs[groups : 2 * groups]
    out_ref = refs[-1]
    per_shard = out_ref.shape[0] // (2 * groups)
    rest = per_shard - own
    side = lax.axis_index("head")
    for at in range(2 * groups):
        group, inner = at // 2, at % 2
        start = at * per_shard
        out_ref[start : start + own] = mine[group][inner]
    for half in range(2):

        @pl.when(side == half)
        def _(skip=(1 - half) * (own - rest)):
            for at in range(2 * groups):
                start = at * per_shard + own
                out_ref[start : start + rest] = theirs[at // 2][at % 2, skip : skip + rest]


def join(mine, theirs, per_shard):
    groups = len(mine)
    _, own, depth = mine[0].shape
    return pl.pallas_call(
        functools.partial(join_kernel, groups, own),
        in_specs=[LOCAL] * (2 * groups),
        out_specs=LOCAL,
        out_shape=pltpu.VMEM((2 * groups * per_shard, depth), BF16),
        compiler_params=params(2),
        cost_estimate=cost(0, 1024),
        name="join",
    )(*map(held, mine), *map(held, theirs))


def attend_kernel(scale, start, heads, q_ref, bias_ref, w_ref, kv_ref, *refs):
    out_ref, scores, probs = refs[-3:]
    tokens = bias_ref.shape[0]
    _, latent, value = w_ref.shape
    pair = scores.shape[1] // tokens

    def score(at):
        row = (start + at * pair) * tokens
        scores[at % 2] = lax.dot_general(
            q_ref[row : row + pair * tokens, :],
            kv_ref[...],
            (((1,), (1,)), ((), ())),
            preferred_element_type=F32,
        )

    def weigh(at):
        totals = []
        for head in range(pair):
            rows = slice(head * tokens, (head + 1) * tokens)
            masked = scores[at % 2, rows, :] + bias_ref[...]
            top = jnp.max(masked, axis=-1, keepdims=True)
            expo = jnp.exp2((masked - top) * F32(scale))
            totals.append(jnp.sum(expo, axis=-1, keepdims=True))
            probs[at % 2, rows, :] = expo.astype(BF16)
        weighted = jnp.dot(probs[at % 2], kv_ref[:, :latent], preferred_element_type=F32)
        for head in range(pair):
            rows = slice(head * tokens, (head + 1) * tokens)
            mixed = (weighted[rows, :] / totals[head]).astype(BF16)
            which = at * pair + head
            out = jnp.dot(mixed, w_ref[start + which], preferred_element_type=F32)
            out_ref[:, which * value : (which + 1) * value] = out.astype(BF16)

    score(0)
    for at in range(heads // pair):
        if at + 1 < heads // pair:
            score(at + 1)
        weigh(at)


def attend(start, heads, queries, bias, w_value, kv, scale, after=()):
    tokens, keys = bias.shape
    value = w_value.shape[2]
    return pl.pallas_call(
        functools.partial(attend_kernel, scale * math.log2(math.e), start, heads),
        in_specs=[LOCAL] * 4 + [ANYWHERE] * len(after),
        out_specs=LOCAL,
        out_shape=pltpu.VMEM((tokens, heads * value), BF16),
        scratch_shapes=[
            pltpu.VMEM((2, 2 * tokens, keys), F32),
            pltpu.VMEM((2, 2 * tokens, keys), BF16),
        ],
        compiler_params=params(12),
        cost_estimate=cost(heads << 30, 1024),
        name=f"attend{start}",
    )(held(queries), held(bias), held(w_value), held(kv), *after)


def project_kernel(start, groups, fresh, w_ref, *refs):
    pairs = refs[:groups]
    out_ref, gathered = refs[-2:]
    tokens, depth = pairs[0].shape[1:]
    for side in range(2):
        for at in range(groups):
            gathered[side, at * tokens : (at + 1) * tokens] = pairs[at][side]
    weights = w_ref[start : start + depth]
    each = 2 * tokens
    for side in range(2):
        for row in range(0, groups * tokens, each):
            rows = slice(row, row + each)
            product = jnp.dot(gathered[side, rows], weights, preferred_element_type=F32)
            out_ref[side, rows] = product if fresh else refs[groups][side, rows] + product


def project(start, pairs, w_output, acc):
    groups = len(pairs)
    _, tokens, depth = pairs[0].shape
    columns = w_output.shape[1]
    return pl.pallas_call(
        functools.partial(project_kernel, start, groups, acc is None),
        in_specs=[LOCAL] * (1 + groups + (acc is not None)),
        out_specs=LOCAL,
        out_shape=pltpu.VMEM((2, groups * tokens, columns), F32),
        scratch_shapes=[pltpu.VMEM((2, groups * tokens, depth), BF16)],
        input_output_aliases={} if acc is None else {1 + groups: 0},
        compiler_params=params(12),
        cost_estimate=cost(0, 1024),
        name=f"project{start}",
    )(held(w_output), *map(held, pairs), *([] if acc is None else [held(acc)]))


def finish_kernel(start, keys, far, keep, w_ref, *refs):
    groups = len(keys)
    pairs = refs[:groups]
    acc_ref, out_ref, gathered = refs[groups:]
    tokens, depth = pairs[0].shape[1:]
    me, side = lax.axis_index("ctx"), lax.axis_index("head")
    other = ((me // groups) ^ side ^ (1 - keep)).astype(jnp.int32)
    for at in range(groups):
        gathered[at * tokens : (at + 1) * tokens] = pairs[at][other]
    product = jnp.dot(
        gathered[...], w_ref[start : start + depth], preferred_element_type=F32
    )
    for at, key in enumerate(keys):
        rows = slice(at * tokens, (at + 1) * tokens)
        place = (me ^ key ^ (far * other)) % groups
        to = pl.ds(pl.multiple_of(place * tokens, tokens), tokens)
        out_ref[to, :] = (acc_ref[other, rows] + product[rows]).astype(out_ref.dtype)


def finish(start, keys, far, keep, pairs, w_output, acc, dtype):
    groups = len(pairs)
    _, tokens, depth = pairs[0].shape
    columns = w_output.shape[1]
    rows = groups * tokens
    return pl.pallas_call(
        functools.partial(finish_kernel, start, keys, far, keep),
        in_specs=[LOCAL] * (2 + groups),
        out_specs=LOCAL,
        out_shape=pltpu.VMEM((rows, columns), dtype),
        scratch_shapes=[pltpu.VMEM((rows, depth), BF16)],
        compiler_params=params(12),
        cost_estimate=cost(0, 1024),
        name=f"finish{keep}",
    )(held(w_output), *map(held, pairs), held(acc))


def local(
    q_nope, q_rope, latent_cache, rope_keys, w_absorb, w_value, w_output, span_offset, valid_lengths
):
    head_count, nope_dim, latent = w_absorb.shape
    tokens = q_nope.shape[0]
    rope_dim = rope_keys.shape[1]
    per_shard = latent_cache.shape[0]
    shards = valid_lengths.shape[0]
    value = w_value.shape[2]
    depth = -(-(latent + rope_dim) // LANES) * LANES
    own = -(-per_shard // 32) * 16
    scale = 1.0 / math.sqrt(nope_dim + rope_dim)

    far = basis_of(shards)[0]
    packed = pack(latent_cache, rope_keys, own, depth)
    queries = prep(q_nope, q_rope, w_absorb, depth)
    mine = spread(packed, shards, [queries])
    keys = sorted(mine)
    theirs = {key: sibling(pair) for key, pair in mine.items()}
    owners = [key ^ (far * inner) for key in keys for inner in range(2)]
    bias = mask(span_offset, valid_lengths, owners, tokens, per_shard, own)
    kv = join([mine[key] for key in keys], [theirs[key] for key in keys], per_shard)

    acc = None
    start = 0
    sent = []
    for chunk, piece in enumerate(PIECES):
        heads = piece * head_count // sum(PIECES)
        after = [sent[-2][0]] if chunk > 1 else []
        if chunk > 2:
            after += [sent[-3][key] for key in basis_of(shards)[1:]]
        if chunk > 3:
            after += [sent[-4][key] for key in keys]
        out = attend(start, heads, queries, bias, w_value, kv, scale, after)
        gathered = spread(out, shards)
        pairs = [gathered[key] for key in keys]
        sent.append(gathered)
        row = start * value
        if chunk < len(PIECES) - 1:
            acc = project(row, pairs, w_output, acc)
        start += heads

    given = finish(row, keys, far, 0, pairs, w_output, acc, BF16)
    other = sibling(given)
    kept = finish(row, keys, far, 1, pairs, w_output, acc, F32)
    return (kept + other.astype(F32)).astype(BF16)


def solution(mesh):
    return jax.shard_map(
        local,
        mesh=mesh,
        in_specs=(
            P(("groups", "ctx"), "head"),
            P(("groups", "ctx"), "head"),
            P(("groups", "ctx"), None),
            P(("groups", "ctx"), None),
            P("head", None, None),
            P("head", None, None),
            P("head", "ctx"),
            P("groups"),
            P("groups"),
        ),
        out_specs=P(("groups", "head"), "ctx"),
        check_vma=False,
    )
```

```python
import functools
import math

import jax
import jax.numpy as jnp
from jax import lax
from jax.experimental import pallas as pl
from jax.experimental.pallas import tpu as pltpu
from jax.sharding import PartitionSpec as P

F32 = jnp.float32
BF16 = jnp.bfloat16
MASKED = -1e30
LANES = 128
STEP = 4
PLAN = ((4, 0), (8, 0), (8, 1), (8, 0), (4, 0))
AHEAD_Y = 2
AHEAD_Z = 3
LOCAL = pl.BlockSpec(memory_space=pltpu.VMEM)
ANYWHERE = pl.BlockSpec(memory_space=pl.ANY)
SCALARS = pl.BlockSpec(memory_space=pltpu.SMEM)


def params(mib):
    return pltpu.CompilerParams(vmem_limit_bytes=mib * 1024 * 1024)


def cost(flops, size, exps=0):
    return pl.CostEstimate(flops=flops, bytes_accessed=size, transcendentals=exps)


def held(x):
    return pltpu.with_memory_space_constraint(x, pltpu.VMEM)


def basis_of(shards):
    if shards == 8:
        return (6, 2, 1)
    return tuple(1 << bit for bit in reversed(range(shards.bit_length() - 1)))


def exchange(x, mask, shards):
    return lax.ppermute(x, "ctx", [(i, i ^ mask) for i in range(shards)])


def sibling(x):
    return lax.ppermute(x, "head", [(0, 1), (1, 0)])


def stack_kernel(first_ref, second_ref, *refs):
    out_ref = refs[-1]
    out_ref[0] = first_ref[...]
    out_ref[1] = second_ref[...]


def stack(first, second, after=()):
    return pl.pallas_call(
        stack_kernel,
        in_specs=[LOCAL, LOCAL] + [ANYWHERE] * len(after),
        out_specs=LOCAL,
        out_shape=pltpu.VMEM((2, *first.shape), first.dtype),
        compiler_params=params(2),
        cost_estimate=cost(0, 1024),
        name="stack",
    )(held(first), held(second), *after)


def spread(x, shards, after=()):
    first, *rest = basis_of(shards)
    pairs = {0: stack(x, exchange(x, first, shards), after)}
    for mask in rest:
        pairs.update({key ^ mask: exchange(pair, mask, shards) for key, pair in pairs.items()})
    return pairs


def gate_kernel(x_ref, *refs):
    refs[-1][...] = x_ref[...]


def gate(x, after):
    return pl.pallas_call(
        gate_kernel,
        in_specs=[LOCAL] + [ANYWHERE] * len(after),
        out_specs=LOCAL,
        out_shape=pltpu.VMEM(x.shape, x.dtype),
        compiler_params=params(2),
        cost_estimate=cost(0, 1024),
        name="gate",
    )(held(x), *after)


class Queue:
    def __init__(self, ahead, shards):
        self.ahead, self.shards, self.sent = ahead, shards, []

    def send(self, x, mask, also=()):
        after = self.sent[-self.ahead :][:1] if len(self.sent) >= self.ahead else []
        after = [*after, *also]
        got = exchange(gate(x, after) if after else x, mask, self.shards)
        self.sent.append(got)
        return got


def pack_kernel(own, latent_ref, rope_ref, out_ref):
    rows, latent = latent_ref.shape
    rope = rope_ref.shape[0]
    side = lax.axis_index("head")
    turned = rope_ref[...].astype(F32).T.astype(BF16)
    out_ref[:, latent:] = jnp.zeros((own, out_ref.shape[1] - latent), BF16)
    for at in range(2):
        span = slice(0, own) if at == 0 else slice(rows - own, rows)

        @pl.when(side == at)
        def _(span=span):
            out_ref[:, :latent] = latent_ref[span, :]
            out_ref[:, latent : latent + rope] = turned[span, :]


def pack(latent_cache, rope_keys, own, depth):
    return pl.pallas_call(
        functools.partial(pack_kernel, own),
        in_specs=[LOCAL, LOCAL],
        out_specs=LOCAL,
        out_shape=pltpu.VMEM((own, depth), BF16),
        compiler_params=params(2),
        cost_estimate=cost(0, 1024),
        name="pack",
    )(latent_cache, rope_keys.T)


def mask_kernel(own, owners, span_ref, valid_ref, bias_ref):
    tokens, keys = bias_ref.shape
    per_shard = keys // len(owners)
    me, side = lax.axis_index("ctx"), lax.axis_index("head")
    column = lax.broadcasted_iota(jnp.int32, (1, keys), 1)
    place = jnp.full((1, keys), 2**30, jnp.int32)
    for at, owner in enumerate(owners):
        shard = me ^ owner
        inner = column - at * per_shard
        mine = jnp.where(side == 0, inner, inner + (per_shard - own))
        others = jnp.where(side == 0, inner, inner - own)
        row = jnp.where(inner < own, mine, others)
        here = (inner >= 0) & (inner < per_shard) & (row < valid_ref[shard])
        place = jnp.where(here, row + shard * per_shard, place)
    position = span_ref[0] + me * tokens + lax.broadcasted_iota(jnp.int32, (tokens, keys), 0)
    bias_ref[...] = jnp.where(place <= position, F32(0.0), F32(MASKED))


def mask(span_offset, valid_lengths, owners, tokens, per_shard, own):
    return pl.pallas_call(
        functools.partial(mask_kernel, own, owners),
        in_specs=[SCALARS, SCALARS],
        out_specs=LOCAL,
        out_shape=pltpu.VMEM((tokens, per_shard * len(owners)), F32),
        compiler_params=params(4),
        cost_estimate=cost(0, 1024),
        name="mask",
    )(span_offset, valid_lengths)


def prep_kernel(q_hbm, r_hbm, w_hbm, lat_ref, q_ref, r_ref, w_ref, sem):
    tokens = q_ref.shape[0]
    heads, nope, latent = w_ref.shape
    rope = r_ref.shape[1] // heads
    whole = (
        pltpu.make_async_copy(q_hbm, q_ref, sem.at[0]),
        pltpu.make_async_copy(r_hbm, r_ref, sem.at[1]),
    )
    pieces = [
        pltpu.make_async_copy(
            w_hbm.at[pl.ds(at, STEP)], w_ref.at[pl.ds(at, STEP)], sem.at[2 + at // STEP]
        )
        for at in range(0, heads, STEP)
    ]
    for copy in (*whole, *pieces):
        copy.start()
    lat_ref[:, latent + rope :] = jnp.zeros(
        (heads * tokens, lat_ref.shape[1] - latent - rope), BF16
    )
    for copy in whole:
        copy.wait()
    for head in range(heads):
        if head % STEP == 0:
            pieces[head // STEP].wait()
        rows = slice(head * tokens, (head + 1) * tokens)
        lat = jnp.dot(
            q_ref[:, head * nope : (head + 1) * nope], w_ref[head], preferred_element_type=F32
        )
        lat_ref[rows, :latent] = lat.astype(BF16)
        lat_ref[rows, latent : latent + rope] = r_ref[:, head * rope : (head + 1) * rope]


def prep(q_nope, q_rope, w_absorb, depth):
    heads = w_absorb.shape[0]
    tokens = q_nope.shape[0]
    arrays = (q_nope, q_rope, w_absorb)
    return pl.pallas_call(
        prep_kernel,
        in_specs=[ANYWHERE] * 3,
        out_specs=LOCAL,
        out_shape=pltpu.VMEM((heads * tokens, depth), BF16),
        scratch_shapes=[pltpu.VMEM(x.shape, x.dtype) for x in arrays]
        + [pltpu.SemaphoreType.DMA((2 + heads // STEP,))],
        compiler_params=params(10),
        cost_estimate=cost(0, 1024),
        name="prep",
    )(*(pltpu.with_memory_space_constraint(x, pltpu.HBM) for x in arrays))


def join_kernel(groups, own, *refs):
    mine = refs[:groups]
    theirs = refs[groups : 2 * groups]
    out_ref = refs[-1]
    per_shard = out_ref.shape[0] // (2 * groups)
    rest = per_shard - own
    side = lax.axis_index("head")
    for at in range(2 * groups):
        group, inner = at // 2, at % 2
        start = at * per_shard
        out_ref[start : start + own] = mine[group][inner]
    for half in range(2):

        @pl.when(side == half)
        def _(skip=(1 - half) * (own - rest)):
            for at in range(2 * groups):
                start = at * per_shard + own
                out_ref[start : start + rest] = theirs[at // 2][at % 2, skip : skip + rest]


def join(mine, theirs, per_shard):
    groups = len(mine)
    _, own, depth = mine[0].shape
    return pl.pallas_call(
        functools.partial(join_kernel, groups, own),
        in_specs=[LOCAL] * (2 * groups),
        out_specs=LOCAL,
        out_shape=pltpu.VMEM((2 * groups * per_shard, depth), BF16),
        compiler_params=params(2),
        cost_estimate=cost(0, 1024),
        name="join",
    )(*map(held, mine), *map(held, theirs))


def attend_kernel(scale, start, heads, q_ref, bias_ref, w_ref, kv_ref, *refs):
    out_ref, scores, probs = refs[-3:]
    tokens = bias_ref.shape[0]
    _, latent, value = w_ref.shape
    pair = scores.shape[1] // tokens

    def score(at):
        row = (start + at * pair) * tokens
        scores[at % 2] = lax.dot_general(
            q_ref[row : row + pair * tokens, :],
            kv_ref[...],
            (((1,), (1,)), ((), ())),
            preferred_element_type=F32,
        )

    def weigh(at):
        totals = []
        for head in range(pair):
            rows = slice(head * tokens, (head + 1) * tokens)
            masked = scores[at % 2, rows, :] + bias_ref[...]
            top = jnp.max(masked, axis=-1, keepdims=True)
            expo = jnp.exp2((masked - top) * F32(scale))
            totals.append(jnp.sum(expo, axis=-1, keepdims=True))
            probs[at % 2, rows, :] = expo.astype(BF16)
        weighted = jnp.dot(probs[at % 2], kv_ref[:, :latent], preferred_element_type=F32)
        for head in range(pair):
            rows = slice(head * tokens, (head + 1) * tokens)
            mixed = (weighted[rows, :] / totals[head]).astype(BF16)
            which = at * pair + head
            out = jnp.dot(mixed, w_ref[start + which], preferred_element_type=F32)
            out_ref[:, which * value : (which + 1) * value] = out.astype(BF16)

    score(0)
    for at in range(heads // pair):
        if at + 1 < heads // pair:
            score(at + 1)
        weigh(at)


def attend(start, heads, queries, bias, w_value, kv, scale, after=()):
    tokens, keys = bias.shape
    value = w_value.shape[2]
    return pl.pallas_call(
        functools.partial(attend_kernel, scale * math.log2(math.e), start, heads),
        in_specs=[LOCAL] * 4 + [ANYWHERE] * len(after),
        out_specs=LOCAL,
        out_shape=pltpu.VMEM((tokens, heads * value), BF16),
        scratch_shapes=[
            pltpu.VMEM((2, 2 * tokens, keys), F32),
            pltpu.VMEM((2, 2 * tokens, keys), BF16),
        ],
        compiler_params=params(12),
        cost_estimate=cost(heads << 26, 1024),
        name=f"attend{start}",
    )(held(queries), held(bias), held(w_value), held(kv), *after)


def project_kernel(start, groups, fresh, w_ref, *refs):
    pairs = refs[:groups]
    out_ref, gathered = refs[-2:]
    tokens, depth = pairs[0].shape[1:]
    for side in range(2):
        for at in range(groups):
            gathered[side, at * tokens : (at + 1) * tokens] = pairs[at][side]
    weights = w_ref[start : start + depth]
    each = 2 * tokens
    for side in range(2):
        for row in range(0, groups * tokens, each):
            rows = slice(row, row + each)
            product = jnp.dot(gathered[side, rows], weights, preferred_element_type=F32)
            out_ref[side, rows] = product if fresh else refs[groups][side, rows] + product


def project(start, pairs, w_output, acc):
    groups = len(pairs)
    _, tokens, depth = pairs[0].shape
    columns = w_output.shape[1]
    return pl.pallas_call(
        functools.partial(project_kernel, start, groups, acc is None),
        in_specs=[LOCAL] * (1 + groups + (acc is not None)),
        out_specs=LOCAL,
        out_shape=pltpu.VMEM((2, groups * tokens, columns), F32),
        scratch_shapes=[pltpu.VMEM((2, groups * tokens, depth), BF16)],
        input_output_aliases={} if acc is None else {1 + groups: 0},
        compiler_params=params(12),
        cost_estimate=cost(0, 1024),
        name=f"project{start}",
    )(held(w_output), *map(held, pairs), *([] if acc is None else [held(acc)]))


def finish_kernel(start, keys, far, keep, w_ref, *refs):
    groups = len(keys)
    pairs = refs[:groups]
    acc_ref, out_ref, gathered = refs[groups:]
    tokens, depth = pairs[0].shape[1:]
    me, side = lax.axis_index("ctx"), lax.axis_index("head")
    other = ((me // groups) ^ side ^ (1 - keep)).astype(jnp.int32)
    for at in range(groups):
        gathered[at * tokens : (at + 1) * tokens] = pairs[at][other]
    product = jnp.dot(
        gathered[...], w_ref[start : start + depth], preferred_element_type=F32
    )
    for at, key in enumerate(keys):
        rows = slice(at * tokens, (at + 1) * tokens)
        place = (me ^ key ^ (far * other)) % groups
        to = pl.ds(pl.multiple_of(place * tokens, tokens), tokens)
        out_ref[to, :] = (acc_ref[other, rows] + product[rows]).astype(out_ref.dtype)


def finish(start, keys, far, keep, pairs, w_output, acc, dtype):
    groups = len(pairs)
    _, tokens, depth = pairs[0].shape
    columns = w_output.shape[1]
    rows = groups * tokens
    return pl.pallas_call(
        functools.partial(finish_kernel, start, keys, far, keep),
        in_specs=[LOCAL] * (2 + groups),
        out_specs=LOCAL,
        out_shape=pltpu.VMEM((rows, columns), dtype),
        scratch_shapes=[pltpu.VMEM((rows, depth), BF16)],
        compiler_params=params(12),
        cost_estimate=cost(0, 1024),
        name=f"finish{keep}",
    )(held(w_output), *map(held, pairs), held(acc))


def local(
    q_nope, q_rope, latent_cache, rope_keys, w_absorb, w_value, w_output, span_offset, valid_lengths
):
    head_count, nope_dim, latent = w_absorb.shape
    tokens = q_nope.shape[0]
    rope_dim = rope_keys.shape[1]
    per_shard = latent_cache.shape[0]
    shards = valid_lengths.shape[0]
    value = w_value.shape[2]
    depth = -(-(latent + rope_dim) // LANES) * LANES
    own = -(-per_shard // 32) * 16
    scale = 1.0 / math.sqrt(nope_dim + rope_dim)

    far = basis_of(shards)[0]
    packed = pack(latent_cache, rope_keys, own, depth)
    queries = prep(q_nope, q_rope, w_absorb, depth)
    mine = spread(packed, shards, [queries])
    keys = sorted(mine)
    theirs = {key: sibling(pair) for key, pair in mine.items()}
    owners = [key ^ (far * inner) for key in keys for inner in range(2)]
    bias = mask(span_offset, valid_lengths, owners, tokens, per_shard, own)
    kv = join([mine[key] for key in keys], [theirs[key] for key in keys], per_shard)

    heads = [count * head_count // 32 for count, _ in PLAN]
    starts = [sum(heads[:chunk]) for chunk in range(len(heads))]
    along_z = Queue(AHEAD_Z, shards)
    along_y = Queue(AHEAD_Y, shards)
    outs, crossed, pairs, accs = [], [], [], [None]
    def last_step(chunk):
        base, side, near = pairs[chunk]
        got = along_z.send(side, 2) if PLAN[chunk][1] else along_y.send(near, 1)
        pairs[chunk].append(got)

    for stage in range(len(heads) + 1):
        if stage < len(heads):
            outs.append(attend(starts[stage], heads[stage], queries, bias, w_value, kv, scale))
        if stage > 0 and shards == 8:
            base = stack(outs[stage - 1], crossed[stage - 1])
            near = along_z.send(base, 2)
            side = along_y.send(base, 1, [accs[-2]] if stage > 4 else [])
        if stage < len(heads):
            crossed.append(along_z.send(outs[stage], far))
        if stage > 0:
            if shards != 8:
                gathered = spread(outs[stage - 1], shards)
                pairs.append([gathered[key] for key in keys])
            elif PLAN[stage - 1][1]:
                pairs.append([base, side, near, along_z.send(side, 2)])
            else:
                pairs.append([base, side, near, along_y.send(near, 1)])
            if stage < len(heads):
                row = starts[stage - 1] * value
                accs.append(project(row, pairs[-1], w_output, accs[-1]))

    row, pairs, acc = starts[-1] * value, pairs[-1], accs[-1]
    given = finish(row, keys, far, 0, pairs, w_output, acc, BF16)
    other = sibling(given)
    kept = finish(row, keys, far, 1, pairs, w_output, acc, F32)
    return (kept + other.astype(F32)).astype(BF16)


def solution(mesh):
    return jax.shard_map(
        local,
        mesh=mesh,
        in_specs=(
            P(("groups", "ctx"), "head"),
            P(("groups", "ctx"), "head"),
            P(("groups", "ctx"), None),
            P(("groups", "ctx"), None),
            P("head", None, None),
            P("head", None, None),
            P("head", "ctx"),
            P("groups"),
            P("groups"),
        ),
        out_specs=P(("groups", "head"), "ctx"),
        check_vma=False,
    )
```

```python
import functools
import math

import jax
import jax.numpy as jnp
from jax import lax
from jax.experimental import pallas as pl
from jax.experimental.pallas import tpu as pltpu
from jax.sharding import PartitionSpec as P

F32 = jnp.float32
BF16 = jnp.bfloat16
MASKED = -1e30
LANES = 128
STEP = 4
PLAN = ((4, 0), (8, 0), (6, 0), (8, 0), (6, 1))
FAR, SIDE, CROSS, NEAR, BOTH = "far", "side", "cross", "near", "both"
ATTEND, STACK, PROJECT, OWN = "attend", "stack", "project", "own"
ORDER = (
    (ATTEND, 0), (ATTEND, 1), (STACK, 0), (FAR, 1), (ATTEND, 2), (BOTH, 0, (SIDE, 1), (SIDE, 2)),
    (CROSS, 0), (FAR, 2), (STACK, 1, (FAR, 0)), (ATTEND, 3, (CROSS, 0)), (ATTEND, 4),
    (CROSS, 1, (BOTH, 0)), (PROJECT, 0, (SIDE, 3)), (STACK, 2), (FAR, 3, (NEAR, 1)),
    (CROSS, 2, (CROSS, 1)), (FAR, 4, (NEAR, 2)), (BOTH, 2, (CROSS, 2)), (STACK, 3),
    (CROSS, 3, (BOTH, 1)), (PROJECT, 1), (STACK, 4), (CROSS, 4), (PROJECT, 2), (BOTH, 3), (BOTH, 4),
    (PROJECT, 3, (NEAR, 4)),
)
LOCAL = pl.BlockSpec(memory_space=pltpu.VMEM)
ANYWHERE = pl.BlockSpec(memory_space=pl.ANY)
SCALARS = pl.BlockSpec(memory_space=pltpu.SMEM)


def params(mib):
    return pltpu.CompilerParams(vmem_limit_bytes=mib * 1024 * 1024)


def cost(flops, size, exps=0):
    return pl.CostEstimate(flops=flops, bytes_accessed=size, transcendentals=exps)


def held(x):
    return pltpu.with_memory_space_constraint(x, pltpu.VMEM)


def basis_of(shards):
    if shards == 8:
        return (6, 2, 1)
    return tuple(1 << bit for bit in reversed(range(shards.bit_length() - 1)))


def exchange(x, mask, shards):
    return lax.ppermute(x, "ctx", [(i, i ^ mask) for i in range(shards)])


def sibling(x):
    return lax.ppermute(x, "head", [(0, 1), (1, 0)])


def stack_kernel(first_ref, second_ref, *refs):
    out_ref = refs[-1]
    out_ref[0] = first_ref[...]
    out_ref[1] = second_ref[...]


def stack(first, second, after=()):
    return pl.pallas_call(
        stack_kernel,
        in_specs=[LOCAL, LOCAL] + [ANYWHERE] * len(after),
        out_specs=LOCAL,
        out_shape=pltpu.VMEM((2, *first.shape), first.dtype),
        compiler_params=params(2),
        cost_estimate=cost(0, 1024),
        name="stack",
    )(held(first), held(second), *after)


def spread(x, shards, after=()):
    first, *rest = basis_of(shards)
    pairs = {0: stack(x, exchange(x, first, shards), after)}
    for mask in rest:
        pairs.update({key ^ mask: exchange(pair, mask, shards) for key, pair in pairs.items()})
    return pairs


def gate_kernel(x_ref, *refs):
    refs[-1][...] = x_ref[...]


def gate(x, after):
    return pl.pallas_call(
        gate_kernel,
        in_specs=[LOCAL] + [ANYWHERE] * len(after),
        out_specs=LOCAL,
        out_shape=pltpu.VMEM(x.shape, x.dtype),
        compiler_params=params(2),
        cost_estimate=cost(0, 1024),
        name="gate",
    )(held(x), *after)


def pack_kernel(own, latent_hbm, rope_hbm, out_ref, latent_ref, rope_ref, sem):
    copies = (
        pltpu.make_async_copy(latent_hbm, latent_ref, sem.at[0]),
        pltpu.make_async_copy(rope_hbm, rope_ref, sem.at[1]),
    )
    for copy in copies:
        copy.start()
    rows, latent = latent_ref.shape
    rope = rope_ref.shape[0]
    side = lax.axis_index("head")
    out_ref[:, latent:] = jnp.zeros((own, out_ref.shape[1] - latent), BF16)
    for copy in copies:
        copy.wait()
    turned = rope_ref[...].astype(F32).T.astype(BF16)
    for at in range(2):
        span = slice(0, own) if at == 0 else slice(rows - own, rows)

        @pl.when(side == at)
        def _(span=span):
            out_ref[:, :latent] = latent_ref[span, :]
            out_ref[:, latent : latent + rope] = turned[span, :]


def pack(latent_cache, rope_keys, own, depth):
    arrays = (latent_cache, rope_keys.T)
    return pl.pallas_call(
        functools.partial(pack_kernel, own),
        in_specs=[ANYWHERE] * 2,
        out_specs=LOCAL,
        out_shape=pltpu.VMEM((own, depth), BF16),
        scratch_shapes=[pltpu.VMEM(x.shape, x.dtype) for x in arrays]
        + [pltpu.SemaphoreType.DMA((2,))],
        compiler_params=params(2),
        cost_estimate=cost(0, 1024),
        name="pack",
    )(*(pltpu.with_memory_space_constraint(x, pltpu.HBM) for x in arrays))


def mask_kernel(own, owners, span_ref, valid_ref, bias_ref):
    tokens, keys = bias_ref.shape
    per_shard = keys // len(owners)
    me, side = lax.axis_index("ctx"), lax.axis_index("head")
    column = lax.broadcasted_iota(jnp.int32, (1, keys), 1)
    place = jnp.full((1, keys), 2**30, jnp.int32)
    for at, owner in enumerate(owners):
        shard = me ^ owner
        inner = column - at * per_shard
        mine = jnp.where(side == 0, inner, inner + (per_shard - own))
        others = jnp.where(side == 0, inner, inner - own)
        row = jnp.where(inner < own, mine, others)
        here = (inner >= 0) & (inner < per_shard) & (row < valid_ref[shard])
        place = jnp.where(here, row + shard * per_shard, place)
    position = span_ref[0] + me * tokens + lax.broadcasted_iota(jnp.int32, (tokens, keys), 0)
    bias_ref[...] = jnp.where(place <= position, F32(0.0), F32(MASKED))


def mask(span_offset, valid_lengths, owners, tokens, per_shard, own):
    return pl.pallas_call(
        functools.partial(mask_kernel, own, owners),
        in_specs=[SCALARS, SCALARS],
        out_specs=LOCAL,
        out_shape=pltpu.VMEM((tokens, per_shard * len(owners)), F32),
        compiler_params=params(4),
        cost_estimate=cost(0, 1024),
        name="mask",
    )(span_offset, valid_lengths)


def prep_kernel(q_hbm, r_hbm, w_hbm, lat_ref, q_ref, r_ref, w_ref, sem):
    tokens = q_ref.shape[0]
    heads, nope, latent = w_ref.shape
    rope = r_ref.shape[1] // heads
    whole = (
        pltpu.make_async_copy(q_hbm, q_ref, sem.at[0]),
        pltpu.make_async_copy(r_hbm, r_ref, sem.at[1]),
    )
    pieces = [
        pltpu.make_async_copy(
            w_hbm.at[pl.ds(at, STEP)], w_ref.at[pl.ds(at, STEP)], sem.at[2 + at // STEP]
        )
        for at in range(0, heads, STEP)
    ]
    for copy in (*whole, *pieces):
        copy.start()
    lat_ref[:, latent + rope :] = jnp.zeros(
        (heads * tokens, lat_ref.shape[1] - latent - rope), BF16
    )
    for copy in whole:
        copy.wait()
    for head in range(heads):
        if head % STEP == 0:
            pieces[head // STEP].wait()
        rows = slice(head * tokens, (head + 1) * tokens)
        lat = jnp.dot(
            q_ref[:, head * nope : (head + 1) * nope], w_ref[head], preferred_element_type=F32
        )
        lat_ref[rows, :latent] = lat.astype(BF16)
        lat_ref[rows, latent : latent + rope] = r_ref[:, head * rope : (head + 1) * rope]


def prep(q_nope, q_rope, w_absorb, depth):
    heads = w_absorb.shape[0]
    tokens = q_nope.shape[0]
    arrays = (q_nope, q_rope, w_absorb)
    return pl.pallas_call(
        prep_kernel,
        in_specs=[ANYWHERE] * 3,
        out_specs=LOCAL,
        out_shape=pltpu.VMEM((heads * tokens, depth), BF16),
        scratch_shapes=[pltpu.VMEM(x.shape, x.dtype) for x in arrays]
        + [pltpu.SemaphoreType.DMA((2 + heads // STEP,))],
        compiler_params=params(10),
        cost_estimate=cost(0, 1024),
        name="prep",
    )(*(pltpu.with_memory_space_constraint(x, pltpu.HBM) for x in arrays))


def join_kernel(groups, own, *refs):
    mine = refs[:groups]
    theirs = refs[groups : 2 * groups]
    out_ref = refs[-1]
    per_shard = out_ref.shape[0] // (2 * groups)
    rest = per_shard - own
    side = lax.axis_index("head")
    for at in range(2 * groups):
        group, inner = at // 2, at % 2
        start = at * per_shard
        out_ref[start : start + own] = mine[group][inner]
    for half in range(2):

        @pl.when(side == half)
        def _(skip=(1 - half) * (own - rest)):
            for at in range(2 * groups):
                start = at * per_shard + own
                out_ref[start : start + rest] = theirs[at // 2][at % 2, skip : skip + rest]


def join(mine, theirs, per_shard):
    groups = len(mine)
    _, own, depth = mine[0].shape
    return pl.pallas_call(
        functools.partial(join_kernel, groups, own),
        in_specs=[LOCAL] * (2 * groups),
        out_specs=LOCAL,
        out_shape=pltpu.VMEM((2 * groups * per_shard, depth), BF16),
        compiler_params=params(2),
        cost_estimate=cost(0, 1024),
        name="join",
    )(*map(held, mine), *map(held, theirs))


def attend_kernel(scale, start, heads, q_ref, bias_ref, w_ref, kv_ref, *refs):
    out_ref, scores, probs = refs[-3:]
    tokens = bias_ref.shape[0]
    _, latent, value = w_ref.shape
    pair = scores.shape[1] // tokens

    def score(at):
        row = (start + at * pair) * tokens
        scores[at % 2] = lax.dot_general(
            q_ref[row : row + pair * tokens, :],
            kv_ref[...],
            (((1,), (1,)), ((), ())),
            preferred_element_type=F32,
        )

    def weigh(at):
        totals = []
        for head in range(pair):
            rows = slice(head * tokens, (head + 1) * tokens)
            masked = scores[at % 2, rows, :] + bias_ref[...]
            top = jnp.max(masked, axis=-1, keepdims=True)
            expo = jnp.exp2((masked - top) * F32(scale))
            totals.append(jnp.sum(expo, axis=-1, keepdims=True))
            probs[at % 2, rows, :] = expo.astype(BF16)
        weighted = jnp.dot(probs[at % 2], kv_ref[:, :latent], preferred_element_type=F32)
        for head in range(pair):
            rows = slice(head * tokens, (head + 1) * tokens)
            mixed = (weighted[rows, :] / totals[head]).astype(BF16)
            which = at * pair + head
            out = jnp.dot(mixed, w_ref[start + which], preferred_element_type=F32)
            out_ref[:, which * value : (which + 1) * value] = out.astype(BF16)

    score(0)
    for at in range(heads // pair):
        if at + 1 < heads // pair:
            score(at + 1)
        weigh(at)


def attend(start, heads, queries, bias, w_value, kv, scale, after=()):
    tokens, keys = bias.shape
    value = w_value.shape[2]
    return pl.pallas_call(
        functools.partial(attend_kernel, scale * math.log2(math.e), start, heads),
        in_specs=[LOCAL] * 4 + [ANYWHERE] * len(after),
        out_specs=LOCAL,
        out_shape=pltpu.VMEM((tokens, heads * value), BF16),
        scratch_shapes=[
            pltpu.VMEM((2, 2 * tokens, keys), F32),
            pltpu.VMEM((2, 2 * tokens, keys), BF16),
        ],
        compiler_params=params(12),
        cost_estimate=cost(0, 1024),
        name=f"attend{start}",
    )(held(queries), held(bias), held(w_value), held(kv), *after)


def gather_into(rows_of, parts, side):
    tokens = parts[0][0].shape[-2]
    for at, part in enumerate(parts):
        rows = pl.ds(at * tokens, tokens)
        if len(part) == 1:
            rows_of[rows] = part[0][side]
        elif isinstance(side, int):
            rows_of[rows] = part[side][...]
        else:
            for which in range(2):

                @pl.when(side == which)
                def _(rows=rows, part=part, which=which):
                    rows_of[rows] = part[which][...]


def grouped(refs, sizes):
    refs = iter(refs)
    return [tuple(next(refs) for _ in range(size)) for size in sizes]


def project_kernel(start, sizes, fresh, w_ref, *refs):
    out_ref, gathered = refs[-2:]
    parts = grouped(refs, sizes)
    tokens, depth = parts[0][0].shape[-2:]
    for side in range(2):
        gather_into(gathered.at[side], parts, side)
    weights = w_ref[start : start + depth]
    each = 2 * tokens
    for side in range(2):
        for row in range(0, len(parts) * tokens, each):
            rows = slice(row, row + each)
            product = jnp.dot(gathered[side, rows], weights, preferred_element_type=F32)
            out_ref[side, rows] = product if fresh else refs[sum(sizes)][side, rows] + product


def project(start, parts, w_output, acc, after=()):
    sizes = tuple(map(len, parts))
    blocks = [block for part in parts for block in part]
    tokens, depth = blocks[0].shape[-2:]
    columns = w_output.shape[1]
    operands = [w_output, *blocks] + ([] if acc is None else [acc])
    return pl.pallas_call(
        functools.partial(project_kernel, start, sizes, acc is None),
        in_specs=[LOCAL] * len(operands) + [ANYWHERE] * len(after),
        out_specs=LOCAL,
        out_shape=pltpu.VMEM((2, len(parts) * tokens, columns), F32),
        scratch_shapes=[pltpu.VMEM((2, len(parts) * tokens, depth), BF16)],
        input_output_aliases={} if acc is None else {len(operands) - 1: 0},
        compiler_params=params(12),
        cost_estimate=cost(0, 1024),
        name=f"project{start}",
    )(*map(held, operands), *after)


def finish_kernel(start, keys, far, keep, sizes, w_ref, *refs):
    groups = len(keys)
    acc_ref, out_ref, gathered = refs[-3:]
    parts = grouped(refs, sizes)
    tokens, depth = parts[0][0].shape[-2:]
    me, side = lax.axis_index("ctx"), lax.axis_index("head")
    other = ((me // groups) ^ side ^ (1 - keep)).astype(jnp.int32)
    gather_into(gathered, parts, other)
    product = jnp.dot(
        gathered[...], w_ref[start : start + depth], preferred_element_type=F32
    )
    for at, key in enumerate(keys):
        rows = slice(at * tokens, (at + 1) * tokens)
        place = (me ^ key ^ (far * other)) % groups
        to = pl.ds(pl.multiple_of(place * tokens, tokens), tokens)
        out_ref[to, :] = (acc_ref[other, rows] + product[rows]).astype(out_ref.dtype)


def finish(start, keys, far, keep, parts, w_output, acc, dtype):
    sizes = tuple(map(len, parts))
    blocks = [block for part in parts for block in part]
    tokens, depth = blocks[0].shape[-2:]
    columns = w_output.shape[1]
    rows = len(parts) * tokens
    return pl.pallas_call(
        functools.partial(finish_kernel, start, keys, far, keep, sizes),
        in_specs=[LOCAL] * (2 + len(blocks)),
        out_specs=LOCAL,
        out_shape=pltpu.VMEM((rows, columns), dtype),
        scratch_shapes=[pltpu.VMEM((rows, depth), BF16)],
        compiler_params=params(12),
        cost_estimate=cost(0, 1024),
        name=f"finish{keep}",
    )(*map(held, [w_output, *blocks, acc]))


def overlap(heads, starts, queries, bias, w_value, kv, w_output, scale):
    value = w_value.shape[2]
    got, ready = {}, {}
    last, acc = [], None
    held_back = {entry[:2] for entry in ORDER}

    def send(name, chunk, after=None):
        nonlocal last
        x, mask = ready.pop((name, chunk))
        if after is not None:
            x = gate(x, after)
            last = [x]
        got[name, chunk] = exchange(x, mask, 8)
        if name == FAR:
            offer(CROSS, chunk, got[FAR, chunk], 1)
        if name == NEAR and not PLAN[chunk][1]:
            offer(BOTH, chunk, got[NEAR, chunk], 1)

    def offer(name, chunk, x, mask):
        ready[name, chunk] = x, mask
        if (name, chunk) not in held_back:
            send(name, chunk)

    def parts_of(chunk):
        apart = [(OWN, FAR), (SIDE, CROSS)], [(NEAR,), (BOTH,)]
        return [tuple(got[name, chunk] for name in names) for half in apart for names in half]

    for action, chunk, *waits in ORDER:
        after = last + [got[wait] for wait in waits]
        if action == ATTEND:
            out = attend(starts[chunk], heads[chunk], queries, bias, w_value, kv, scale, after)
            last = [out]
            got[OWN, chunk] = out
            offer(FAR, chunk, out, 6)
            offer(SIDE, chunk, out, 1)
        elif action == STACK:
            base = stack(got[OWN, chunk], got[FAR, chunk], after)
            last = [base]
            offer(NEAR, chunk, base, 2)
        elif action == PROJECT:
            acc = project(starts[chunk] * value, parts_of(chunk), w_output, acc, after)
            last = [acc]
        elif action == BOTH and PLAN[chunk][1]:
            pair = stack(got[SIDE, chunk], got[CROSS, chunk], after)
            last = [pair]
            got[BOTH, chunk] = exchange(pair, 2, 8)
        else:
            send(action, chunk, after)
    return parts_of(len(heads) - 1), acc


def local(
    q_nope, q_rope, latent_cache, rope_keys, w_absorb, w_value, w_output, span_offset, valid_lengths
):
    head_count, nope_dim, latent = w_absorb.shape
    tokens = q_nope.shape[0]
    rope_dim = rope_keys.shape[1]
    per_shard = latent_cache.shape[0]
    shards = valid_lengths.shape[0]
    value = w_value.shape[2]
    depth = -(-(latent + rope_dim) // LANES) * LANES
    own = -(-per_shard // 32) * 16
    scale = 1.0 / math.sqrt(nope_dim + rope_dim)

    far = basis_of(shards)[0]
    packed = pack(latent_cache, rope_keys, own, depth)
    queries = prep(q_nope, q_rope, w_absorb, depth)
    mine = spread(packed, shards, [queries])
    keys = sorted(mine)
    theirs = {key: sibling(pair) for key, pair in mine.items()}
    owners = [key ^ (far * inner) for key in keys for inner in range(2)]
    bias = mask(span_offset, valid_lengths, owners, tokens, per_shard, own)
    kv = join([mine[key] for key in keys], [theirs[key] for key in keys], per_shard)

    heads = [count * head_count // 32 for count, _ in PLAN]
    starts = [sum(heads[:chunk]) for chunk in range(len(heads))]
    if shards == 8:
        parts, acc = overlap(heads, starts, queries, bias, w_value, kv, w_output, scale)
    else:
        acc = None
        for chunk, start in enumerate(starts):
            out = attend(start, heads[chunk], queries, bias, w_value, kv, scale)
            gathered = spread(out, shards)
            parts = [(gathered[key],) for key in keys]
            if chunk < len(heads) - 1:
                acc = project(start * value, parts, w_output, acc)
    row = starts[-1] * value

    given = finish(row, keys, far, 0, parts, w_output, acc, BF16)
    other = sibling(given)
    kept = finish(row, keys, far, 1, parts, w_output, acc, F32)
    return (kept + other.astype(F32)).astype(BF16)


def solution(mesh):
    return jax.shard_map(
        local,
        mesh=mesh,
        in_specs=(
            P(("groups", "ctx"), "head"),
            P(("groups", "ctx"), "head"),
            P(("groups", "ctx"), None),
            P(("groups", "ctx"), None),
            P("head", None, None),
            P("head", None, None),
            P("head", "ctx"),
            P("groups"),
            P("groups"),
        ),
        out_specs=P(("groups", "head"), "ctx"),
        check_vma=False,
    )
```

```python
import functools
import math

import jax
import jax.numpy as jnp
from jax import lax
from jax.experimental import pallas as pl
from jax.experimental.pallas import tpu as pltpu
from jax.sharding import PartitionSpec as P

F32 = jnp.float32
BF16 = jnp.bfloat16
MASKED = -1e30
LANES = 128
STEP = 4
WIDE = 256
ROWS = 32
PLAN = ((4, 0, 0), (8, 0, 0), (6, 0, 0), (8, 0, 0), (6, 1, 0))
FAR, SIDE, CROSS, NEAR, BOTH = "far", "side", "cross", "near", "both"
ATTEND, STACK, PROJECT, OWN = "attend", "stack", "project", "own"
ORDER = (
    (ATTEND, 0), (ATTEND, 1), (CROSS, 0), (STACK, 0), (ATTEND, 2), (STACK, 1, (FAR, 0)), (FAR, 2),
    (BOTH, 0, (SIDE, 1), (SIDE, 2)), (ATTEND, 3, (CROSS, 0)), (ATTEND, 4),
    (CROSS, 1, (BOTH, 0), (FAR, 1)), (PROJECT, 0, (SIDE, 3)), (STACK, 2), (FAR, 3, (NEAR, 1)),
    (CROSS, 2, (CROSS, 1)), (BOTH, 1, (SIDE, 4)), (FAR, 4, (NEAR, 2)), (BOTH, 2, (CROSS, 2)),
    (STACK, 3), (CROSS, 3, (BOTH, 1)), (PROJECT, 1, (NEAR, 1)), (CROSS, 4), (STACK, 4),
    (PROJECT, 2), (BOTH, 4), (PROJECT, 3, (NEAR, 4)),
)
LOCAL = pl.BlockSpec(memory_space=pltpu.VMEM)
ANYWHERE = pl.BlockSpec(memory_space=pl.ANY)
SCALARS = pl.BlockSpec(memory_space=pltpu.SMEM)


def params(mib):
    return pltpu.CompilerParams(vmem_limit_bytes=mib * 1024 * 1024)


def cost(flops, size, exps=0):
    return pl.CostEstimate(flops=flops, bytes_accessed=size, transcendentals=exps)


def held(x):
    return pltpu.with_memory_space_constraint(x, pltpu.VMEM)


def basis_of(shards):
    if shards == 8:
        return (6, 2, 1)
    return tuple(1 << bit for bit in reversed(range(shards.bit_length() - 1)))


def exchange(x, mask, shards):
    return lax.ppermute(x, "ctx", [(i, i ^ mask) for i in range(shards)])


def sibling(x):
    return lax.ppermute(x, "head", [(0, 1), (1, 0)])


def stack_kernel(first_ref, second_ref, *refs):
    out_ref = refs[-1]
    out_ref[0] = first_ref[...]
    out_ref[1] = second_ref[...]


def stack(first, second, after=()):
    return pl.pallas_call(
        stack_kernel,
        in_specs=[LOCAL, LOCAL] + [ANYWHERE] * len(after),
        out_specs=LOCAL,
        out_shape=pltpu.VMEM((2, *first.shape), first.dtype),
        compiler_params=params(2),
        cost_estimate=cost(0, 1024),
        name="stack",
    )(held(first), held(second), *after)


def spread(x, shards, after=()):
    first, *rest = basis_of(shards)
    pairs = {0: stack(x, exchange(x, first, shards), after)}
    for mask in rest:
        pairs.update({key ^ mask: exchange(pair, mask, shards) for key, pair in pairs.items()})
    return pairs


def gate_kernel(x_ref, *refs):
    refs[-1][...] = x_ref[...]


def gate(x, after):
    return pl.pallas_call(
        gate_kernel,
        in_specs=[LOCAL] + [ANYWHERE] * len(after),
        out_specs=LOCAL,
        out_shape=pltpu.VMEM(x.shape, x.dtype),
        compiler_params=params(2),
        cost_estimate=cost(0, 1024),
        name="gate",
    )(held(x), *after)


def pack_kernel(latent_hbm, rope_hbm, out_ref, latent_ref, rope_ref, sem):
    copies = (
        pltpu.make_async_copy(latent_hbm, latent_ref, sem.at[0]),
        pltpu.make_async_copy(rope_hbm, rope_ref, sem.at[1]),
    )
    for copy in copies:
        copy.start()
    rows, latent = latent_ref.shape
    rope = rope_ref.shape[0]
    tiles = latent // LANES // 2
    pairs, own = packed_rows(rows)
    side = lax.axis_index("head")
    for copy in copies:
        copy.wait()
    turned = rope_ref[...].astype(F32).T.astype(BF16)
    for at in range(2):

        @pl.when(side == at)
        def _(at=at):
            for tile in range(tiles):
                lanes = slice((at * tiles + tile) * LANES, (at * tiles + tile + 1) * LANES)
                out_ref[tile * rows : (tile + 1) * rows, :] = latent_ref[:, lanes]
            first = at * (pairs - own)
            to = slice(tiles * rows, tiles * rows + own)
            out_ref[to, :rope] = turned[first : first + own, :]
            second = first + rows - pairs
            out_ref[to, rope:] = turned[second : second + own, :]


def packed_rows(rows):
    pairs = -(-rows // 32) * 16
    return pairs, -(-pairs // 32) * 16


def pack(latent_cache, rope_keys):
    arrays = (latent_cache, rope_keys.T)
    rows, latent = latent_cache.shape
    _, own = packed_rows(rows)
    return pl.pallas_call(
        pack_kernel,
        in_specs=[ANYWHERE] * 2,
        out_specs=LOCAL,
        out_shape=pltpu.VMEM((latent // LANES // 2 * rows + own, LANES), BF16),
        scratch_shapes=[pltpu.VMEM(x.shape, x.dtype) for x in arrays]
        + [pltpu.SemaphoreType.DMA((2,))],
        compiler_params=params(2),
        cost_estimate=cost(0, 1024),
        name="pack",
    )(*(pltpu.with_memory_space_constraint(x, pltpu.HBM) for x in arrays))


def prep_kernel(
    owners, q_hbm, r_hbm, w_hbm, span_ref, valid_ref, lat_ref, bias_ref, q_ref, r_ref, w_ref, sem
):
    tokens, keys = bias_ref.shape
    heads, nope, latent = w_ref.shape
    rope = r_ref.shape[1] // heads
    whole = (
        pltpu.make_async_copy(q_hbm, q_ref, sem.at[0]),
        pltpu.make_async_copy(r_hbm, r_ref, sem.at[1]),
    )
    pieces = [
        pltpu.make_async_copy(
            w_hbm.at[pl.ds(at, STEP)], w_ref.at[pl.ds(at, STEP)], sem.at[2 + at // STEP]
        )
        for at in range(0, heads, STEP)
    ]
    for copy in (*whole, *pieces):
        copy.start()

    per_shard = keys // len(owners)
    me = lax.axis_index("ctx")
    column = lax.broadcasted_iota(jnp.int32, (1, keys), 1)
    place = jnp.full((1, keys), 2**30, jnp.int32)
    for at, owner in enumerate(owners):
        shard = me ^ owner
        row = column - at * per_shard
        here = (row >= 0) & (row < valid_ref[shard])
        here = here & (row < per_shard)
        place = jnp.where(here, row + shard * per_shard, place)
    position = span_ref[0] + me * tokens + lax.broadcasted_iota(jnp.int32, (tokens, keys), 0)
    bias_ref[...] = jnp.where(place <= position, F32(0.0), F32(MASKED))

    for copy in whole:
        copy.wait()
    for head in range(heads):
        if head % STEP == 0:
            pieces[head // STEP].wait()
        rows = slice(head * tokens, (head + 1) * tokens)
        lat = jnp.dot(
            q_ref[:, head * nope : (head + 1) * nope], w_ref[head], preferred_element_type=F32
        )
        lat_ref[rows, :latent] = lat.astype(BF16)
        turned = r_ref[:, head * rope : (head + 1) * rope]
        lat_ref[rows, latent : latent + rope] = turned
        lat_ref[rows, latent + rope :] = turned


def prep(q_nope, q_rope, w_absorb, span_offset, valid_lengths, owners, per_shard):
    heads, _, latent = w_absorb.shape
    tokens = q_nope.shape[0]
    arrays = (q_nope, q_rope, w_absorb)
    return pl.pallas_call(
        functools.partial(prep_kernel, owners),
        in_specs=[ANYWHERE] * 3 + [SCALARS] * 2,
        out_specs=[LOCAL] * 2,
        out_shape=[
            pltpu.VMEM((heads * tokens, latent + LANES), BF16),
            pltpu.VMEM((tokens, per_shard * len(owners)), F32),
        ],
        scratch_shapes=[pltpu.VMEM(x.shape, x.dtype) for x in arrays]
        + [pltpu.SemaphoreType.DMA((2 + heads // STEP,))],
        compiler_params=params(12),
        cost_estimate=cost(0, 1024),
        name="prep",
    )(*(pltpu.with_memory_space_constraint(x, pltpu.HBM) for x in arrays), span_offset, valid_lengths)


def join_kernel(groups, *refs):
    mine = refs[:groups]
    theirs = refs[groups : 2 * groups]
    out_ref = refs[-1]
    rows = out_ref.shape[0] // (2 * groups)
    latent = out_ref.shape[1] - LANES
    tiles = latent // LANES // 2
    pairs, own = packed_rows(rows)
    side = lax.axis_index("head")
    half = lax.broadcasted_iota(jnp.int32, (pairs, LANES), 1) < LANES // 2
    nothing = jnp.zeros((pairs, LANES), BF16)
    for which in range(2):

        @pl.when(side == which)
        def _(which=which):
            for at in range(2 * groups):
                start = at * rows
                sides = [mine[at // 2], theirs[at // 2]][:: 1 - 2 * which]
                for tile in range(2 * tiles):
                    block = sides[tile // tiles][at % 2, tile % tiles * rows : (tile % tiles + 1) * rows]
                    out_ref[start : start + rows, tile * LANES : (tile + 1) * LANES] = block
                low = sides[0][at % 2, tiles * rows : tiles * rows + own]
                high = sides[1][at % 2, tiles * rows + 2 * own - pairs : tiles * rows + own]
                both = jnp.concatenate([low, high], axis=0)
                out_ref[start : start + pairs, latent:] = jnp.where(half, both, nothing)
                rest = jnp.where(half, nothing, both)[2 * pairs - rows :]
                out_ref[start + pairs : start + rows, latent:] = rest


def join(mine, theirs, per_shard, depth):
    groups = len(mine)
    return pl.pallas_call(
        functools.partial(join_kernel, groups),
        in_specs=[LOCAL] * (2 * groups),
        out_specs=LOCAL,
        out_shape=pltpu.VMEM((2 * groups * per_shard, depth), BF16),
        compiler_params=params(4),
        cost_estimate=cost(0, 1024),
        name="join",
    )(*map(held, mine), *map(held, theirs))


def interleave(first, second):
    steps = [((at + 0.5) / len(x), which, step) for which, x in enumerate((first, second)) for at, step in enumerate(x)]
    for *_, step in sorted(steps, key=lambda entry: entry[:2]):
        step()


def attend_kernel(scale, start, heads, q_ref, bias_ref, w_ref, kv_ref, *refs):
    out_ref, scores, probs, totals, mixed = refs[-5:]
    tokens, keys = bias_ref.shape
    _, latent, value = w_ref.shape
    block = scores.shape[1]
    pair = block // tokens

    def score(at):
        row = start * tokens + at * block

        def part(low):
            span = slice(low, min(low + WIDE, keys))
            scores[at % 2, :, span] = lax.dot_general(
                q_ref[row : row + block, :],
                kv_ref[span, :],
                (((1,), (1,)), ((), ())),
                preferred_element_type=F32,
            )

        return [functools.partial(part, low) for low in range(0, keys, WIDE)]

    def soften(at):
        def part(low):
            rows = slice(low, low + ROWS)
            masked = scores[at % 2, rows, :] + bias_ref[low % tokens : low % tokens + ROWS, :]
            top = jnp.max(masked, axis=-1, keepdims=True)
            expo = jnp.exp2((masked - top) * F32(scale))
            totals[at % 2, rows, :] = jnp.sum(expo, axis=-1, keepdims=True)
            probs[at % 2, rows, :] = expo.astype(BF16)

        return [functools.partial(part, low) for low in range(0, block, ROWS)]

    def weigh(at):
        def part(low):
            span = slice(low, low + WIDE)
            weighted = jnp.dot(probs[at % 2], kv_ref[:, span], preferred_element_type=F32)
            mixed[:, span] = (weighted / totals[at % 2]).astype(BF16)

        def last(head):
            which = at * pair + head
            rows = slice(head * tokens, (head + 1) * tokens)
            out = jnp.dot(mixed[rows, :], w_ref[start + which], preferred_element_type=F32)
            out_ref[:, which * value : (which + 1) * value] = out.astype(BF16)

        parts = [functools.partial(part, low) for low in range(0, latent, WIDE)]
        return parts + [functools.partial(last, head) for head in range(pair)]

    blocks = heads // pair
    for step in range(blocks + 2):
        products = weigh(step - 2) if step > 1 else []
        if step < blocks:
            products = products + score(step)
        interleave(products, soften(step - 1) if 0 < step <= blocks else [])


def attend(start, heads, queries, bias, w_value, kv, scale, after=()):
    tokens, keys = bias.shape
    value = w_value.shape[2]
    return pl.pallas_call(
        functools.partial(attend_kernel, scale * math.log2(math.e), start, heads),
        in_specs=[LOCAL] * 4 + [ANYWHERE] * len(after),
        out_specs=LOCAL,
        out_shape=pltpu.VMEM((tokens, heads * value), BF16),
        scratch_shapes=[
            pltpu.VMEM((2, 2 * tokens, keys), F32),
            pltpu.VMEM((2, 2 * tokens, keys), BF16),
            pltpu.VMEM((2, 2 * tokens, 1), F32),
            pltpu.VMEM((2 * tokens, w_value.shape[1]), BF16),
        ],
        compiler_params=params(12),
        cost_estimate=cost(0, 1024),
        name=f"attend{start}",
    )(held(queries), held(bias), held(w_value), held(kv), *after)


def gather_into(rows_of, parts, side):
    tokens = parts[0][0].shape[-2]
    for at, part in enumerate(parts):
        rows = pl.ds(at * tokens, tokens)
        if len(part) == 1:
            rows_of[rows] = part[0][side]
        elif isinstance(side, int):
            rows_of[rows] = part[side][...]
        else:
            for which in range(2):

                @pl.when(side == which)
                def _(rows=rows, part=part, which=which):
                    rows_of[rows] = part[which][...]


def grouped(refs, sizes):
    refs = iter(refs)
    return [tuple(next(refs) for _ in range(size)) for size in sizes]


def project_kernel(start, sizes, fresh, w_ref, *refs):
    out_ref, gathered = refs[-2:]
    parts = grouped(refs, sizes)
    tokens, depth = parts[0][0].shape[-2:]
    for side in range(2):
        gather_into(gathered.at[side], parts, side)
    weights = w_ref[start : start + depth]
    each = 2 * tokens
    for side in range(2):
        for row in range(0, len(parts) * tokens, each):
            rows = slice(row, row + each)
            product = jnp.dot(gathered[side, rows], weights, preferred_element_type=F32)
            out_ref[side, rows] = product if fresh else refs[sum(sizes)][side, rows] + product


def project(start, parts, w_output, acc, after=()):
    sizes = tuple(map(len, parts))
    blocks = [block for part in parts for block in part]
    tokens, depth = blocks[0].shape[-2:]
    columns = w_output.shape[1]
    operands = [w_output, *blocks] + ([] if acc is None else [acc])
    return pl.pallas_call(
        functools.partial(project_kernel, start, sizes, acc is None),
        in_specs=[LOCAL] * len(operands) + [ANYWHERE] * len(after),
        out_specs=LOCAL,
        out_shape=pltpu.VMEM((2, len(parts) * tokens, columns), F32),
        scratch_shapes=[pltpu.VMEM((2, len(parts) * tokens, depth), BF16)],
        input_output_aliases={} if acc is None else {len(operands) - 1: 0},
        compiler_params=params(12),
        cost_estimate=cost(0, 1024),
        name=f"project{start}",
    )(*map(held, operands), *after)


def finish_kernel(start, keys, far, keep, sizes, w_ref, *refs):
    groups = len(keys)
    acc_ref, out_ref, gathered = refs[-3:]
    parts = grouped(refs, sizes)
    tokens, depth = parts[0][0].shape[-2:]
    me, side = lax.axis_index("ctx"), lax.axis_index("head")
    other = ((me // groups) ^ side ^ (1 - keep)).astype(jnp.int32)
    gather_into(gathered, parts, other)
    product = jnp.dot(
        gathered[...], w_ref[start : start + depth], preferred_element_type=F32
    )
    for at, key in enumerate(keys):
        rows = slice(at * tokens, (at + 1) * tokens)
        place = (me ^ key ^ (far * other)) % groups
        to = pl.ds(pl.multiple_of(place * tokens, tokens), tokens)
        out_ref[to, :] = (acc_ref[other, rows] + product[rows]).astype(out_ref.dtype)


def finish(start, keys, far, keep, parts, w_output, acc, dtype):
    sizes = tuple(map(len, parts))
    blocks = [block for part in parts for block in part]
    tokens, depth = blocks[0].shape[-2:]
    columns = w_output.shape[1]
    rows = len(parts) * tokens
    return pl.pallas_call(
        functools.partial(finish_kernel, start, keys, far, keep, sizes),
        in_specs=[LOCAL] * (2 + len(blocks)),
        out_specs=LOCAL,
        out_shape=pltpu.VMEM((rows, columns), dtype),
        scratch_shapes=[pltpu.VMEM((rows, depth), BF16)],
        compiler_params=params(12),
        cost_estimate=cost(0, 1024),
        name=f"finish{keep}",
    )(*map(held, [w_output, *blocks, acc]))


def overlap(heads, starts, queries, bias, w_value, kv, w_output, scale):
    value = w_value.shape[2]
    got, ready = {}, {}
    last, acc = [], None
    held_back = {entry[:2] for entry in ORDER}

    def send(name, chunk, after=None):
        nonlocal last
        x, mask = ready.pop((name, chunk))
        if after is not None:
            x = gate(x, after)
            last = [x]
        got[name, chunk] = exchange(x, mask, 8)
        along_z, paired = PLAN[chunk][1:]
        if name == FAR and not paired:
            offer(CROSS, chunk, got[FAR, chunk], 1)
        if name == NEAR and not along_z:
            offer(BOTH, chunk, got[NEAR, chunk], 1)
        if name == SIDE and along_z and paired:
            offer(BOTH, chunk, got[SIDE, chunk], 2)

    def offer(name, chunk, x, mask):
        ready[name, chunk] = x, mask
        if (name, chunk) not in held_back:
            send(name, chunk)

    def parts_of(chunk):
        sides = (SIDE,) if PLAN[chunk][2] else (SIDE, CROSS)
        names = (OWN, FAR), sides, (NEAR,), (BOTH,)
        return [tuple(got[name, chunk] for name in part) for part in names]

    for action, chunk, *waits in ORDER:
        after = last + [got[wait] for wait in waits]
        if action == ATTEND:
            out = attend(starts[chunk], heads[chunk], queries, bias, w_value, kv, scale, after)
            last = [out]
            got[OWN, chunk] = out
            offer(FAR, chunk, out, 6)
            if not PLAN[chunk][2]:
                offer(SIDE, chunk, out, 1)
        elif action == STACK:
            base = stack(got[OWN, chunk], got[FAR, chunk], after)
            last = [base]
            offer(NEAR, chunk, base, 2)
            if PLAN[chunk][2]:
                offer(SIDE, chunk, base, 1)
        elif action == PROJECT:
            acc = project(starts[chunk] * value, parts_of(chunk), w_output, acc, after)
            last = [acc]
        elif action == BOTH and PLAN[chunk][1:] == (1, 0):
            pair = stack(got[SIDE, chunk], got[CROSS, chunk], after)
            last = [pair]
            got[BOTH, chunk] = exchange(pair, 2, 8)
        else:
            send(action, chunk, after)
    return parts_of(len(heads) - 1), acc


def local(
    q_nope, q_rope, latent_cache, rope_keys, w_absorb, w_value, w_output, span_offset, valid_lengths
):
    head_count, nope_dim, latent = w_absorb.shape
    tokens = q_nope.shape[0]
    rope_dim = rope_keys.shape[1]
    per_shard = latent_cache.shape[0]
    shards = valid_lengths.shape[0]
    value = w_value.shape[2]
    scale = 1.0 / math.sqrt(nope_dim + rope_dim)

    far, *rest = basis_of(shards)
    keys = [0]
    for mask in rest:
        keys += [key ^ mask for key in keys]
    keys = sorted(keys)
    owners = [key ^ (far * inner) for key in keys for inner in range(2)]
    packed = pack(latent_cache, rope_keys)
    queries, bias = prep(
        q_nope, q_rope, w_absorb, span_offset, valid_lengths, owners, per_shard
    )
    mine = spread(packed, shards, [queries])
    theirs = {key: sibling(pair) for key, pair in mine.items()}
    kv = join([mine[key] for key in keys], [theirs[key] for key in keys], per_shard, latent + LANES)

    heads = [count * head_count // 32 for count, *_ in PLAN]
    starts = [sum(heads[:chunk]) for chunk in range(len(heads))]
    if shards == 8:
        parts, acc = overlap(heads, starts, queries, bias, w_value, kv, w_output, scale)
    else:
        acc = None
        for chunk, start in enumerate(starts):
            out = attend(start, heads[chunk], queries, bias, w_value, kv, scale)
            gathered = spread(out, shards)
            parts = [(gathered[key],) for key in keys]
            if chunk < len(heads) - 1:
                acc = project(start * value, parts, w_output, acc)
    row = starts[-1] * value

    given = finish(row, keys, far, 0, parts, w_output, acc, BF16)
    other = sibling(given)
    kept = finish(row, keys, far, 1, parts, w_output, acc, F32)
    return (kept + other.astype(F32)).astype(BF16)


def solution(mesh):
    return jax.shard_map(
        local,
        mesh=mesh,
        in_specs=(
            P(("groups", "ctx"), "head"),
            P(("groups", "ctx"), "head"),
            P(("groups", "ctx"), None),
            P(("groups", "ctx"), None),
            P("head", None, None),
            P("head", None, None),
            P("head", "ctx"),
            P("groups"),
            P("groups"),
        ),
        out_specs=P(("groups", "head"), "ctx"),
        check_vma=False,
    )
```

```python
import functools
import math

import jax
import jax.numpy as jnp
from jax import lax
from jax.experimental import pallas as pl
from jax.experimental.pallas import tpu as pltpu
from jax.sharding import PartitionSpec as P

F32 = jnp.float32
BF16 = jnp.bfloat16
MASKED = -1e30
LANES = 128
STEP = 4
WIDE = 256
ROWS = 32
PLAN = ((4, 0, 0), (8, 0, 0), (6, 0, 0), (8, 0, 0), (6, 1, 0))
FAR, SIDE, CROSS, NEAR, BOTH = "far", "side", "cross", "near", "both"
ATTEND, STACK, PROJECT, FINISH, OWN = "attend", "stack", "project", "finish", "own"
ORDER = (
    (ATTEND, 0), (ATTEND, 1), (STACK, 0), (ATTEND, 2), (FAR, 2), (STACK, 1, (FAR, 0)),
    (BOTH, 0, (SIDE, 1), (SIDE, 2)), (CROSS, 0), (ATTEND, 3, (CROSS, 0)), (ATTEND, 4),
    (CROSS, 1, (FAR, 1)), (PROJECT, 0, (SIDE, 3)), (FAR, 3, (NEAR, 1)), (STACK, 2),
    (BOTH, 1, (SIDE, 4)), (NEAR, 2), (FAR, 4, (NEAR, 2)), (STACK, 3), (BOTH, 2, (CROSS, 2)),
    (CROSS, 3), (PROJECT, 1, (FAR, 2)), (STACK, 4), (PROJECT, 2), (BOTH, 4, (NEAR, 0)),
    (PROJECT, 3), (FINISH, 4),
)
LOCAL = pl.BlockSpec(memory_space=pltpu.VMEM)
ANYWHERE = pl.BlockSpec(memory_space=pl.ANY)
SCALARS = pl.BlockSpec(memory_space=pltpu.SMEM)


def params(mib):
    return pltpu.CompilerParams(vmem_limit_bytes=mib * 1024 * 1024)


def cost(flops, size, exps=0):
    return pl.CostEstimate(flops=flops, bytes_accessed=size, transcendentals=exps)


def held(x):
    return pltpu.with_memory_space_constraint(x, pltpu.VMEM)


def basis_of(shards):
    if shards == 8:
        return (6, 2, 1)
    return tuple(1 << bit for bit in reversed(range(shards.bit_length() - 1)))


def exchange(x, mask, shards):
    return lax.ppermute(x, "ctx", [(i, i ^ mask) for i in range(shards)])


def sibling(x):
    return lax.ppermute(x, "head", [(0, 1), (1, 0)])


def stack_kernel(first_ref, second_ref, *refs):
    out_ref = refs[-1]
    out_ref[0] = first_ref[...]
    out_ref[1] = second_ref[...]


def stack(first, second, after=()):
    return pl.pallas_call(
        stack_kernel,
        in_specs=[LOCAL, LOCAL] + [ANYWHERE] * len(after),
        out_specs=LOCAL,
        out_shape=pltpu.VMEM((2, *first.shape), first.dtype),
        compiler_params=params(2),
        cost_estimate=cost(0, 1024),
        name="stack",
    )(held(first), held(second), *after)


def spread(x, shards, after=()):
    first, *rest = basis_of(shards)
    pairs = {0: stack(x, exchange(x, first, shards), after)}
    for mask in rest:
        pairs.update({key ^ mask: exchange(pair, mask, shards) for key, pair in pairs.items()})
    return pairs


def gate_kernel(x_ref, *refs):
    refs[-1][...] = x_ref[...]


def gate(x, after):
    return pl.pallas_call(
        gate_kernel,
        in_specs=[LOCAL] + [ANYWHERE] * len(after),
        out_specs=LOCAL,
        out_shape=pltpu.VMEM(x.shape, x.dtype),
        compiler_params=params(2),
        cost_estimate=cost(0, 1024),
        name="gate",
    )(held(x), *after)


def pack_kernel(latent_hbm, rope_hbm, out_ref, latent_ref, rope_ref, sem):
    copies = (
        pltpu.make_async_copy(latent_hbm, latent_ref, sem.at[0]),
        pltpu.make_async_copy(rope_hbm, rope_ref, sem.at[1]),
    )
    for copy in copies:
        copy.start()
    rows, latent = latent_ref.shape
    rope = rope_ref.shape[0]
    tiles = latent // LANES // 2
    pairs, own = packed_rows(rows)
    side = lax.axis_index("head")
    for copy in copies:
        copy.wait()
    turned = rope_ref[...].astype(F32).T.astype(BF16)
    for at in range(2):

        @pl.when(side == at)
        def _(at=at):
            for tile in range(tiles):
                lanes = slice((at * tiles + tile) * LANES, (at * tiles + tile + 1) * LANES)
                out_ref[tile * rows : (tile + 1) * rows, :] = latent_ref[:, lanes]
            first = at * (pairs - own)
            to = slice(tiles * rows, tiles * rows + own)
            out_ref[to, :rope] = turned[first : first + own, :]
            second = first + rows - pairs
            out_ref[to, rope:] = turned[second : second + own, :]


def packed_rows(rows):
    pairs = -(-rows // 32) * 16
    return pairs, -(-pairs // 32) * 16


def pack(latent_cache, rope_keys):
    arrays = (latent_cache, rope_keys.T)
    rows, latent = latent_cache.shape
    _, own = packed_rows(rows)
    return pl.pallas_call(
        pack_kernel,
        in_specs=[ANYWHERE] * 2,
        out_specs=LOCAL,
        out_shape=pltpu.VMEM((latent // LANES // 2 * rows + own, LANES), BF16),
        scratch_shapes=[pltpu.VMEM(x.shape, x.dtype) for x in arrays]
        + [pltpu.SemaphoreType.DMA((2,))],
        compiler_params=params(2),
        cost_estimate=cost(0, 1024),
        name="pack",
    )(*(pltpu.with_memory_space_constraint(x, pltpu.HBM) for x in arrays))


def mask_kernel(owners, span_ref, valid_ref, bias_ref):
    tokens, keys = bias_ref.shape
    per_shard = keys // len(owners)
    me = lax.axis_index("ctx")
    column = lax.broadcasted_iota(jnp.int32, (1, keys), 1)
    place = jnp.full((1, keys), 2**30, jnp.int32)
    for at, owner in enumerate(owners):
        shard = me ^ owner
        row = column - at * per_shard
        here = (row >= 0) & (row < per_shard) & (row < valid_ref[shard])
        place = jnp.where(here, row + shard * per_shard, place)
    position = span_ref[0] + me * tokens + lax.broadcasted_iota(jnp.int32, (tokens, keys), 0)
    bias_ref[...] = jnp.where(place <= position, F32(0.0), F32(MASKED))


def mask(span_offset, valid_lengths, owners, tokens, per_shard):
    return pl.pallas_call(
        functools.partial(mask_kernel, owners),
        in_specs=[SCALARS, SCALARS],
        out_specs=LOCAL,
        out_shape=pltpu.VMEM((tokens, per_shard * len(owners)), F32),
        compiler_params=params(4),
        cost_estimate=cost(0, 1024),
        name="mask",
    )(span_offset, valid_lengths)


def prep_kernel(q_hbm, r_hbm, w_hbm, lat_ref, q_ref, r_ref, w_ref, sem):
    tokens = q_ref.shape[0]
    heads, nope, latent = w_ref.shape
    rope = r_ref.shape[1] // heads
    whole = (
        pltpu.make_async_copy(q_hbm, q_ref, sem.at[0]),
        pltpu.make_async_copy(r_hbm, r_ref, sem.at[1]),
    )
    pieces = [
        pltpu.make_async_copy(
            w_hbm.at[pl.ds(at, STEP)], w_ref.at[pl.ds(at, STEP)], sem.at[2 + at // STEP]
        )
        for at in range(0, heads, STEP)
    ]
    for copy in (*whole, *pieces):
        copy.start()
    for copy in whole:
        copy.wait()
    for head in range(heads):
        if head % STEP == 0:
            pieces[head // STEP].wait()
        rows = slice(head * tokens, (head + 1) * tokens)
        lat = jnp.dot(
            q_ref[:, head * nope : (head + 1) * nope], w_ref[head], preferred_element_type=F32
        )
        lat_ref[rows, :latent] = lat.astype(BF16)
        turned = r_ref[:, head * rope : (head + 1) * rope]
        lat_ref[rows, latent : latent + rope] = turned
        lat_ref[rows, latent + rope :] = turned


def prep(q_nope, q_rope, w_absorb):
    heads, _, latent = w_absorb.shape
    tokens = q_nope.shape[0]
    arrays = (q_nope, q_rope, w_absorb)
    return pl.pallas_call(
        prep_kernel,
        in_specs=[ANYWHERE] * 3,
        out_specs=LOCAL,
        out_shape=pltpu.VMEM((heads * tokens, latent + LANES), BF16),
        scratch_shapes=[pltpu.VMEM(x.shape, x.dtype) for x in arrays]
        + [pltpu.SemaphoreType.DMA((2 + heads // STEP,))],
        compiler_params=params(10),
        cost_estimate=cost(0, 1024),
        name="prep",
    )(*(pltpu.with_memory_space_constraint(x, pltpu.HBM) for x in arrays))


def join_kernel(groups, *refs):
    mine = refs[:groups]
    theirs = refs[groups : 2 * groups]
    out_ref = refs[-1]
    rows = out_ref.shape[0] // (2 * groups)
    latent = out_ref.shape[1] - LANES
    tiles = latent // LANES // 2
    pairs, own = packed_rows(rows)
    side = lax.axis_index("head")
    half = lax.broadcasted_iota(jnp.int32, (pairs, LANES), 1) < LANES // 2
    nothing = jnp.zeros((pairs, LANES), BF16)
    for which in range(2):

        @pl.when(side == which)
        def _(which=which):
            for at in range(2 * groups):
                start = at * rows
                sides = [mine[at // 2], theirs[at // 2]][:: 1 - 2 * which]
                for tile in range(2 * tiles):
                    block = sides[tile // tiles][at % 2, tile % tiles * rows : (tile % tiles + 1) * rows]
                    out_ref[start : start + rows, tile * LANES : (tile + 1) * LANES] = block
                low = sides[0][at % 2, tiles * rows : tiles * rows + own]
                high = sides[1][at % 2, tiles * rows + 2 * own - pairs : tiles * rows + own]
                both = jnp.concatenate([low, high], axis=0)
                out_ref[start : start + pairs, latent:] = jnp.where(half, both, nothing)
                rest = jnp.where(half, nothing, both)[2 * pairs - rows :]
                out_ref[start + pairs : start + rows, latent:] = rest


def join(mine, theirs, per_shard, depth):
    groups = len(mine)
    return pl.pallas_call(
        functools.partial(join_kernel, groups),
        in_specs=[LOCAL] * (2 * groups),
        out_specs=LOCAL,
        out_shape=pltpu.VMEM((2 * groups * per_shard, depth), BF16),
        compiler_params=params(4),
        cost_estimate=cost(0, 1024),
        name="join",
    )(*map(held, mine), *map(held, theirs))


def interleave(first, second):
    steps = [((at + 0.5) / len(x), which, step) for which, x in enumerate((first, second)) for at, step in enumerate(x)]
    for *_, step in sorted(steps, key=lambda entry: entry[:2]):
        step()


def attend_kernel(scale, start, heads, q_ref, bias_ref, w_ref, kv_ref, *refs):
    out_ref, scores, probs, totals, mixed = refs[-5:]
    tokens, keys = bias_ref.shape
    _, latent, value = w_ref.shape
    block = scores.shape[1]
    pair = block // tokens

    def score(at):
        row = start * tokens + at * block

        def part(low):
            span = slice(low, min(low + WIDE, keys))
            scores[at % 2, :, span] = lax.dot_general(
                q_ref[row : row + block, :],
                kv_ref[span, :],
                (((1,), (1,)), ((), ())),
                preferred_element_type=F32,
            )

        return [functools.partial(part, low) for low in range(0, keys, WIDE)]

    def soften(at):
        def part(low):
            rows = slice(low, low + ROWS)
            masked = scores[at % 2, rows, :] + bias_ref[low % tokens : low % tokens + ROWS, :]
            top = jnp.max(masked, axis=-1, keepdims=True)
            expo = jnp.exp2((masked - top) * F32(scale))
            totals[at % 2, rows, :] = jnp.sum(expo, axis=-1, keepdims=True)
            probs[at % 2, rows, :] = expo.astype(BF16)

        return [functools.partial(part, low) for low in range(0, block, ROWS)]

    def weigh(at):
        def part(low):
            span = slice(low, low + WIDE)
            weighted = jnp.dot(probs[at % 2], kv_ref[:, span], preferred_element_type=F32)
            mixed[:, span] = (weighted / totals[at % 2]).astype(BF16)

        def last(head):
            which = at * pair + head
            rows = slice(head * tokens, (head + 1) * tokens)
            out = jnp.dot(mixed[rows, :], w_ref[start + which], preferred_element_type=F32)
            out_ref[:, which * value : (which + 1) * value] = out.astype(BF16)

        parts = [functools.partial(part, low) for low in range(0, latent, WIDE)]
        return parts + [functools.partial(last, head) for head in range(pair)]

    blocks = heads // pair
    for step in range(blocks + 2):
        products = weigh(step - 2) if step > 1 else []
        if step < blocks:
            products = products + score(step)
        interleave(products, soften(step - 1) if 0 < step <= blocks else [])


def attend(start, heads, queries, bias, w_value, kv, scale, after=()):
    tokens, keys = bias.shape
    value = w_value.shape[2]
    block = next(count for count in (4, 3, 2, 1) if heads % count == 0) * tokens
    return pl.pallas_call(
        functools.partial(attend_kernel, scale * math.log2(math.e), start, heads),
        in_specs=[LOCAL] * 4 + [ANYWHERE] * len(after),
        out_specs=LOCAL,
        out_shape=pltpu.VMEM((tokens, heads * value), BF16),
        scratch_shapes=[
            pltpu.VMEM((2, block, keys), F32),
            pltpu.VMEM((2, block, keys), BF16),
            pltpu.VMEM((2, block, 1), F32),
            pltpu.VMEM((block, w_value.shape[1]), BF16),
        ],
        compiler_params=params(20),
        cost_estimate=cost(0, 1024),
        name=f"attend{start}",
    )(held(queries), held(bias), held(w_value), held(kv), *after)


def gather_into(rows_of, parts, side):
    tokens = parts[0][0].shape[-2]
    for at, part in enumerate(parts):
        rows = pl.ds(at * tokens, tokens)
        if len(part) == 1:
            rows_of[rows] = part[0][side]
        elif isinstance(side, int):
            rows_of[rows] = part[side][...]
        else:
            for which in range(2):

                @pl.when(side == which)
                def _(rows=rows, part=part, which=which):
                    rows_of[rows] = part[which][...]


def grouped(refs, sizes):
    refs = iter(refs)
    return [tuple(next(refs) for _ in range(size)) for size in sizes]


def project_kernel(start, sizes, first, fresh, w_ref, *refs):
    out_ref, gathered = refs[-2:]
    parts = grouped(refs, sizes)
    tokens, depth = parts[0][0].shape[-2:]
    for side in range(2):
        gather_into(gathered.at[side], parts, side)
    weights = w_ref[start : start + depth]
    each = min(2, len(parts)) * tokens
    for side in range(2):
        for row in range(0, len(parts) * tokens, each):
            rows = slice(row, min(row + each, len(parts) * tokens))
            to = slice(first * tokens + rows.start, first * tokens + rows.stop)
            product = jnp.dot(gathered[side, rows], weights, preferred_element_type=F32)
            out_ref[side, to] = product if fresh else refs[sum(sizes)][side, to] + product


def project(start, parts, w_output, acc, after=(), first=0):
    sizes = tuple(map(len, parts))
    blocks = [block for part in parts for block in part]
    tokens, depth = blocks[0].shape[-2:]
    columns = w_output.shape[1]
    operands = [w_output, *blocks] + ([] if acc is None else [acc])
    shape = (2, len(parts) * tokens, columns) if acc is None else acc.shape
    return pl.pallas_call(
        functools.partial(project_kernel, start, sizes, first, acc is None),
        in_specs=[LOCAL] * len(operands) + [ANYWHERE] * len(after),
        out_specs=LOCAL,
        out_shape=pltpu.VMEM(shape, F32),
        scratch_shapes=[pltpu.VMEM((2, len(parts) * tokens, depth), BF16)],
        input_output_aliases={} if acc is None else {len(operands) - 1: 0},
        compiler_params=params(12),
        cost_estimate=cost(0, 1024),
        name=f"project{start}",
    )(*map(held, operands), *after)


def other_half(groups, keep):
    me, side = lax.axis_index("ctx"), lax.axis_index("head")
    return ((me // groups) ^ side ^ (1 - keep)).astype(jnp.int32)


def finish_kernel(start, sizes, first, w_ref, *refs):
    given_ref, kept_ref, gathered = refs[-3:]
    acc_ref = refs[sum(sizes)]
    parts = grouped(refs, sizes)
    tokens, depth = parts[0][0].shape[-2:]
    rows = slice(first * tokens, (first + len(parts)) * tokens)
    for keep, out_ref in enumerate((given_ref, kept_ref)):
        other = other_half(acc_ref.shape[1] // tokens, keep)
        gather_into(gathered.at[keep], parts, other)
        product = jnp.dot(
            gathered[keep], w_ref[start : start + depth], preferred_element_type=F32
        )
        out_ref[...] = (acc_ref[other, rows] + product).astype(out_ref.dtype)


def finish(start, parts, w_output, acc, after=(), first=0):
    sizes = tuple(map(len, parts))
    blocks = [block for part in parts for block in part]
    tokens, depth = blocks[0].shape[-2:]
    columns = w_output.shape[1]
    rows = len(parts) * tokens
    return pl.pallas_call(
        functools.partial(finish_kernel, start, sizes, first),
        in_specs=[LOCAL] * (2 + len(blocks)) + [ANYWHERE] * len(after),
        out_specs=[LOCAL] * 2,
        out_shape=[pltpu.VMEM((rows, columns), BF16), pltpu.VMEM((rows, columns), F32)],
        scratch_shapes=[pltpu.VMEM((2, rows, depth), BF16)],
        compiler_params=params(12),
        cost_estimate=cost(0, 1024),
        name="finish",
    )(*map(held, [w_output, *blocks, acc]), *after)


def total_kernel(keys, far, groups, mine_ref, other_ref, *refs):
    out_ref, rounded, sem = refs[-3:]
    tokens = mine_ref.shape[0] // len(keys)
    me = lax.axis_index("ctx")
    other = other_half(groups, 1)
    copies = []
    for at, key in enumerate(keys):
        rows = pl.ds(at * tokens, tokens)
        place = (me ^ key ^ (far * other)) % groups
        to = pl.ds(pl.multiple_of(place * tokens, tokens), tokens)
        rounded[rows] = (mine_ref[rows] + other_ref[rows].astype(F32)).astype(BF16)
        copies.append(pltpu.make_async_copy(rounded.at[rows], out_ref.at[to], sem.at[at]))
        copies[-1].start()
    for copy in copies:
        copy.wait()


def total(keys, far, groups, mine, other, out, after):
    rows, columns = mine.shape
    tokens = rows // len(keys)
    given = [] if out is None else [out]
    return pl.pallas_call(
        functools.partial(total_kernel, keys, far, groups),
        in_specs=[LOCAL] * 2 + [ANYWHERE] * (len(given) + len(after)),
        out_specs=ANYWHERE,
        out_shape=jax.ShapeDtypeStruct((groups * tokens, columns), BF16),
        scratch_shapes=[pltpu.VMEM((rows, columns), BF16), pltpu.SemaphoreType.DMA((len(keys),))],
        input_output_aliases={2: 0} if given else {},
        compiler_params=params(4),
        cost_estimate=cost(0, 1024),
        name="total",
    )(held(mine), held(other), *given, *after)


def overlap(heads, starts, queries, bias, w_value, kv, w_output, scale):
    value = w_value.shape[2]
    got, ready = {}, {}
    last, acc = [], None
    held_back = {entry[:2] for entry in ORDER}

    def send(name, chunk, after=None):
        nonlocal last
        x, mask = ready.pop((name, chunk))
        if after is not None:
            x = gate(x, after)
            last = [x]
        got[name, chunk] = exchange(x, mask, 8)
        along_z, paired = PLAN[chunk][1:]
        if name == FAR and not paired:
            offer(CROSS, chunk, got[FAR, chunk], 1)
        if name == NEAR and not along_z:
            offer(BOTH, chunk, got[NEAR, chunk], 1)
        if name == SIDE and along_z and paired:
            offer(BOTH, chunk, got[SIDE, chunk], 2)

    def offer(name, chunk, x, mask):
        ready[name, chunk] = x, mask
        if (name, chunk) not in held_back:
            send(name, chunk)

    def parts_of(chunk):
        sides = (SIDE,) if PLAN[chunk][2] else (SIDE, CROSS)
        names = (OWN, FAR), sides, (NEAR,), (BOTH,)
        return [tuple(got[name, chunk] for name in part) for part in names]

    for action, chunk, *waits in ORDER:
        after = last + [got[wait] for wait in waits]
        if action == ATTEND:
            out = attend(starts[chunk], heads[chunk], queries, bias, w_value, kv, scale, after)
            last = [out]
            got[OWN, chunk] = out
            offer(FAR, chunk, out, 6)
            if not PLAN[chunk][2]:
                offer(SIDE, chunk, out, 1)
        elif action == STACK:
            base = stack(got[OWN, chunk], got[FAR, chunk], after)
            last = [base]
            offer(NEAR, chunk, base, 2)
            if PLAN[chunk][2]:
                offer(SIDE, chunk, base, 1)
        elif action == PROJECT:
            some = parts_of(chunk)[: 3 if chunk == len(heads) - 2 else 4]
            acc = project(starts[chunk] * value, some, w_output, acc, after)
            last = [acc]
        elif action == FINISH:
            sums = [finish(starts[chunk] * value, parts_of(chunk)[:3], w_output, acc, after)]
            last = [sums[0][1]]
        elif action == BOTH and PLAN[chunk][1:] == (1, 0):
            pair = stack(got[SIDE, chunk], got[CROSS, chunk], after)
            last = [pair]
            got[BOTH, chunk] = exchange(pair, 2, 8)
        else:
            send(action, chunk, after)
    before, row = (start * value for start in starts[-2:])
    rests = [parts_of(chunk)[3:] for chunk in range(len(heads))][-2:]
    acc = project(before, rests[0], w_output, acc, last, 3)
    return [*sums, finish(row, rests[1], w_output, acc, [acc], 3)]


def local(
    q_nope, q_rope, latent_cache, rope_keys, w_absorb, w_value, w_output, span_offset, valid_lengths
):
    head_count, nope_dim, latent = w_absorb.shape
    tokens = q_nope.shape[0]
    rope_dim = rope_keys.shape[1]
    per_shard = latent_cache.shape[0]
    shards = valid_lengths.shape[0]
    value = w_value.shape[2]
    scale = 1.0 / math.sqrt(nope_dim + rope_dim)

    far, *rest = basis_of(shards)
    keys = [0]
    for bit in rest:
        keys += [key ^ bit for key in keys]
    keys = sorted(keys)
    owners = [key ^ (far * inner) for key in keys for inner in range(2)]
    packed = pack(latent_cache, rope_keys)
    queries = prep(q_nope, q_rope, w_absorb)
    bias = mask(span_offset, valid_lengths, owners, tokens, per_shard)
    mine = spread(packed, shards, [queries])
    theirs = {key: sibling(pair) for key, pair in mine.items()}
    kv = join([mine[key] for key in keys], [theirs[key] for key in keys], per_shard, latent + LANES)

    heads = [count * head_count // 32 for count, *_ in PLAN]
    starts = [sum(heads[:chunk]) for chunk in range(len(heads))]
    if shards == 8:
        sums = overlap(heads, starts, queries, bias, w_value, kv, w_output, scale)
        split = (keys[:3], keys[3:])
    else:
        acc = None
        for chunk, start in enumerate(starts):
            out = attend(start, heads[chunk], queries, bias, w_value, kv, scale)
            gathered = spread(out, shards)
            parts = [(gathered[key],) for key in keys]
            if chunk < len(heads) - 1:
                acc = project(start * value, parts, w_output, acc)
        sums = [finish(starts[-1] * value, parts, w_output, acc)]
        split = (keys,)

    out, after = None, [sums[-1][1]]
    others = [sibling(given) for given, _ in sums]
    for some, (_, kept), other in zip(split, sums, others):
        out = total(some, far, len(keys), kept, other, out, after)
        after = []
    return out


def solution(mesh):
    return jax.shard_map(
        local,
        mesh=mesh,
        in_specs=(
            P(("groups", "ctx"), "head"),
            P(("groups", "ctx"), "head"),
            P(("groups", "ctx"), None),
            P(("groups", "ctx"), None),
            P("head", None, None),
            P("head", None, None),
            P("head", "ctx"),
            P("groups"),
            P("groups"),
        ),
        out_specs=P(("groups", "head"), "ctx"),
        check_vma=False,
    )
```

```python
import functools
import math

import jax
import jax.numpy as jnp
from jax import lax
from jax.experimental import pallas as pl
from jax.experimental.pallas import tpu as pltpu
from jax.sharding import PartitionSpec as P

F32 = jnp.float32
BF16 = jnp.bfloat16
MASKED = -1e30
LANES = 128
STEP = 4
WIDE = 256
ROWS = 32
PLAN = ((4, 0, 0), (8, 0, 0), (6, 0, 0), (8, 0, 0), (6, 1, 0))
FAR, SIDE, CROSS, NEAR, BOTH = "far", "side", "cross", "near", "both"
ATTEND, STACK, PROJECT, FINISH, OWN = "attend", "stack", "project", "finish", "own"
ORDER = (
    (ATTEND, 0), (ATTEND, 1), (CROSS, 0), (STACK, 0), (ATTEND, 2), (STACK, 1, (FAR, 0)), (FAR, 2),
    (BOTH, 0, (SIDE, 1), (SIDE, 2)), (ATTEND, 3, (CROSS, 0)), (ATTEND, 4),
    (CROSS, 1, (BOTH, 0), (FAR, 1)), (PROJECT, 0, (SIDE, 3)), (STACK, 2), (FAR, 3, (NEAR, 1)),
    (CROSS, 2, (CROSS, 1)), (BOTH, 1, (SIDE, 4)), (FAR, 4, (NEAR, 2)), (BOTH, 2, (CROSS, 2)),
    (STACK, 3), (CROSS, 3, (BOTH, 1)), (PROJECT, 1, (NEAR, 1)), (CROSS, 4), (STACK, 4),
    (PROJECT, 2, (CROSS, 3)), (BOTH, 4), (PROJECT, 3, (NEAR, 4)),
)
LOCAL = pl.BlockSpec(memory_space=pltpu.VMEM)
ANYWHERE = pl.BlockSpec(memory_space=pl.ANY)
SCALARS = pl.BlockSpec(memory_space=pltpu.SMEM)


def params(mib):
    return pltpu.CompilerParams(vmem_limit_bytes=mib * 1024 * 1024)


def cost(flops, size, exps=0):
    return pl.CostEstimate(flops=flops, bytes_accessed=size, transcendentals=exps)


def held(x):
    return pltpu.with_memory_space_constraint(x, pltpu.VMEM)


def basis_of(shards):
    if shards == 8:
        return (6, 2, 1)
    return tuple(1 << bit for bit in reversed(range(shards.bit_length() - 1)))


def exchange(x, mask, shards):
    return lax.ppermute(x, "ctx", [(i, i ^ mask) for i in range(shards)])


def sibling(x):
    return lax.ppermute(x, "head", [(0, 1), (1, 0)])


def stack_kernel(first_ref, second_ref, *refs):
    out_ref = refs[-1]
    out_ref[0] = first_ref[...]
    out_ref[1] = second_ref[...]


def stack(first, second, after=()):
    return pl.pallas_call(
        stack_kernel,
        in_specs=[LOCAL, LOCAL] + [ANYWHERE] * len(after),
        out_specs=LOCAL,
        out_shape=pltpu.VMEM((2, *first.shape), first.dtype),
        compiler_params=params(2),
        cost_estimate=cost(0, 1024),
        name="stack",
    )(held(first), held(second), *after)


def spread(x, shards, after=()):
    first, *rest = basis_of(shards)
    pairs = {0: stack(x, exchange(x, first, shards), after)}
    for mask in rest:
        pairs.update({key ^ mask: exchange(pair, mask, shards) for key, pair in pairs.items()})
    return pairs


def gate_kernel(x_ref, *refs):
    refs[-1][...] = x_ref[...]


def gate(x, after):
    return pl.pallas_call(
        gate_kernel,
        in_specs=[LOCAL] + [ANYWHERE] * len(after),
        out_specs=LOCAL,
        out_shape=pltpu.VMEM(x.shape, x.dtype),
        compiler_params=params(2),
        cost_estimate=cost(0, 1024),
        name="gate",
    )(held(x), *after)


def pack_kernel(latent_hbm, rope_hbm, out_ref, latent_ref, rope_ref, sem):
    copies = (
        pltpu.make_async_copy(latent_hbm, latent_ref, sem.at[0]),
        pltpu.make_async_copy(rope_hbm, rope_ref, sem.at[1]),
    )
    for copy in copies:
        copy.start()
    rows, latent = latent_ref.shape
    rope = rope_ref.shape[0]
    tiles = latent // LANES // 2
    pairs, own = packed_rows(rows)
    side = lax.axis_index("head")
    for copy in copies:
        copy.wait()
    turned = rope_ref[...].astype(F32).T.astype(BF16)
    for at in range(2):

        @pl.when(side == at)
        def _(at=at):
            for tile in range(tiles):
                lanes = slice((at * tiles + tile) * LANES, (at * tiles + tile + 1) * LANES)
                out_ref[tile * rows : (tile + 1) * rows, :] = latent_ref[:, lanes]
            first = at * (pairs - own)
            to = slice(tiles * rows, tiles * rows + own)
            out_ref[to, :rope] = turned[first : first + own, :]
            second = first + rows - pairs
            out_ref[to, rope:] = turned[second : second + own, :]


def packed_rows(rows):
    pairs = -(-rows // 32) * 16
    return pairs, -(-pairs // 32) * 16


def pack(latent_cache, rope_keys):
    arrays = (latent_cache, rope_keys.T)
    rows, latent = latent_cache.shape
    _, own = packed_rows(rows)
    return pl.pallas_call(
        pack_kernel,
        in_specs=[ANYWHERE] * 2,
        out_specs=LOCAL,
        out_shape=pltpu.VMEM((latent // LANES // 2 * rows + own, LANES), BF16),
        scratch_shapes=[pltpu.VMEM(x.shape, x.dtype) for x in arrays]
        + [pltpu.SemaphoreType.DMA((2,))],
        compiler_params=params(2),
        cost_estimate=cost(0, 1024),
        name="pack",
    )(*(pltpu.with_memory_space_constraint(x, pltpu.HBM) for x in arrays))


def mask_kernel(owners, span_ref, valid_ref, bias_ref):
    tokens, keys = bias_ref.shape
    per_shard = keys // len(owners)
    me = lax.axis_index("ctx")
    column = lax.broadcasted_iota(jnp.int32, (1, keys), 1)
    place = jnp.full((1, keys), 2**30, jnp.int32)
    for at, owner in enumerate(owners):
        shard = me ^ owner
        row = column - at * per_shard
        here = (row >= 0) & (row < per_shard) & (row < valid_ref[shard])
        place = jnp.where(here, row + shard * per_shard, place)
    position = span_ref[0] + me * tokens + lax.broadcasted_iota(jnp.int32, (tokens, keys), 0)
    bias_ref[...] = jnp.where(place <= position, F32(0.0), F32(MASKED))


def mask(span_offset, valid_lengths, owners, tokens, per_shard):
    return pl.pallas_call(
        functools.partial(mask_kernel, owners),
        in_specs=[SCALARS, SCALARS],
        out_specs=LOCAL,
        out_shape=pltpu.VMEM((tokens, per_shard * len(owners)), F32),
        compiler_params=params(4),
        cost_estimate=cost(0, 1024),
        name="mask",
    )(span_offset, valid_lengths)


def prep_kernel(q_hbm, r_hbm, w_hbm, lat_ref, q_ref, r_ref, w_ref, sem):
    tokens = q_ref.shape[0]
    heads, nope, latent = w_ref.shape
    rope = r_ref.shape[1] // heads
    whole = (
        pltpu.make_async_copy(q_hbm, q_ref, sem.at[0]),
        pltpu.make_async_copy(r_hbm, r_ref, sem.at[1]),
    )
    pieces = [
        pltpu.make_async_copy(
            w_hbm.at[pl.ds(at, STEP)], w_ref.at[pl.ds(at, STEP)], sem.at[2 + at // STEP]
        )
        for at in range(0, heads, STEP)
    ]
    for copy in (*whole, *pieces):
        copy.start()
    for copy in whole:
        copy.wait()
    for head in range(heads):
        if head % STEP == 0:
            pieces[head // STEP].wait()
        rows = slice(head * tokens, (head + 1) * tokens)
        lat = jnp.dot(
            q_ref[:, head * nope : (head + 1) * nope], w_ref[head], preferred_element_type=F32
        )
        lat_ref[rows, :latent] = lat.astype(BF16)
        turned = r_ref[:, head * rope : (head + 1) * rope]
        lat_ref[rows, latent : latent + rope] = turned
        lat_ref[rows, latent + rope :] = turned


def prep(q_nope, q_rope, w_absorb):
    heads, _, latent = w_absorb.shape
    tokens = q_nope.shape[0]
    arrays = (q_nope, q_rope, w_absorb)
    return pl.pallas_call(
        prep_kernel,
        in_specs=[ANYWHERE] * 3,
        out_specs=LOCAL,
        out_shape=pltpu.VMEM((heads * tokens, latent + LANES), BF16),
        scratch_shapes=[pltpu.VMEM(x.shape, x.dtype) for x in arrays]
        + [pltpu.SemaphoreType.DMA((2 + heads // STEP,))],
        compiler_params=params(10),
        cost_estimate=cost(0, 1024),
        name="prep",
    )(*(pltpu.with_memory_space_constraint(x, pltpu.HBM) for x in arrays))


def join_kernel(groups, *refs):
    mine = refs[:groups]
    theirs = refs[groups : 2 * groups]
    out_ref = refs[-1]
    rows = out_ref.shape[0] // (2 * groups)
    latent = out_ref.shape[1] - LANES
    tiles = latent // LANES // 2
    pairs, own = packed_rows(rows)
    side = lax.axis_index("head")
    half = lax.broadcasted_iota(jnp.int32, (pairs, LANES), 1) < LANES // 2
    nothing = jnp.zeros((pairs, LANES), BF16)
    for which in range(2):

        @pl.when(side == which)
        def _(which=which):
            for at in range(2 * groups):
                start = at * rows
                sides = [mine[at // 2], theirs[at // 2]][:: 1 - 2 * which]
                for tile in range(2 * tiles):
                    block = sides[tile // tiles][at % 2, tile % tiles * rows : (tile % tiles + 1) * rows]
                    out_ref[start : start + rows, tile * LANES : (tile + 1) * LANES] = block
                low = sides[0][at % 2, tiles * rows : tiles * rows + own]
                high = sides[1][at % 2, tiles * rows + 2 * own - pairs : tiles * rows + own]
                both = jnp.concatenate([low, high], axis=0)
                out_ref[start : start + pairs, latent:] = jnp.where(half, both, nothing)
                rest = jnp.where(half, nothing, both)[2 * pairs - rows :]
                out_ref[start + pairs : start + rows, latent:] = rest


def join(mine, theirs, per_shard, depth):
    groups = len(mine)
    return pl.pallas_call(
        functools.partial(join_kernel, groups),
        in_specs=[LOCAL] * (2 * groups),
        out_specs=LOCAL,
        out_shape=pltpu.VMEM((2 * groups * per_shard, depth), BF16),
        compiler_params=params(4),
        cost_estimate=cost(0, 1024),
        name="join",
    )(*map(held, mine), *map(held, theirs))


def interleave(first, second):
    steps = [((at + 0.5) / len(x), which, step) for which, x in enumerate((first, second)) for at, step in enumerate(x)]
    for *_, step in sorted(steps, key=lambda entry: entry[:2]):
        step()


def attend_kernel(scale, start, heads, q_ref, bias_ref, w_ref, kv_ref, *refs):
    out_ref, scores, probs, totals, mixed = refs[-5:]
    tokens, keys = bias_ref.shape
    _, latent, value = w_ref.shape
    block = scores.shape[1]
    pair = block // tokens

    def score(at):
        row = start * tokens + at * block

        def part(low):
            span = slice(low, min(low + WIDE, keys))
            scores[at % 2, :, span] = lax.dot_general(
                q_ref[row : row + block, :],
                kv_ref[span, :],
                (((1,), (1,)), ((), ())),
                preferred_element_type=F32,
            )

        return [functools.partial(part, low) for low in range(0, keys, WIDE)]

    def soften(at):
        def part(low):
            rows = slice(low, low + ROWS)
            masked = scores[at % 2, rows, :] + bias_ref[low % tokens : low % tokens + ROWS, :]
            top = jnp.max(masked, axis=-1, keepdims=True)
            expo = jnp.exp2((masked - top) * F32(scale))
            totals[at % 2, rows, :] = jnp.sum(expo, axis=-1, keepdims=True)
            probs[at % 2, rows, :] = expo.astype(BF16)

        return [functools.partial(part, low) for low in range(0, block, ROWS)]

    def weigh(at):
        def part(low):
            span = slice(low, low + WIDE)
            weighted = jnp.dot(probs[at % 2], kv_ref[:, span], preferred_element_type=F32)
            mixed[:, span] = (weighted / totals[at % 2]).astype(BF16)

        def last(head):
            which = at * pair + head
            rows = slice(head * tokens, (head + 1) * tokens)
            out = jnp.dot(mixed[rows, :], w_ref[start + which], preferred_element_type=F32)
            out_ref[:, which * value : (which + 1) * value] = out.astype(BF16)

        parts = [functools.partial(part, low) for low in range(0, latent, WIDE)]
        return parts + [functools.partial(last, head) for head in range(pair)]

    blocks = heads // pair
    for step in range(blocks + 2):
        products = weigh(step - 2) if step > 1 else []
        if step < blocks:
            products = products + score(step)
        interleave(products, soften(step - 1) if 0 < step <= blocks else [])


def attend(start, heads, queries, bias, w_value, kv, scale, after=()):
    tokens, keys = bias.shape
    value = w_value.shape[2]
    block = next(count for count in (4, 3, 2, 1) if heads % count == 0) * tokens
    return pl.pallas_call(
        functools.partial(attend_kernel, scale * math.log2(math.e), start, heads),
        in_specs=[LOCAL] * 4 + [ANYWHERE] * len(after),
        out_specs=LOCAL,
        out_shape=pltpu.VMEM((tokens, heads * value), BF16),
        scratch_shapes=[
            pltpu.VMEM((2, block, keys), F32),
            pltpu.VMEM((2, block, keys), BF16),
            pltpu.VMEM((2, block, 1), F32),
            pltpu.VMEM((block, w_value.shape[1]), BF16),
        ],
        compiler_params=params(20),
        cost_estimate=cost(0, 1024),
        name=f"attend{start}",
    )(held(queries), held(bias), held(w_value), held(kv), *after)


def gather_into(rows_of, parts, side):
    tokens = parts[0][0].shape[-2]
    for at, part in enumerate(parts):
        rows = pl.ds(at * tokens, tokens)
        if len(part) == 1:
            rows_of[rows] = part[0][side]
        elif isinstance(side, int):
            rows_of[rows] = part[side][...]
        else:
            for which in range(2):

                @pl.when(side == which)
                def _(rows=rows, part=part, which=which):
                    rows_of[rows] = part[which][...]


def grouped(refs, sizes):
    refs = iter(refs)
    return [tuple(next(refs) for _ in range(size)) for size in sizes]


def project_kernel(start, sizes, first, fresh, w_ref, *refs):
    out_ref, gathered = refs[-2:]
    parts = grouped(refs, sizes)
    tokens, depth = parts[0][0].shape[-2:]
    for side in range(2):
        gather_into(gathered.at[side], parts, side)
    weights = w_ref[start : start + depth]
    each = min(2, len(parts)) * tokens
    for side in range(2):
        for row in range(0, len(parts) * tokens, each):
            rows = slice(row, min(row + each, len(parts) * tokens))
            to = slice(first * tokens + rows.start, first * tokens + rows.stop)
            product = jnp.dot(gathered[side, rows], weights, preferred_element_type=F32)
            out_ref[side, to] = product if fresh else refs[sum(sizes)][side, to] + product


def project(start, parts, w_output, acc, after=(), first=0):
    sizes = tuple(map(len, parts))
    blocks = [block for part in parts for block in part]
    tokens, depth = blocks[0].shape[-2:]
    columns = w_output.shape[1]
    operands = [w_output, *blocks] + ([] if acc is None else [acc])
    shape = (2, len(parts) * tokens, columns) if acc is None else acc.shape
    return pl.pallas_call(
        functools.partial(project_kernel, start, sizes, first, acc is None),
        in_specs=[LOCAL] * len(operands) + [ANYWHERE] * len(after),
        out_specs=LOCAL,
        out_shape=pltpu.VMEM(shape, F32),
        scratch_shapes=[pltpu.VMEM((2, len(parts) * tokens, depth), BF16)],
        input_output_aliases={} if acc is None else {len(operands) - 1: 0},
        compiler_params=params(12),
        cost_estimate=cost(0, 1024),
        name=f"project{start}",
    )(*map(held, operands), *after)


def other_half(groups, keep):
    me, side = lax.axis_index("ctx"), lax.axis_index("head")
    return ((me // groups) ^ side ^ (1 - keep)).astype(jnp.int32)


def finish_kernel(start, sizes, first, w_ref, *refs):
    given_ref, kept_ref, gathered = refs[-3:]
    acc_ref = refs[sum(sizes)]
    parts = grouped(refs, sizes)
    tokens, depth = parts[0][0].shape[-2:]
    rows = slice(first * tokens, (first + len(parts)) * tokens)
    for keep, out_ref in enumerate((given_ref, kept_ref)):
        other = other_half(acc_ref.shape[1] // tokens, keep)
        gather_into(gathered.at[keep], parts, other)
        product = jnp.dot(
            gathered[keep], w_ref[start : start + depth], preferred_element_type=F32
        )
        out_ref[...] = (acc_ref[other, rows] + product).astype(out_ref.dtype)


def finish(start, parts, w_output, acc, after=(), first=0):
    sizes = tuple(map(len, parts))
    blocks = [block for part in parts for block in part]
    tokens, depth = blocks[0].shape[-2:]
    columns = w_output.shape[1]
    rows = len(parts) * tokens
    return pl.pallas_call(
        functools.partial(finish_kernel, start, sizes, first),
        in_specs=[LOCAL] * (2 + len(blocks)) + [ANYWHERE] * len(after),
        out_specs=[LOCAL] * 2,
        out_shape=[pltpu.VMEM((rows, columns), BF16), pltpu.VMEM((rows, columns), F32)],
        scratch_shapes=[pltpu.VMEM((2, rows, depth), BF16)],
        compiler_params=params(12),
        cost_estimate=cost(0, 1024),
        name="finish",
    )(*map(held, [w_output, *blocks, acc]), *after)


def total_kernel(keys, far, groups, mine_ref, other_ref, *refs):
    out_ref, rounded, sem = refs[-3:]
    tokens = mine_ref.shape[0] // len(keys)
    me = lax.axis_index("ctx")
    other = other_half(groups, 1)
    copies = []
    for at, key in enumerate(keys):
        rows = pl.ds(at * tokens, tokens)
        place = (me ^ key ^ (far * other)) % groups
        to = pl.ds(pl.multiple_of(place * tokens, tokens), tokens)
        rounded[rows] = (mine_ref[rows] + other_ref[rows].astype(F32)).astype(BF16)
        copies.append(pltpu.make_async_copy(rounded.at[rows], out_ref.at[to], sem.at[at]))
        copies[-1].start()
    for copy in copies:
        copy.wait()


def total(keys, far, groups, mine, other, out, after):
    rows, columns = mine.shape
    tokens = rows // len(keys)
    given = [] if out is None else [out]
    return pl.pallas_call(
        functools.partial(total_kernel, keys, far, groups),
        in_specs=[LOCAL] * 2 + [ANYWHERE] * (len(given) + len(after)),
        out_specs=ANYWHERE,
        out_shape=jax.ShapeDtypeStruct((groups * tokens, columns), BF16),
        scratch_shapes=[pltpu.VMEM((rows, columns), BF16), pltpu.SemaphoreType.DMA((len(keys),))],
        input_output_aliases={2: 0} if given else {},
        compiler_params=params(4),
        cost_estimate=cost(0, 1024),
        name="total",
    )(held(mine), held(other), *given, *after)


def overlap(heads, starts, queries, bias, w_value, kv, w_output, scale):
    value = w_value.shape[2]
    got, ready = {}, {}
    last, acc, sums = [], None, []
    held_back = {entry[:2] for entry in ORDER}

    def send(name, chunk, after=None):
        nonlocal last
        x, mask = ready.pop((name, chunk))
        if after is not None:
            x = gate(x, after)
            last = [x]
        got[name, chunk] = exchange(x, mask, 8)
        along_z, paired = PLAN[chunk][1:]
        if name == FAR and not paired:
            offer(CROSS, chunk, got[FAR, chunk], 1)
        if name == NEAR and not along_z:
            offer(BOTH, chunk, got[NEAR, chunk], 1)
        if name == SIDE and along_z and paired:
            offer(BOTH, chunk, got[SIDE, chunk], 2)

    def offer(name, chunk, x, mask):
        ready[name, chunk] = x, mask
        if (name, chunk) not in held_back:
            send(name, chunk)

    def parts_of(chunk):
        sides = (SIDE,) if PLAN[chunk][2] else (SIDE, CROSS)
        names = (OWN, FAR), sides, (NEAR,), (BOTH,)
        return [tuple(got[name, chunk] for name in part) for part in names]

    for action, chunk, *waits in ORDER:
        after = last + [got[wait] for wait in waits]
        if action == ATTEND:
            out = attend(starts[chunk], heads[chunk], queries, bias, w_value, kv, scale, after)
            last = [out]
            got[OWN, chunk] = out
            offer(FAR, chunk, out, 6)
            if not PLAN[chunk][2]:
                offer(SIDE, chunk, out, 1)
        elif action == STACK:
            base = stack(got[OWN, chunk], got[FAR, chunk], after)
            last = [base]
            offer(NEAR, chunk, base, 2)
            if PLAN[chunk][2]:
                offer(SIDE, chunk, base, 1)
        elif action == PROJECT:
            some = parts_of(chunk)[: 3 if chunk == len(heads) - 2 else 4]
            acc = project(starts[chunk] * value, some, w_output, acc, after)
            last = [acc]
        elif action == FINISH:
            sums = [finish(starts[chunk] * value, parts_of(chunk)[:3], w_output, acc, after)]
            last = [sums[0][1]]
        elif action == BOTH and PLAN[chunk][1:] == (1, 0):
            pair = stack(got[SIDE, chunk], got[CROSS, chunk], after)
            last = [pair]
            got[BOTH, chunk] = exchange(pair, 2, 8)
        else:
            send(action, chunk, after)
    chunk = len(heads) - 2
    first = 3 if (PROJECT, chunk) in held_back else 0
    some = parts_of(chunk)[first:]
    acc = project(starts[chunk] * value, some, w_output, acc, last, first)
    chunk += 1
    first = 3 if sums else 0
    some = parts_of(chunk)[first:]
    return [*sums, finish(starts[chunk] * value, some, w_output, acc, [acc], first)]


def local(
    q_nope, q_rope, latent_cache, rope_keys, w_absorb, w_value, w_output, span_offset, valid_lengths
):
    head_count, nope_dim, latent = w_absorb.shape
    tokens = q_nope.shape[0]
    rope_dim = rope_keys.shape[1]
    per_shard = latent_cache.shape[0]
    shards = valid_lengths.shape[0]
    value = w_value.shape[2]
    scale = 1.0 / math.sqrt(nope_dim + rope_dim)

    far, *rest = basis_of(shards)
    keys = [0]
    for bit in rest:
        keys += [key ^ bit for key in keys]
    keys = sorted(keys)
    owners = [key ^ (far * inner) for key in keys for inner in range(2)]
    packed = pack(latent_cache, rope_keys)
    queries = prep(q_nope, q_rope, w_absorb)
    bias = mask(span_offset, valid_lengths, owners, tokens, per_shard)
    mine = spread(packed, shards, [queries])
    theirs = {key: sibling(pair) for key, pair in mine.items()}
    kv = join([mine[key] for key in keys], [theirs[key] for key in keys], per_shard, latent + LANES)

    heads = [count * head_count // 32 for count, *_ in PLAN]
    starts = [sum(heads[:chunk]) for chunk in range(len(heads))]
    if shards == 8:
        sums = overlap(heads, starts, queries, bias, w_value, kv, w_output, scale)
        split = (keys[:3], keys[3:]) if len(sums) > 1 else (keys,)
    else:
        acc = None
        for chunk, start in enumerate(starts):
            out = attend(start, heads[chunk], queries, bias, w_value, kv, scale)
            gathered = spread(out, shards)
            parts = [(gathered[key],) for key in keys]
            if chunk < len(heads) - 1:
                acc = project(start * value, parts, w_output, acc)
        sums = [finish(starts[-1] * value, parts, w_output, acc)]
        split = (keys,)

    out, after = None, [sums[-1][1]]
    others = [sibling(given) for given, _ in sums]
    for some, (_, kept), other in zip(split, sums, others):
        out = total(some, far, len(keys), kept, other, out, after)
        after = []
    return out


def solution(mesh):
    return jax.shard_map(
        local,
        mesh=mesh,
        in_specs=(
            P(("groups", "ctx"), "head"),
            P(("groups", "ctx"), "head"),
            P(("groups", "ctx"), None),
            P(("groups", "ctx"), None),
            P("head", None, None),
            P("head", None, None),
            P("head", "ctx"),
            P("groups"),
            P("groups"),
        ),
        out_specs=P(("groups", "head"), "ctx"),
        check_vma=False,
    )
```

```python
import functools
import math

import jax
import jax.numpy as jnp
from jax import lax
from jax.experimental import pallas as pl
from jax.experimental.pallas import tpu as pltpu
from jax.sharding import PartitionSpec as P

F32 = jnp.float32
BF16 = jnp.bfloat16
MASKED = -1e30
LANES = 128
STEP = 4
WIDE = 256
ROWS = 32
PLAN = ((4, 0, 0), (8, 0, 0), (6, 0, 0), (8, 0, 0), (6, 1, 0))
FAR, SIDE, CROSS, NEAR, BOTH = "far", "side", "cross", "near", "both"
ATTEND, STACK, PROJECT, FINISH, OWN = "attend", "stack", "project", "finish", "own"
ORDER = (
    (ATTEND, 0), (ATTEND, 1), (STACK, 0), (ATTEND, 2), (CROSS, 0), (STACK, 1), (FAR, 2),
    (BOTH, 0, (SIDE, 1), (SIDE, 2)), (ATTEND, 3, (CROSS, 0)), (ATTEND, 4), (CROSS, 1, (BOTH, 0)),
    (PROJECT, 0, (SIDE, 3), (NEAR, 0)), (STACK, 2), (FAR, 3, (NEAR, 1)), (CROSS, 2, (CROSS, 1)),
    (BOTH, 1, (SIDE, 4)), (BOTH, 2, (CROSS, 2)), (FAR, 4, (NEAR, 2)), (STACK, 3),
    (CROSS, 3, (BOTH, 1), (SIDE, 3)), (PROJECT, 1, (NEAR, 1)), (CROSS, 4), (STACK, 4),
    (PROJECT, 2, (CROSS, 3)), (BOTH, 4), (PROJECT, 3, (NEAR, 4)),
)
LOCAL = pl.BlockSpec(memory_space=pltpu.VMEM)
ANYWHERE = pl.BlockSpec(memory_space=pl.ANY)
SCALARS = pl.BlockSpec(memory_space=pltpu.SMEM)


def params(mib):
    return pltpu.CompilerParams(vmem_limit_bytes=mib * 1024 * 1024)


def cost(flops, size, exps=0):
    return pl.CostEstimate(flops=flops, bytes_accessed=size, transcendentals=exps)


def held(x):
    return pltpu.with_memory_space_constraint(x, pltpu.VMEM)


def basis_of(shards):
    if shards == 8:
        return (6, 2, 1)
    return tuple(1 << bit for bit in reversed(range(shards.bit_length() - 1)))


def exchange(x, mask, shards):
    return lax.ppermute(x, "ctx", [(i, i ^ mask) for i in range(shards)])


def sibling(x):
    return lax.ppermute(x, "head", [(0, 1), (1, 0)])


def stack_kernel(first_ref, second_ref, *refs):
    out_ref = refs[-1]
    out_ref[0] = first_ref[...]
    out_ref[1] = second_ref[...]


def stack(first, second, after=()):
    return pl.pallas_call(
        stack_kernel,
        in_specs=[LOCAL, LOCAL] + [ANYWHERE] * len(after),
        out_specs=LOCAL,
        out_shape=pltpu.VMEM((2, *first.shape), first.dtype),
        compiler_params=params(2),
        cost_estimate=cost(0, 1024),
        name="stack",
    )(held(first), held(second), *after)


def spread(x, shards, after=()):
    first, *rest = basis_of(shards)
    pairs = {0: stack(x, exchange(x, first, shards), after)}
    for mask in rest:
        pairs.update({key ^ mask: exchange(pair, mask, shards) for key, pair in pairs.items()})
    return pairs


def gate_kernel(x_ref, *refs):
    refs[-1][...] = x_ref[...]


def gate(x, after):
    return pl.pallas_call(
        gate_kernel,
        in_specs=[LOCAL] + [ANYWHERE] * len(after),
        out_specs=LOCAL,
        out_shape=pltpu.VMEM(x.shape, x.dtype),
        compiler_params=params(2),
        cost_estimate=cost(0, 1024),
        name="gate",
    )(held(x), *after)


def pack_kernel(latent_hbm, rope_hbm, out_ref, latent_ref, rope_ref, sem):
    copies = (
        pltpu.make_async_copy(latent_hbm, latent_ref, sem.at[0]),
        pltpu.make_async_copy(rope_hbm, rope_ref, sem.at[1]),
    )
    for copy in copies:
        copy.start()
    rows, latent = latent_ref.shape
    rope = rope_ref.shape[0]
    tiles = latent // LANES // 2
    pairs, own = packed_rows(rows)
    side = lax.axis_index("head")
    for copy in copies:
        copy.wait()
    turned = rope_ref[...].astype(F32).T.astype(BF16)
    for at in range(2):

        @pl.when(side == at)
        def _(at=at):
            for tile in range(tiles):
                lanes = slice((at * tiles + tile) * LANES, (at * tiles + tile + 1) * LANES)
                out_ref[tile * rows : (tile + 1) * rows, :] = latent_ref[:, lanes]
            first = at * (pairs - own)
            to = slice(tiles * rows, tiles * rows + own)
            out_ref[to, :rope] = turned[first : first + own, :]
            second = first + rows - pairs
            out_ref[to, rope:] = turned[second : second + own, :]


def packed_rows(rows):
    pairs = -(-rows // 32) * 16
    return pairs, -(-pairs // 32) * 16


def pack(latent_cache, rope_keys):
    arrays = (latent_cache, rope_keys.T)
    rows, latent = latent_cache.shape
    _, own = packed_rows(rows)
    return pl.pallas_call(
        pack_kernel,
        in_specs=[ANYWHERE] * 2,
        out_specs=LOCAL,
        out_shape=pltpu.VMEM((latent // LANES // 2 * rows + own, LANES), BF16),
        scratch_shapes=[pltpu.VMEM(x.shape, x.dtype) for x in arrays]
        + [pltpu.SemaphoreType.DMA((2,))],
        compiler_params=params(2),
        cost_estimate=cost(0, 1024),
        name="pack",
    )(*(pltpu.with_memory_space_constraint(x, pltpu.HBM) for x in arrays))


def mask_kernel(owners, span_ref, valid_ref, bias_ref):
    tokens, keys = bias_ref.shape
    per_shard = keys // len(owners)
    me = lax.axis_index("ctx")
    column = lax.broadcasted_iota(jnp.int32, (1, keys), 1)
    place = jnp.full((1, keys), 2**30, jnp.int32)
    for at, owner in enumerate(owners):
        shard = me ^ owner
        row = column - at * per_shard
        here = (row >= 0) & (row < per_shard) & (row < valid_ref[shard])
        place = jnp.where(here, row + shard * per_shard, place)
    position = span_ref[0] + me * tokens + lax.broadcasted_iota(jnp.int32, (tokens, keys), 0)
    bias_ref[...] = jnp.where(place <= position, F32(0.0), F32(MASKED))


def mask(span_offset, valid_lengths, owners, tokens, per_shard):
    return pl.pallas_call(
        functools.partial(mask_kernel, owners),
        in_specs=[SCALARS, SCALARS],
        out_specs=LOCAL,
        out_shape=pltpu.VMEM((tokens, per_shard * len(owners)), F32),
        compiler_params=params(4),
        cost_estimate=cost(0, 1024),
        name="mask",
    )(span_offset, valid_lengths)


def prep_kernel(q_hbm, r_hbm, w_hbm, lat_ref, q_ref, r_ref, w_ref, sem):
    tokens = q_ref.shape[0]
    heads, nope, latent = w_ref.shape
    rope = r_ref.shape[1] // heads
    whole = (
        pltpu.make_async_copy(q_hbm, q_ref, sem.at[0]),
        pltpu.make_async_copy(r_hbm, r_ref, sem.at[1]),
    )
    pieces = [
        pltpu.make_async_copy(
            w_hbm.at[pl.ds(at, STEP)], w_ref.at[pl.ds(at, STEP)], sem.at[2 + at // STEP]
        )
        for at in range(0, heads, STEP)
    ]
    for copy in (*whole, *pieces):
        copy.start()
    for copy in whole:
        copy.wait()
    for head in range(heads):
        if head % STEP == 0:
            pieces[head // STEP].wait()
        rows = slice(head * tokens, (head + 1) * tokens)
        lat = jnp.dot(
            q_ref[:, head * nope : (head + 1) * nope], w_ref[head], preferred_element_type=F32
        )
        lat_ref[rows, :latent] = lat.astype(BF16)
        turned = r_ref[:, head * rope : (head + 1) * rope]
        lat_ref[rows, latent : latent + rope] = turned
        lat_ref[rows, latent + rope :] = turned


def prep(q_nope, q_rope, w_absorb):
    heads, _, latent = w_absorb.shape
    tokens = q_nope.shape[0]
    arrays = (q_nope, q_rope, w_absorb)
    return pl.pallas_call(
        prep_kernel,
        in_specs=[ANYWHERE] * 3,
        out_specs=LOCAL,
        out_shape=pltpu.VMEM((heads * tokens, latent + LANES), BF16),
        scratch_shapes=[pltpu.VMEM(x.shape, x.dtype) for x in arrays]
        + [pltpu.SemaphoreType.DMA((2 + heads // STEP,))],
        compiler_params=params(10),
        cost_estimate=cost(0, 1024),
        name="prep",
    )(*(pltpu.with_memory_space_constraint(x, pltpu.HBM) for x in arrays))


def join_kernel(groups, *refs):
    mine = refs[:groups]
    theirs = refs[groups : 2 * groups]
    out_ref = refs[-1]
    rows = out_ref.shape[0] // (2 * groups)
    latent = out_ref.shape[1] - LANES
    tiles = latent // LANES // 2
    pairs, own = packed_rows(rows)
    side = lax.axis_index("head")
    half = lax.broadcasted_iota(jnp.int32, (pairs, LANES), 1) < LANES // 2
    nothing = jnp.zeros((pairs, LANES), BF16)
    for which in range(2):

        @pl.when(side == which)
        def _(which=which):
            for at in range(2 * groups):
                start = at * rows
                sides = [mine[at // 2], theirs[at // 2]][:: 1 - 2 * which]
                for tile in range(2 * tiles):
                    block = sides[tile // tiles][at % 2, tile % tiles * rows : (tile % tiles + 1) * rows]
                    out_ref[start : start + rows, tile * LANES : (tile + 1) * LANES] = block
                low = sides[0][at % 2, tiles * rows : tiles * rows + own]
                high = sides[1][at % 2, tiles * rows + 2 * own - pairs : tiles * rows + own]
                both = jnp.concatenate([low, high], axis=0)
                out_ref[start : start + pairs, latent:] = jnp.where(half, both, nothing)
                rest = jnp.where(half, nothing, both)[2 * pairs - rows :]
                out_ref[start + pairs : start + rows, latent:] = rest


def join(mine, theirs, per_shard, depth):
    groups = len(mine)
    return pl.pallas_call(
        functools.partial(join_kernel, groups),
        in_specs=[LOCAL] * (2 * groups),
        out_specs=LOCAL,
        out_shape=pltpu.VMEM((2 * groups * per_shard, depth), BF16),
        compiler_params=params(4),
        cost_estimate=cost(0, 1024),
        name="join",
    )(*map(held, mine), *map(held, theirs))


def interleave(first, second):
    steps = [((at + 0.5) / len(x), which, step) for which, x in enumerate((first, second)) for at, step in enumerate(x)]
    for *_, step in sorted(steps, key=lambda entry: entry[:2]):
        step()


def attend_kernel(scale, start, heads, q_ref, bias_ref, w_ref, kv_ref, *refs):
    out_ref, scores, probs, totals, mixed = refs[-5:]
    tokens, keys = bias_ref.shape
    _, latent, value = w_ref.shape
    block = scores.shape[1]
    pair = block // tokens

    def score(at):
        row = start * tokens + at * block

        def part(low):
            span = slice(low, min(low + WIDE, keys))
            scores[at % 2, :, span] = lax.dot_general(
                q_ref[row : row + block, :],
                kv_ref[span, :],
                (((1,), (1,)), ((), ())),
                preferred_element_type=F32,
            )

        return [functools.partial(part, low) for low in range(0, keys, WIDE)]

    def soften(at):
        def part(low):
            rows = slice(low, low + ROWS)
            masked = scores[at % 2, rows, :] + bias_ref[low % tokens : low % tokens + ROWS, :]
            top = jnp.max(masked, axis=-1, keepdims=True)
            expo = jnp.exp2((masked - top) * F32(scale))
            totals[at % 2, rows, :] = jnp.sum(expo, axis=-1, keepdims=True)
            probs[at % 2, rows, :] = expo.astype(BF16)

        return [functools.partial(part, low) for low in range(0, block, ROWS)]

    def weigh(at):
        def part(low):
            span = slice(low, low + WIDE)
            weighted = jnp.dot(probs[at % 2], kv_ref[:, span], preferred_element_type=F32)
            mixed[:, span] = (weighted / totals[at % 2]).astype(BF16)

        def last(head):
            which = at * pair + head
            rows = slice(head * tokens, (head + 1) * tokens)
            out = jnp.dot(mixed[rows, :], w_ref[start + which], preferred_element_type=F32)
            out_ref[:, which * value : (which + 1) * value] = out.astype(BF16)

        parts = [functools.partial(part, low) for low in range(0, latent, WIDE)]
        return parts + [functools.partial(last, head) for head in range(pair)]

    blocks = heads // pair
    for step in range(blocks + 2):
        products = weigh(step - 2) if step > 1 else []
        if step < blocks:
            products = products + score(step)
        interleave(products, soften(step - 1) if 0 < step <= blocks else [])


def attend(start, heads, queries, bias, w_value, kv, scale, after=()):
    tokens, keys = bias.shape
    value = w_value.shape[2]
    block = next(count for count in (4, 3, 2, 1) if heads % count == 0 and heads > count) * tokens
    return pl.pallas_call(
        functools.partial(attend_kernel, scale * math.log2(math.e), start, heads),
        in_specs=[LOCAL] * 4 + [ANYWHERE] * len(after),
        out_specs=LOCAL,
        out_shape=pltpu.VMEM((tokens, heads * value), BF16),
        scratch_shapes=[
            pltpu.VMEM((2, block, keys), F32),
            pltpu.VMEM((2, block, keys), BF16),
            pltpu.VMEM((2, block, 1), F32),
            pltpu.VMEM((block, w_value.shape[1]), BF16),
        ],
        compiler_params=params(20),
        cost_estimate=cost(0, 1024),
        name=f"attend{start}",
    )(held(queries), held(bias), held(w_value), held(kv), *after)


def gather_into(rows_of, parts, side):
    tokens = parts[0][0].shape[-2]
    for at, part in enumerate(parts):
        rows = pl.ds(at * tokens, tokens)
        if len(part) == 1:
            rows_of[rows] = part[0][side]
        elif isinstance(side, int):
            rows_of[rows] = part[side][...]
        else:
            for which in range(2):

                @pl.when(side == which)
                def _(rows=rows, part=part, which=which):
                    rows_of[rows] = part[which][...]


def grouped(refs, sizes):
    refs = iter(refs)
    return [tuple(next(refs) for _ in range(size)) for size in sizes]


def project_kernel(start, sizes, first, fresh, w_ref, *refs):
    out_ref, gathered = refs[-2:]
    parts = grouped(refs, sizes)
    tokens, depth = parts[0][0].shape[-2:]
    for side in range(2):
        gather_into(gathered.at[side], parts, side)
    weights = w_ref[start : start + depth]
    each = min(2, len(parts)) * tokens
    for side in range(2):
        for row in range(0, len(parts) * tokens, each):
            rows = slice(row, min(row + each, len(parts) * tokens))
            to = slice(first * tokens + rows.start, first * tokens + rows.stop)
            product = jnp.dot(gathered[side, rows], weights, preferred_element_type=F32)
            out_ref[side, to] = product if fresh else refs[sum(sizes)][side, to] + product


def project(start, parts, w_output, acc, after=(), first=0):
    sizes = tuple(map(len, parts))
    blocks = [block for part in parts for block in part]
    tokens, depth = blocks[0].shape[-2:]
    columns = w_output.shape[1]
    operands = [w_output, *blocks] + ([] if acc is None else [acc])
    shape = (2, len(parts) * tokens, columns) if acc is None else acc.shape
    return pl.pallas_call(
        functools.partial(project_kernel, start, sizes, first, acc is None),
        in_specs=[LOCAL] * len(operands) + [ANYWHERE] * len(after),
        out_specs=LOCAL,
        out_shape=pltpu.VMEM(shape, F32),
        scratch_shapes=[pltpu.VMEM((2, len(parts) * tokens, depth), BF16)],
        input_output_aliases={} if acc is None else {len(operands) - 1: 0},
        compiler_params=params(12),
        cost_estimate=cost(0, 1024),
        name=f"project{start}",
    )(*map(held, operands), *after)


def other_half(groups, keep):
    me, side = lax.axis_index("ctx"), lax.axis_index("head")
    return ((me // groups) ^ side ^ (1 - keep)).astype(jnp.int32)


def finish_kernel(start, sizes, first, keep, w_ref, *refs):
    out_ref, gathered = refs[-2:]
    acc_ref = refs[sum(sizes)]
    parts = grouped(refs, sizes)
    tokens, depth = parts[0][0].shape[-2:]
    rows = slice(first * tokens, (first + len(parts)) * tokens)
    other = other_half(acc_ref.shape[1] // tokens, keep)
    gather_into(gathered, parts, other)
    product = jnp.dot(
        gathered[...], w_ref[start : start + depth], preferred_element_type=F32
    )
    out_ref[...] = (acc_ref[other, rows] + product).astype(out_ref.dtype)


def finish(start, parts, w_output, acc, after=(), first=0):
    sizes = tuple(map(len, parts))
    blocks = [block for part in parts for block in part]
    tokens, depth = blocks[0].shape[-2:]
    columns = w_output.shape[1]
    rows = len(parts) * tokens
    outs = []
    for keep, dtype in enumerate((BF16, F32)):
        after = [*after, *outs]
        outs.append(
            pl.pallas_call(
                functools.partial(finish_kernel, start, sizes, first, keep),
                in_specs=[LOCAL] * (2 + len(blocks)) + [ANYWHERE] * len(after),
                out_specs=LOCAL,
                out_shape=pltpu.VMEM((rows, columns), dtype),
                scratch_shapes=[pltpu.VMEM((rows, depth), BF16)],
                compiler_params=params(12),
                cost_estimate=cost(0, 1024),
                name=f"finish{keep}",
            )(*map(held, [w_output, *blocks, acc]), *after)
        )
    return outs


def total_kernel(keys, far, groups, mine_ref, other_ref, *refs):
    out_ref, rounded, sem = refs[-3:]
    tokens = mine_ref.shape[0] // len(keys)
    me = lax.axis_index("ctx")
    other = other_half(groups, 1)
    copies = []
    for at, key in enumerate(keys):
        rows = pl.ds(at * tokens, tokens)
        place = (me ^ key ^ (far * other)) % groups
        to = pl.ds(pl.multiple_of(place * tokens, tokens), tokens)
        rounded[rows] = (mine_ref[rows] + other_ref[rows].astype(F32)).astype(BF16)
        copies.append(pltpu.make_async_copy(rounded.at[rows], out_ref.at[to], sem.at[at]))
        copies[-1].start()
    for copy in copies:
        copy.wait()


def total(keys, far, groups, mine, other, out, after):
    rows, columns = mine.shape
    tokens = rows // len(keys)
    given = [] if out is None else [out]
    return pl.pallas_call(
        functools.partial(total_kernel, keys, far, groups),
        in_specs=[LOCAL] * 2 + [ANYWHERE] * (len(given) + len(after)),
        out_specs=ANYWHERE,
        out_shape=jax.ShapeDtypeStruct((groups * tokens, columns), BF16),
        scratch_shapes=[pltpu.VMEM((rows, columns), BF16), pltpu.SemaphoreType.DMA((len(keys),))],
        input_output_aliases={2: 0} if given else {},
        compiler_params=params(4),
        cost_estimate=cost(0, 1024),
        name="total",
    )(held(mine), held(other), *given, *after)


def overlap(heads, starts, queries, bias, w_value, kv, w_output, scale):
    value = w_value.shape[2]
    got, ready = {}, {}
    last, acc, sums = [], None, []
    held_back = {entry[:2] for entry in ORDER}

    def send(name, chunk, after=None):
        nonlocal last
        x, mask = ready.pop((name, chunk))
        if after is not None:
            x = gate(x, after)
            last = [x]
        got[name, chunk] = exchange(x, mask, 8)
        along_z, paired = PLAN[chunk][1:]
        if name == FAR and not paired:
            offer(CROSS, chunk, got[FAR, chunk], 1)
        if name == NEAR and not along_z:
            offer(BOTH, chunk, got[NEAR, chunk], 1)
        if name == SIDE and along_z and paired:
            offer(BOTH, chunk, got[SIDE, chunk], 2)

    def offer(name, chunk, x, mask):
        ready[name, chunk] = x, mask
        if (name, chunk) not in held_back:
            send(name, chunk)

    def parts_of(chunk):
        sides = (SIDE,) if PLAN[chunk][2] else (SIDE, CROSS)
        names = (OWN, FAR), sides, (NEAR,), (BOTH,)
        return [tuple(got[name, chunk] for name in part) for part in names]

    for action, chunk, *waits in ORDER:
        after = last + [got[wait] for wait in waits]
        if action == ATTEND:
            out = attend(starts[chunk], heads[chunk], queries, bias, w_value, kv, scale, after)
            last = [out]
            got[OWN, chunk] = out
            offer(FAR, chunk, out, 6)
            if not PLAN[chunk][2]:
                offer(SIDE, chunk, out, 1)
        elif action == STACK:
            base = stack(got[OWN, chunk], got[FAR, chunk], after)
            last = [base]
            offer(NEAR, chunk, base, 2)
            if PLAN[chunk][2]:
                offer(SIDE, chunk, base, 1)
        elif action == PROJECT:
            some = parts_of(chunk)[: 3 if chunk == len(heads) - 2 else 4]
            acc = project(starts[chunk] * value, some, w_output, acc, after)
            last = [acc]
        elif action == FINISH:
            sums = [finish(starts[chunk] * value, parts_of(chunk)[:3], w_output, acc, after)]
            last = [sums[0][1]]
        elif action == BOTH and PLAN[chunk][1:] == (1, 0):
            pair = stack(got[SIDE, chunk], got[CROSS, chunk], after)
            last = [pair]
            got[BOTH, chunk] = exchange(pair, 2, 8)
        else:
            send(action, chunk, after)
    chunk = len(heads) - 2
    first = 3 if (PROJECT, chunk) in held_back else 0
    some = parts_of(chunk)[first:]
    acc = project(starts[chunk] * value, some, w_output, acc, last, first)
    chunk += 1
    first = 3 if sums else 0
    some = parts_of(chunk)[first:]
    return [*sums, finish(starts[chunk] * value, some, w_output, acc, [acc], first)]


def local(
    q_nope, q_rope, latent_cache, rope_keys, w_absorb, w_value, w_output, span_offset, valid_lengths
):
    head_count, nope_dim, latent = w_absorb.shape
    tokens = q_nope.shape[0]
    rope_dim = rope_keys.shape[1]
    per_shard = latent_cache.shape[0]
    shards = valid_lengths.shape[0]
    value = w_value.shape[2]
    scale = 1.0 / math.sqrt(nope_dim + rope_dim)

    far, *rest = basis_of(shards)
    keys = [0]
    for bit in rest:
        keys += [key ^ bit for key in keys]
    keys = sorted(keys)
    owners = [key ^ (far * inner) for key in keys for inner in range(2)]
    packed = pack(latent_cache, rope_keys)
    queries = prep(q_nope, q_rope, w_absorb)
    bias = mask(span_offset, valid_lengths, owners, tokens, per_shard)
    mine = spread(packed, shards, [queries])
    theirs = {key: sibling(pair) for key, pair in mine.items()}
    kv = join([mine[key] for key in keys], [theirs[key] for key in keys], per_shard, latent + LANES)

    heads = [count * head_count // 32 for count, *_ in PLAN]
    starts = [sum(heads[:chunk]) for chunk in range(len(heads))]
    if shards == 8:
        sums = overlap(heads, starts, queries, bias, w_value, kv, w_output, scale)
        split = (keys[:3], keys[3:]) if len(sums) > 1 else (keys,)
    else:
        acc = None
        for chunk, start in enumerate(starts):
            out = attend(start, heads[chunk], queries, bias, w_value, kv, scale)
            gathered = spread(out, shards)
            parts = [(gathered[key],) for key in keys]
            if chunk < len(heads) - 1:
                acc = project(start * value, parts, w_output, acc)
        sums = [finish(starts[-1] * value, parts, w_output, acc)]
        split = (keys,)

    out, after = None, [sums[-1][1]]
    others = [sibling(given) for given, _ in sums]
    for some, (_, kept), other in zip(split, sums, others):
        out = total(some, far, len(keys), kept, other, out, after)
        after = []
    return out


def solution(mesh):
    return jax.shard_map(
        local,
        mesh=mesh,
        in_specs=(
            P(("groups", "ctx"), "head"),
            P(("groups", "ctx"), "head"),
            P(("groups", "ctx"), None),
            P(("groups", "ctx"), None),
            P("head", None, None),
            P("head", None, None),
            P("head", "ctx"),
            P("groups"),
            P("groups"),
        ),
        out_specs=P(("groups", "head"), "ctx"),
        check_vma=False,
    )
```

```python
import functools
import math

import jax
import jax.numpy as jnp
from jax import lax
from jax.experimental import pallas as pl
from jax.experimental.pallas import tpu as pltpu
from jax.sharding import PartitionSpec as P

F32 = jnp.float32
BF16 = jnp.bfloat16
MASKED = -1e30
LANES = 128
STEP = 4
WIDE = 256
ROWS = 32
PLAN = ((4, 0, 0), (8, 0, 0), (6, 0, 0), (8, 0, 0), (6, 1, 0))
FAR, SIDE, CROSS, NEAR, BOTH = "far", "side", "cross", "near", "both"
ATTEND, STACK, PROJECT, FINISH, OWN = "attend", "stack", "project", "finish", "own"
ORDER = (
    (ATTEND, 0), (ATTEND, 1), (STACK, 0), (ATTEND, 2), (CROSS, 0), (STACK, 1), (FAR, 2),
    (BOTH, 0, (SIDE, 1), (SIDE, 2)), (ATTEND, 3, (CROSS, 0)), (ATTEND, 4), (CROSS, 1, (BOTH, 0)),
    (PROJECT, 0, (SIDE, 3), (NEAR, 0)), (STACK, 2), (FAR, 3, (NEAR, 1)), (CROSS, 2, (CROSS, 1)),
    (BOTH, 1, (SIDE, 4)), (BOTH, 2, (CROSS, 2)), (FAR, 4, (NEAR, 2)), (STACK, 3),
    (CROSS, 3, (BOTH, 1), (SIDE, 3)), (PROJECT, 1, (NEAR, 1)), (CROSS, 4), (STACK, 4),
    (PROJECT, 2, (CROSS, 3)), (BOTH, 4), (PROJECT, 3, (NEAR, 4)),
)
LOCAL = pl.BlockSpec(memory_space=pltpu.VMEM)
ANYWHERE = pl.BlockSpec(memory_space=pl.ANY)
SCALARS = pl.BlockSpec(memory_space=pltpu.SMEM)


def params(mib):
    return pltpu.CompilerParams(vmem_limit_bytes=mib * 1024 * 1024)


def cost(flops, size, exps=0):
    return pl.CostEstimate(flops=flops, bytes_accessed=size, transcendentals=exps)


def held(x):
    return pltpu.with_memory_space_constraint(x, pltpu.VMEM)


def basis_of(shards):
    if shards == 8:
        return (6, 2, 1)
    return tuple(1 << bit for bit in reversed(range(shards.bit_length() - 1)))


def exchange(x, mask, shards):
    return lax.ppermute(x, "ctx", [(i, i ^ mask) for i in range(shards)])


def sibling(x):
    return lax.ppermute(x, "head", [(0, 1), (1, 0)])


def stack_kernel(first_ref, second_ref, *refs):
    out_ref = refs[-1]
    out_ref[0] = first_ref[...]
    out_ref[1] = second_ref[...]


def stack(first, second, after=()):
    return pl.pallas_call(
        stack_kernel,
        in_specs=[LOCAL, LOCAL] + [ANYWHERE] * len(after),
        out_specs=LOCAL,
        out_shape=pltpu.VMEM((2, *first.shape), first.dtype),
        compiler_params=params(2),
        cost_estimate=cost(0, 1024),
        name="stack",
    )(held(first), held(second), *after)


def spread(x, shards, after=()):
    first, *rest = basis_of(shards)
    pairs = {0: stack(x, exchange(x, first, shards), after)}
    for mask in rest:
        pairs.update({key ^ mask: exchange(pair, mask, shards) for key, pair in pairs.items()})
    return pairs


def gate_kernel(x_ref, *refs):
    refs[-1][...] = x_ref[...]


def gate(x, after):
    return pl.pallas_call(
        gate_kernel,
        in_specs=[LOCAL] + [ANYWHERE] * len(after),
        out_specs=LOCAL,
        out_shape=pltpu.VMEM(x.shape, x.dtype),
        compiler_params=params(2),
        cost_estimate=cost(0, 1024),
        name="gate",
    )(held(x), *after)


def pack_kernel(latent_hbm, rope_hbm, out_ref, latent_ref, rope_ref, sem):
    copies = (
        pltpu.make_async_copy(latent_hbm, latent_ref, sem.at[0]),
        pltpu.make_async_copy(rope_hbm, rope_ref, sem.at[1]),
    )
    for copy in copies:
        copy.start()
    rows, latent = latent_ref.shape
    rope = rope_ref.shape[0]
    tiles = latent // LANES // 2
    pairs, own = packed_rows(rows)
    side = lax.axis_index("head")
    for copy in copies:
        copy.wait()
    turned = rope_ref[...].astype(F32).T.astype(BF16)
    for at in range(2):

        @pl.when(side == at)
        def _(at=at):
            for tile in range(tiles):
                lanes = slice((at * tiles + tile) * LANES, (at * tiles + tile + 1) * LANES)
                out_ref[tile * rows : (tile + 1) * rows, :] = latent_ref[:, lanes]
            first = at * (pairs - own)
            to = slice(tiles * rows, tiles * rows + own)
            out_ref[to, :rope] = turned[first : first + own, :]
            second = first + rows - pairs
            out_ref[to, rope:] = turned[second : second + own, :]


def packed_rows(rows):
    pairs = -(-rows // 32) * 16
    return pairs, -(-pairs // 32) * 16


def pack(latent_cache, rope_keys):
    arrays = (latent_cache, rope_keys.T)
    rows, latent = latent_cache.shape
    _, own = packed_rows(rows)
    return pl.pallas_call(
        pack_kernel,
        in_specs=[ANYWHERE] * 2,
        out_specs=LOCAL,
        out_shape=pltpu.VMEM((latent // LANES // 2 * rows + own, LANES), BF16),
        scratch_shapes=[pltpu.VMEM(x.shape, x.dtype) for x in arrays]
        + [pltpu.SemaphoreType.DMA((2,))],
        compiler_params=params(2),
        cost_estimate=cost(0, 1024),
        name="pack",
    )(*(pltpu.with_memory_space_constraint(x, pltpu.HBM) for x in arrays))


def mask_kernel(owners, span_ref, valid_ref, bias_ref):
    tokens, keys = bias_ref.shape
    per_shard = keys // len(owners)
    me = lax.axis_index("ctx")
    column = lax.broadcasted_iota(jnp.int32, (1, keys), 1)
    place = jnp.full((1, keys), 2**30, jnp.int32)
    for at, owner in enumerate(owners):
        shard = me ^ owner
        row = column - at * per_shard
        here = (row >= 0) & (row < per_shard) & (row < valid_ref[shard])
        place = jnp.where(here, row + shard * per_shard, place)
    position = span_ref[0] + me * tokens + lax.broadcasted_iota(jnp.int32, (tokens, keys), 0)
    bias_ref[...] = jnp.where(place <= position, F32(0.0), F32(MASKED))


def mask(span_offset, valid_lengths, owners, tokens, per_shard):
    return pl.pallas_call(
        functools.partial(mask_kernel, owners),
        in_specs=[SCALARS, SCALARS],
        out_specs=LOCAL,
        out_shape=pltpu.VMEM((tokens, per_shard * len(owners)), F32),
        compiler_params=params(4),
        cost_estimate=cost(0, 1024),
        name="mask",
    )(span_offset, valid_lengths)


def prep_kernel(q_hbm, r_hbm, w_hbm, lat_ref, q_ref, r_ref, w_ref, sem):
    tokens = q_ref.shape[0]
    heads, nope, latent = w_ref.shape
    rope = r_ref.shape[1] // heads
    whole = (
        pltpu.make_async_copy(q_hbm, q_ref, sem.at[0]),
        pltpu.make_async_copy(r_hbm, r_ref, sem.at[1]),
    )
    pieces = [
        pltpu.make_async_copy(
            w_hbm.at[pl.ds(at, STEP)], w_ref.at[pl.ds(at, STEP)], sem.at[2 + at // STEP]
        )
        for at in range(0, heads, STEP)
    ]
    for copy in (*whole, *pieces):
        copy.start()
    for copy in whole:
        copy.wait()
    for head in range(heads):
        if head % STEP == 0:
            pieces[head // STEP].wait()
        rows = slice(head * tokens, (head + 1) * tokens)
        lat = jnp.dot(
            q_ref[:, head * nope : (head + 1) * nope], w_ref[head], preferred_element_type=F32
        )
        lat_ref[rows, :latent] = lat.astype(BF16)
        turned = r_ref[:, head * rope : (head + 1) * rope]
        lat_ref[rows, latent : latent + rope] = turned
        lat_ref[rows, latent + rope :] = turned


def prep(q_nope, q_rope, w_absorb):
    heads, _, latent = w_absorb.shape
    tokens = q_nope.shape[0]
    arrays = (q_nope, q_rope, w_absorb)
    return pl.pallas_call(
        prep_kernel,
        in_specs=[ANYWHERE] * 3,
        out_specs=LOCAL,
        out_shape=pltpu.VMEM((heads * tokens, latent + LANES), BF16),
        scratch_shapes=[pltpu.VMEM(x.shape, x.dtype) for x in arrays]
        + [pltpu.SemaphoreType.DMA((2 + heads // STEP,))],
        compiler_params=params(10),
        cost_estimate=cost(0, 1024),
        name="prep",
    )(*(pltpu.with_memory_space_constraint(x, pltpu.HBM) for x in arrays))


def join_kernel(groups, *refs):
    mine = refs[:groups]
    theirs = refs[groups : 2 * groups]
    out_ref = refs[-1]
    rows = out_ref.shape[0] // (2 * groups)
    latent = out_ref.shape[1] - LANES
    tiles = latent // LANES // 2
    pairs, own = packed_rows(rows)
    side = lax.axis_index("head")
    half = lax.broadcasted_iota(jnp.int32, (pairs, LANES), 1) < LANES // 2
    nothing = jnp.zeros((pairs, LANES), BF16)
    for which in range(2):

        @pl.when(side == which)
        def _(which=which):
            for at in range(2 * groups):
                start = at * rows
                sides = [mine[at // 2], theirs[at // 2]][:: 1 - 2 * which]
                for tile in range(2 * tiles):
                    block = sides[tile // tiles][at % 2, tile % tiles * rows : (tile % tiles + 1) * rows]
                    out_ref[start : start + rows, tile * LANES : (tile + 1) * LANES] = block
                low = sides[0][at % 2, tiles * rows : tiles * rows + own]
                high = sides[1][at % 2, tiles * rows + 2 * own - pairs : tiles * rows + own]
                both = jnp.concatenate([low, high], axis=0)
                out_ref[start : start + pairs, latent:] = jnp.where(half, both, nothing)
                rest = jnp.where(half, nothing, both)[2 * pairs - rows :]
                out_ref[start + pairs : start + rows, latent:] = rest


def join(mine, theirs, per_shard, depth):
    groups = len(mine)
    return pl.pallas_call(
        functools.partial(join_kernel, groups),
        in_specs=[LOCAL] * (2 * groups),
        out_specs=LOCAL,
        out_shape=pltpu.VMEM((2 * groups * per_shard, depth), BF16),
        compiler_params=params(4),
        cost_estimate=cost(0, 1024),
        name="join",
    )(*map(held, mine), *map(held, theirs))


def interleave(first, second):
    steps = [((at + 0.5) / len(x), which, step) for which, x in enumerate((first, second)) for at, step in enumerate(x)]
    for *_, step in sorted(steps, key=lambda entry: entry[:2]):
        step()


def attend_kernel(scale, start, heads, q_ref, bias_ref, w_ref, kv_ref, *refs):
    out_ref, scores, probs, totals, mixed = refs[-5:]
    tokens, keys = bias_ref.shape
    _, latent, value = w_ref.shape
    block = scores.shape[1]
    pair = block // tokens

    def score(at):
        row = start * tokens + at * block

        def part(low):
            span = slice(low, min(low + WIDE, keys))
            scores[at % 2, :, span] = lax.dot_general(
                q_ref[row : row + block, :],
                kv_ref[span, :],
                (((1,), (1,)), ((), ())),
                preferred_element_type=F32,
            )

        return [functools.partial(part, low) for low in range(0, keys, WIDE)]

    def soften(at):
        def part(low):
            rows = slice(low, low + ROWS)
            masked = scores[at % 2, rows, :] + bias_ref[low % tokens : low % tokens + ROWS, :]
            top = jnp.max(masked, axis=-1, keepdims=True)
            expo = jnp.exp2((masked - top) * F32(scale))
            totals[at % 2, rows, :] = jnp.sum(expo, axis=-1, keepdims=True)
            probs[at % 2, rows, :] = expo.astype(BF16)

        return [functools.partial(part, low) for low in range(0, block, ROWS)]

    def weigh(at):
        def part(low):
            span = slice(low, low + WIDE)
            weighted = jnp.dot(probs[at % 2], kv_ref[:, span], preferred_element_type=F32)
            mixed[:, span] = (weighted / totals[at % 2]).astype(BF16)

        def last(head):
            which = at * pair + head
            rows = slice(head * tokens, (head + 1) * tokens)
            out = jnp.dot(mixed[rows, :], w_ref[start + which], preferred_element_type=F32)
            out_ref[:, which * value : (which + 1) * value] = out.astype(BF16)

        parts = [functools.partial(part, low) for low in range(0, latent, WIDE)]
        return parts + [functools.partial(last, head) for head in range(pair)]

    blocks = heads // pair
    for step in range(blocks + 2):
        products = weigh(step - 2) if step > 1 else []
        if step < blocks:
            products = products + score(step)
        interleave(products, soften(step - 1) if 0 < step <= blocks else [])


def attend(start, heads, queries, bias, w_value, kv, scale, after=()):
    tokens, keys = bias.shape
    value = w_value.shape[2]
    block = next(count for count in (4, 3, 2, 1) if heads % count == 0 and heads > count) * tokens
    return pl.pallas_call(
        functools.partial(attend_kernel, scale * math.log2(math.e), start, heads),
        in_specs=[LOCAL] * 4 + [ANYWHERE] * len(after),
        out_specs=LOCAL,
        out_shape=pltpu.VMEM((tokens, heads * value), BF16),
        scratch_shapes=[
            pltpu.VMEM((2, block, keys), F32),
            pltpu.VMEM((2, block, keys), BF16),
            pltpu.VMEM((2, block, 1), F32),
            pltpu.VMEM((block, w_value.shape[1]), BF16),
        ],
        compiler_params=params(20),
        cost_estimate=cost(0, 1024),
        name=f"attend{start}",
    )(held(queries), held(bias), held(w_value), held(kv), *after)


def gather_into(rows_of, parts, side):
    tokens = parts[0][0].shape[-2]
    for at, part in enumerate(parts):
        rows = pl.ds(at * tokens, tokens)
        if len(part) == 1:
            rows_of[rows] = part[0][side]
        elif isinstance(side, int):
            rows_of[rows] = part[side][...]
        else:
            for which in range(2):

                @pl.when(side == which)
                def _(rows=rows, part=part, which=which):
                    rows_of[rows] = part[which][...]


def grouped(refs, sizes):
    refs = iter(refs)
    return [tuple(next(refs) for _ in range(size)) for size in sizes]


def project_kernel(start, sizes, first, fresh, w_ref, *refs):
    out_ref, gathered = refs[-2:]
    parts = grouped(refs, sizes)
    tokens, depth = parts[0][0].shape[-2:]
    for side in range(2):
        gather_into(gathered.at[side], parts, side)
    weights = w_ref[start : start + depth]
    each = min(2, len(parts)) * tokens
    for side in range(2):
        for row in range(0, len(parts) * tokens, each):
            rows = slice(row, min(row + each, len(parts) * tokens))
            to = slice(first * tokens + rows.start, first * tokens + rows.stop)
            product = jnp.dot(gathered[side, rows], weights, preferred_element_type=F32)
            out_ref[side, to] = product if fresh else refs[sum(sizes)][side, to] + product


def project(start, parts, w_output, acc, after=(), first=0):
    sizes = tuple(map(len, parts))
    blocks = [block for part in parts for block in part]
    tokens, depth = blocks[0].shape[-2:]
    columns = w_output.shape[1]
    operands = [w_output, *blocks] + ([] if acc is None else [acc])
    shape = (2, len(parts) * tokens, columns) if acc is None else acc.shape
    return pl.pallas_call(
        functools.partial(project_kernel, start, sizes, first, acc is None),
        in_specs=[LOCAL] * len(operands) + [ANYWHERE] * len(after),
        out_specs=LOCAL,
        out_shape=pltpu.VMEM(shape, F32),
        scratch_shapes=[pltpu.VMEM((2, len(parts) * tokens, depth), BF16)],
        input_output_aliases={} if acc is None else {len(operands) - 1: 0},
        compiler_params=params(12),
        cost_estimate=cost(0, 1024),
        name=f"project{start}",
    )(*map(held, operands), *after)


def other_half(groups, keep):
    me, side = lax.axis_index("ctx"), lax.axis_index("head")
    return ((me // groups) ^ side ^ (1 - keep)).astype(jnp.int32)


def finish_kernel(start, sizes, first, keep, w_ref, *refs):
    out_ref, gathered = refs[-2:]
    acc_ref = refs[sum(sizes)]
    parts = grouped(refs, sizes)
    tokens, depth = parts[0][0].shape[-2:]
    rows = slice(first * tokens, (first + len(parts)) * tokens)
    other = other_half(acc_ref.shape[1] // tokens, keep)
    gather_into(gathered, parts, other)
    product = jnp.dot(
        gathered[...], w_ref[start : start + depth], preferred_element_type=F32
    )
    out_ref[...] = (acc_ref[other, rows] + product).astype(out_ref.dtype)


def finish(start, parts, w_output, acc, after=(), first=0):
    sizes = tuple(map(len, parts))
    blocks = [block for part in parts for block in part]
    tokens, depth = blocks[0].shape[-2:]
    columns = w_output.shape[1]
    rows = len(parts) * tokens
    outs = []
    for keep, dtype in enumerate((BF16, F32)):
        after = [*after, *outs]
        outs.append(
            pl.pallas_call(
                functools.partial(finish_kernel, start, sizes, first, keep),
                in_specs=[LOCAL] * (2 + len(blocks)) + [ANYWHERE] * len(after),
                out_specs=LOCAL,
                out_shape=pltpu.VMEM((rows, columns), dtype),
                scratch_shapes=[pltpu.VMEM((rows, depth), BF16)],
                compiler_params=params(12),
                cost_estimate=cost(0, 1024),
                name=f"finish{keep}",
            )(*map(held, [w_output, *blocks, acc]), *after)
        )
    return outs


def total_kernel(keys, far, groups, mine_ref, other_ref, *refs):
    out_ref, rounded, sem = refs[-3:]
    tokens = mine_ref.shape[0] // len(keys)
    me = lax.axis_index("ctx")
    other = other_half(groups, 1)
    copies = []
    for at, key in enumerate(keys):
        rows = pl.ds(at * tokens, tokens)
        place = (me ^ key ^ (far * other)) % groups
        to = pl.ds(pl.multiple_of(place * tokens, tokens), tokens)
        rounded[rows] = (mine_ref[rows] + other_ref[rows].astype(F32)).astype(BF16)
        copies.append(pltpu.make_async_copy(rounded.at[rows], out_ref.at[to], sem.at[at]))
        copies[-1].start()
    for copy in copies:
        copy.wait()


def total(keys, far, groups, mine, other, out, after):
    rows, columns = mine.shape
    tokens = rows // len(keys)
    given = [] if out is None else [out]
    return pl.pallas_call(
        functools.partial(total_kernel, keys, far, groups),
        in_specs=[LOCAL] * 2 + [ANYWHERE] * (len(given) + len(after)),
        out_specs=ANYWHERE,
        out_shape=jax.ShapeDtypeStruct((groups * tokens, columns), BF16),
        scratch_shapes=[pltpu.VMEM((rows, columns), BF16), pltpu.SemaphoreType.DMA((len(keys),))],
        input_output_aliases={2: 0} if given else {},
        compiler_params=params(4),
        cost_estimate=cost(0, 1024),
        name="total",
    )(held(mine), held(other), *given, *after)


def overlap(heads, starts, queries, bias, w_value, kv, w_output, scale):
    value = w_value.shape[2]
    got, ready = {}, {}
    last, acc, sums = [], None, []
    held_back = {entry[:2] for entry in ORDER}

    def send(name, chunk, after=None):
        nonlocal last
        x, mask = ready.pop((name, chunk))
        if after is not None:
            x = gate(x, after)
            last = [x]
        got[name, chunk] = exchange(x, mask, 8)
        along_z, paired = PLAN[chunk][1:]
        if name == FAR and not paired:
            offer(CROSS, chunk, got[FAR, chunk], 1)
        if name == NEAR and not along_z:
            offer(BOTH, chunk, got[NEAR, chunk], 1)
        if name == SIDE and along_z and paired:
            offer(BOTH, chunk, got[SIDE, chunk], 2)

    def offer(name, chunk, x, mask):
        ready[name, chunk] = x, mask
        if (name, chunk) not in held_back:
            send(name, chunk)

    def parts_of(chunk):
        sides = (SIDE,) if PLAN[chunk][2] else (SIDE, CROSS)
        names = (OWN, FAR), sides, (NEAR,), (BOTH,)
        return [tuple(got[name, chunk] for name in part) for part in names]

    for action, chunk, *waits in ORDER:
        after = last + [got[wait] for wait in waits]
        if action == ATTEND:
            out = attend(starts[chunk], heads[chunk], queries, bias, w_value, kv, scale, after)
            last = [out]
            got[OWN, chunk] = out
            offer(FAR, chunk, out, 6)
            if not PLAN[chunk][2]:
                offer(SIDE, chunk, out, 1)
        elif action == STACK:
            base = stack(got[OWN, chunk], got[FAR, chunk], after)
            last = [base]
            offer(NEAR, chunk, base, 2)
            if PLAN[chunk][2]:
                offer(SIDE, chunk, base, 1)
        elif action == PROJECT:
            some = parts_of(chunk)[: 3 if chunk == len(heads) - 2 else 4]
            acc = project(starts[chunk] * value, some, w_output, acc, after)
            last = [acc]
        elif action == FINISH:
            sums = [finish(starts[chunk] * value, parts_of(chunk)[:3], w_output, acc, after)]
            last = [sums[0][1]]
        elif action == BOTH and PLAN[chunk][1:] == (1, 0):
            pair = stack(got[SIDE, chunk], got[CROSS, chunk], after)
            last = [pair]
            got[BOTH, chunk] = exchange(pair, 2, 8)
        else:
            send(action, chunk, after)
    chunk = len(heads) - 2
    first = 3 if (PROJECT, chunk) in held_back else 0
    some = parts_of(chunk)[first:]
    acc = project(starts[chunk] * value, some, w_output, acc, last, first)
    chunk += 1
    first = 3 if sums else 0
    some = parts_of(chunk)[first:]
    row, after = starts[chunk] * value, [acc, some[-1][0]]
    cuts = [some] if sums else [some[:2], some[2:]]
    for cut in cuts:
        sums.append(finish(row, cut, w_output, acc, after, first))
        first, after = first + len(cut), [sums[-1][1]]
    return sums


def local(
    q_nope, q_rope, latent_cache, rope_keys, w_absorb, w_value, w_output, span_offset, valid_lengths
):
    head_count, nope_dim, latent = w_absorb.shape
    tokens = q_nope.shape[0]
    rope_dim = rope_keys.shape[1]
    per_shard = latent_cache.shape[0]
    shards = valid_lengths.shape[0]
    value = w_value.shape[2]
    scale = 1.0 / math.sqrt(nope_dim + rope_dim)

    far, *rest = basis_of(shards)
    keys = [0]
    for bit in rest:
        keys += [key ^ bit for key in keys]
    keys = sorted(keys)
    owners = [key ^ (far * inner) for key in keys for inner in range(2)]
    packed = pack(latent_cache, rope_keys)
    queries = prep(q_nope, q_rope, w_absorb)
    bias = mask(span_offset, valid_lengths, owners, tokens, per_shard)
    mine = spread(packed, shards, [queries])
    theirs = {key: sibling(pair) for key, pair in mine.items()}
    kv = join([mine[key] for key in keys], [theirs[key] for key in keys], per_shard, latent + LANES)

    heads = [count * head_count // 32 for count, *_ in PLAN]
    starts = [sum(heads[:chunk]) for chunk in range(len(heads))]
    if shards == 8:
        sums = overlap(heads, starts, queries, bias, w_value, kv, w_output, scale)
        cut = sums[0][1].shape[0] // tokens
        split = (keys[:cut], keys[cut:])
    else:
        acc = None
        for chunk, start in enumerate(starts):
            out = attend(start, heads[chunk], queries, bias, w_value, kv, scale)
            gathered = spread(out, shards)
            parts = [(gathered[key],) for key in keys]
            if chunk < len(heads) - 1:
                acc = project(start * value, parts, w_output, acc)
        sums = [finish(starts[-1] * value, parts, w_output, acc)]
        split = (keys,)

    out, after = None, [sums[-1][1]]
    others = [sibling(given) for given, _ in sums]
    for some, (_, kept), other in zip(split, sums, others):
        out = total(some, far, len(keys), kept, other, out, after)
        after = []
    return out


def solution(mesh):
    return jax.shard_map(
        local,
        mesh=mesh,
        in_specs=(
            P(("groups", "ctx"), "head"),
            P(("groups", "ctx"), "head"),
            P(("groups", "ctx"), None),
            P(("groups", "ctx"), None),
            P("head", None, None),
            P("head", None, None),
            P("head", "ctx"),
            P("groups"),
            P("groups"),
        ),
        out_specs=P(("groups", "head"), "ctx"),
        check_vma=False,
    )
```
